32 devices in a mesh: wide: 16 (over z, y, x), narrow: 2 (over core).
Axes of the slice: x: 2, y: 2, z: 4, core: 2. Of those that a mesh axis runs over, the one named last changes fastest.
Arguments:
- x_src: bfloat16 [2048, 16384], P('narrow', 'wide'), may hold values from -6 to 6
- cond: bfloat16 [128, 1024], P('narrow', 'wide'), may hold values from -6 to 6
- lengths: int32 [128], replicated, may hold values from 0 to 1024, as said below
- bucket: int32 [128], replicated, may hold values from 0 to 15
- w_mod: bfloat16 [1024, 6144], replicated, may hold values from -0.1875 to 0.1875
- b_mod: bfloat16 [6144], replicated, may hold values from -3 to 3
- w_qkv: bfloat16 [1024, 3072], replicated, may hold values from -0.1875 to 0.1875
- b_qv: bfloat16 [2048], replicated, may hold values from -0.29882812 to 0.29882812
- w_proj: bfloat16 [1024, 1024], replicated, may hold values from -3 to 3
- b_proj: bfloat16 [1024], replicated, may hold values from -2 to 2
- w_fc1: bfloat16 [1024, 4096], replicated, may hold values from -0.1875 to 0.1875
- b_fc1: bfloat16 [4096], replicated, may hold values from -2 to 2
- w_fc2: bfloat16 [4096, 1024], replicated, may hold values from -0.09375 to 0.09375
- b_fc2: bfloat16 [1024], replicated, may hold values from -2 to 2
- grad_out: bfloat16 [32768, 1024], P(('wide', 'narrow')), may hold values from -6 to 6
Outputs:
- y_dest: bfloat16 [32768, 1024], P(('wide', 'narrow'))
- dx_src: bfloat16 [2048, 16384], P('narrow', 'wide')
- dcond: bfloat16 [128, 1024], P('narrow', 'wide')
- grad_w_mod: float32 [1024, 6144], P(('wide', 'narrow'))
- grad_b_mod: float32 [6144], P(('wide', 'narrow'))
- grad_w_qkv: float32 [1024, 3072], P(('wide', 'narrow'))
- grad_b_qv: float32 [2048], P(('wide', 'narrow'))
- grad_w_proj: float32 [1024, 1024], P(('wide', 'narrow'))
- grad_b_proj: float32 [1024], P(('wide', 'narrow'))
- grad_w_fc1: float32 [1024, 4096], P(('wide', 'narrow'))
- grad_b_fc1: float32 [4096], P(('wide', 'narrow'))
- grad_w_fc2: float32 [4096, 1024], P(('wide', 'narrow'))
- grad_b_fc2: float32 [1024], P(('wide', 'narrow'))
The draws below stay inside these ranges and needn't reach their ends.
Inputs may be any that keep to these rules, and one draw needn't show every extreme that they name: `lengths`: every entry is 0 (an empty place), 256 or 1024. In each half, the live places of one bucket hold at most 1024 tokens and at most 4 places; in each half some bucket holds exactly 1024 tokens in places of 1024, and another exactly 4 places.
All inputs are finite; a program needn't handle non-finite values.
Results may differ from the reference program's by a relative error of at most 0.012.
The reference program's roundings to bfloat16 on the way count: a program that leaves them out, or rounds other values in their place, can miss the bound.
Values may be sent and summed in bfloat16 or wider, within the bound.
No kernel may reach another device: no remote copies, remote signals or barrier semaphores. Data moves between devices by JAX's collectives and lax.ppermute only.
A program may use at most 320 MiB of HBM per device.

```python
import math
import jax
import jax.numpy as jnp
from jax import lax

D = 1024
HEADS = 16
HEAD_DIM = 64
MLP = 4096
SHORT = 256
LONG = 1024
TOK_DEV = 1024
SLOTS = 4
SAMP = 64
SRC_ROWS = 2048
SRC_COLS = 16384
DEST_ROWS = 32768
N_WIDE = 16
N_NARROW = 2


def shuffle_order(order_key):
    return jax.random.permutation(order_key, SAMP)


def sample_plan(key):
    kind_key, first_key, second_key, order_key = jax.random.split(key, 4)
    kind_table = jnp.array([0, 1, 1, 2, 2, 1, 3, 1], dtype=jnp.int32)
    kinds = kind_table[jax.random.randint(kind_key, (N_NARROW, N_WIDE), 0, 8)]
    group_ids = jnp.arange(N_WIDE, dtype=jnp.int32)[None, :]
    first = jax.random.randint(first_key, (N_NARROW, 1), 0, N_WIDE)
    second = (first + 1 + jax.random.randint(second_key, (N_NARROW, 1), 0, N_WIDE - 1)) % N_WIDE
    kinds = jnp.where(group_ids == first, 0, kinds)
    kinds = jnp.where(group_ids == second, 3, kinds)
    slot_ids = jnp.arange(SLOTS, dtype=jnp.int32)[None, None, :]
    kind_cube = kinds[:, :, None]
    long_part = jnp.where(slot_ids < TOK_DEV // LONG, LONG, 0)
    short_count = jnp.where(kind_cube == 1, 1, jnp.where(kind_cube == 2, SLOTS // 2, SLOTS))
    short_part = jnp.where(slot_ids < short_count, SHORT, 0)
    sample_len = jnp.where(kind_cube == 0, long_part, short_part).astype(jnp.int32)
    sample_bucket = jnp.broadcast_to(jnp.arange(N_WIDE, dtype=jnp.int32)[None, :, None], sample_len.shape).astype(jnp.int32)
    orders = jax.vmap(shuffle_order)(jax.random.split(order_key, N_NARROW))
    shuffled_len = jnp.take_along_axis(sample_len.reshape(N_NARROW, SAMP), orders, axis=1)
    shuffled_bucket = jnp.take_along_axis(sample_bucket.reshape(N_NARROW, SAMP), orders, axis=1)
    return (shuffled_len.reshape(-1).astype(jnp.int32), shuffled_bucket.reshape(-1).astype(jnp.int32))


def draw_lengths(key, part):
    return sample_plan(key)[0]


def draw_bucket(key, part):
    return sample_plan(key)[1]


def levels(own_key, extent, cuts, low, high):
    loudness = 1.0
    for axis_at, blocks in cuts:
        steps = jax.random.uniform(jax.random.fold_in(jax.random.fold_in(own_key, 6), axis_at), (blocks,), jnp.float32, low / len(cuts), high / len(cuts))
        loudness = loudness * jnp.repeat(jnp.exp(steps), extent[axis_at] // blocks).reshape((-1,) + (1,) * (len(extent) - 1 - axis_at))
    return loudness


def gaussian(own_key, extent, scale, bound, cuts=(), kind=jnp.bfloat16):
    result = jax.random.normal(own_key, extent, jnp.float32) * scale
    if len(cuts) > 0:
        result = levels(own_key, extent, cuts, -0.22, 0.18) * result
    return jnp.clip(result, min=-bound, max=bound).astype(kind)


def setup_inputs(seed: int = 0) -> dict:
    arg_keys = jax.random.split(jax.random.key(seed), 16)
    x_src = gaussian(arg_keys[0], (SRC_ROWS, SRC_COLS), 1.0, 6.0, ((0, 2), (1, 16)))
    cond = gaussian(arg_keys[1], (N_NARROW * SAMP, D), 1.0, 6.0, ((0, 2), (1, 16)))
    lengths = draw_lengths(jax.random.fold_in(arg_keys[15], 71), 0)
    bucket = draw_bucket(jax.random.fold_in(arg_keys[15], 71), 0)
    w_mod = gaussian(arg_keys[4], (D, 6 * D), D ** -0.5, 0.1875)
    b_mod = gaussian(arg_keys[5], (6 * D,), 0.5, 3.0)
    w_qkv = gaussian(arg_keys[6], (D, 3 * D), D ** -0.5, 0.1875)
    b_qv = gaussian(arg_keys[7], (2 * D,), 0.05, 0.29882812)
    w_proj = gaussian(arg_keys[8], (D, D), 4 ** -0.5, 3.0)
    b_proj = gaussian(arg_keys[9], (D,), 0.3, 2.0)
    w_fc1 = gaussian(arg_keys[10], (D, MLP), D ** -0.5, 0.1875)
    b_fc1 = gaussian(arg_keys[11], (MLP,), 0.3, 2.0)
    w_fc2 = gaussian(arg_keys[12], (MLP, D), MLP ** -0.5, 0.09375)
    b_fc2 = gaussian(arg_keys[13], (D,), 0.3, 2.0)
    grad_out = gaussian(arg_keys[14], (DEST_ROWS, D), 1.0, 6.0, ((0, 32),))
    return dict(x_src=x_src, cond=cond, lengths=lengths, bucket=bucket, w_mod=w_mod, b_mod=b_mod, w_qkv=w_qkv, b_qv=b_qv, w_proj=w_proj, b_proj=b_proj, w_fc1=w_fc1, b_fc1=b_fc1, w_fc2=w_fc2, b_fc2=b_fc2, grad_out=grad_out)


@jax.custom_vjp
def low(v):
    return lax.optimization_barrier(v.astype(jnp.bfloat16)).astype(jnp.float32)

@jax.custom_vjp
def low_back(v):
    return v

def low_keep(v):
    return (low(v), None)

def low_pass(kept, grad):
    return (grad,)

def back_keep(v):
    return (v, None)

def back_low(kept, grad):
    return (low(grad),)
low.defvjp(low_keep, low_pass)
low_back.defvjp(back_keep, back_low)
EPS = 1e-06
HIGH = lax.Precision.HIGHEST
MASKED = -1000000000.0

def plan_tables(sample_len, sample_bucket, wide_count):
    units = (sample_len // wide_count).astype(jnp.int32)
    count_all = sample_len.shape[0]
    order_idx = jnp.arange(count_all, dtype=jnp.int32)
    earlier = (order_idx[:, None] < order_idx[None, :]) & (sample_bucket[:, None] == sample_bucket[None, :])
    live_flag = (sample_len > 0).astype(jnp.int32)
    offset = (jnp.cumsum(units) - units).astype(jnp.int32)
    dest_off = lax.optimization_barrier(jnp.sum(jnp.where(earlier, units[:, None], 0), axis=0)).astype(jnp.int32)
    slot_num = lax.optimization_barrier(jnp.sum(jnp.where(earlier, live_flag[:, None], 0), axis=0)).astype(jnp.int32)
    return (units, offset, dest_off, slot_num, live_flag)

def row_tables(tables, sample_bucket, group_idx, row_count, wide_count):
    units, offset, dest_off, slot_num, live_flag = tables
    position = jnp.arange(row_count, dtype=jnp.int32)
    start_row = dest_off * wide_count
    member = (sample_bucket[None, :] == group_idx) & (live_flag[None, :] > 0) & (position[:, None] >= start_row[None, :]) & (position[:, None] < (start_row + units * wide_count)[None, :])
    hit_int = member.astype(jnp.int32)
    row_valid = lax.optimization_barrier(jnp.sum(hit_int, axis=1)).astype(jnp.int32)
    row_slot = lax.optimization_barrier(jnp.sum(hit_int * slot_num[None, :], axis=1)).astype(jnp.int32)
    stream_row = (lax.optimization_barrier(jnp.sum(hit_int * (offset * wide_count - start_row)[None, :], axis=1)) + position).astype(jnp.int32)
    return (row_valid, row_slot, stream_row)

def normalize(values):
    centre = values - lax.optimization_barrier(jnp.mean(values, axis=1, keepdims=True))
    spread = lax.optimization_barrier(jnp.mean(centre * centre, axis=1, keepdims=True))
    return centre * lax.rsqrt(spread + EPS)

def layer(params, rows_in, cond_in, select, segment):
    w_mod, b_mod, w_qkv, b_qv, w_proj, b_proj, w_fc1, b_fc1, w_fc2, b_fc2 = params
    feat_dim = rows_in.shape[1]
    tok_count = rows_in.shape[0]
    x_val = low_back(rows_in)
    cond_val = low_back(cond_in)
    modulate = low_back(jnp.dot(low(jax.nn.silu(cond_val)), w_mod, precision=HIGH) + b_mod)
    per_row = jnp.dot(select, modulate, precision=HIGH)
    shift_one, scale_one, gate_one, shift_two, scale_two, gate_two = jnp.split(per_row, 6, axis=1)
    attn_in = low(normalize(x_val) * (1.0 + scale_one) + shift_one)
    bias_full = jnp.concatenate([b_qv[:feat_dim], jnp.zeros((feat_dim,), jnp.float32), b_qv[feat_dim:]])
    mixed = low(low_back(jnp.dot(attn_in, w_qkv, precision=HIGH) + bias_full))
    queries = mixed[:, :feat_dim].reshape(tok_count, HEADS, HEAD_DIM)
    keys_all = mixed[:, feat_dim:2 * feat_dim].reshape(tok_count, HEADS, HEAD_DIM)
    values_all = mixed[:, 2 * feat_dim:].reshape(tok_count, HEADS, HEAD_DIM)
    scores = jnp.einsum('qhd,khd->hqk', queries, keys_all, precision=HIGH) / math.sqrt(HEAD_DIM)
    scores = low_back(scores)
    same_seg = segment[:, None] == segment[None, :]
    scores = jnp.where(same_seg[None], scores, MASKED)
    probs = jax.nn.softmax(scores, axis=-1)
    attended = jnp.einsum('hqk,khd->qhd', low(probs), values_all, precision=HIGH).reshape(tok_count, feat_dim)
    attended = low(low_back(attended))
    branch_one = low_back(jnp.dot(attended, w_proj, precision=HIGH) + b_proj)
    resid_one = x_val + gate_one * branch_one
    mlp_in = low(normalize(resid_one) * (1.0 + scale_two) + shift_two)
    hidden_pre = low_back(jnp.dot(mlp_in, w_fc1, precision=HIGH) + b_fc1)
    hidden_act = low(jax.nn.gelu(hidden_pre, approximate=True))
    branch_two = low_back(jnp.dot(hidden_act, w_fc2, precision=HIGH) + b_fc2)
    return resid_one + gate_two * branch_two

def reference(x_src, cond, lengths, bucket, w_mod, b_mod, w_qkv, b_qv, w_proj, b_proj, w_fc1, b_fc1, w_fc2, b_fc2, grad_out):
    wide_count = N_WIDE
    half_count = N_NARROW
    tok_rows = TOK_DEV
    feat_dim = D
    slot_count = SLOTS
    sample_count = SAMP
    dest_count = wide_count * half_count
    len_halves = lengths.reshape(half_count, sample_count)
    buck_halves = bucket.reshape(half_count, sample_count)
    dest_ids = jnp.arange(dest_count, dtype=jnp.int32)

    def dest_tables(dest_id):
        group_idx = dest_id // half_count
        half_idx = dest_id % half_count
        sample_len = len_halves[half_idx]
        sample_bucket = buck_halves[half_idx]
        tables = plan_tables(sample_len, sample_bucket, wide_count)
        row_valid, row_slot, stream_row = row_tables(tables, sample_bucket, group_idx, tok_rows, wide_count)
        slot_ids = jnp.arange(slot_count, dtype=jnp.int32)
        hit_int = ((sample_bucket[None, :] == group_idx) & (tables[4][None, :] > 0) & (tables[3][None, :] == slot_ids[:, None])).astype(jnp.int32)
        slot_sample = lax.optimization_barrier(jnp.sum(hit_int * jnp.arange(sample_count, dtype=jnp.int32)[None, :], axis=1)).astype(jnp.int32)
        slot_valid = lax.optimization_barrier(jnp.sum(hit_int, axis=1)).astype(jnp.int32)
        return (row_valid, row_slot, stream_row, slot_sample, slot_valid)
    all_tables = lax.map(dest_tables, dest_ids)

    def forward(x_whole, cond_whole, params):
        stream = x_whole.reshape(half_count, tok_rows, wide_count, feat_dim).reshape(half_count, tok_rows * wide_count, feat_dim)
        cond_rows = cond_whole.reshape(half_count, sample_count, feat_dim)

        def one_dest(packed):
            dest_id, row_valid, row_slot, stream_row, slot_sample, slot_valid = packed
            half_idx = dest_id % half_count
            rows_in = jnp.where(row_valid[:, None] > 0, jnp.take(stream[half_idx], stream_row, axis=0), 0.0)
            cond_in = jnp.where(slot_valid[:, None] > 0, jnp.take(cond_rows[half_idx], slot_sample, axis=0), 0.0)
            slot_ids = jnp.arange(slot_count, dtype=jnp.int32)
            select = ((row_slot[:, None] == slot_ids[None, :]) & (row_valid[:, None] > 0)).astype(jnp.float32)
            segment = jnp.where(row_valid > 0, row_slot, -1)
            return layer(params, rows_in, cond_in, select, segment)
        return lax.map(jax.checkpoint(one_dest), (dest_ids,) + tuple(all_tables))
    params = (w_mod.astype(jnp.float32), b_mod.astype(jnp.float32), w_qkv.astype(jnp.float32), b_qv.astype(jnp.float32), w_proj.astype(jnp.float32), b_proj.astype(jnp.float32), w_fc1.astype(jnp.float32), b_fc1.astype(jnp.float32), w_fc2.astype(jnp.float32), b_fc2.astype(jnp.float32))
    y_blocks, pullback = jax.vjp(forward, x_src.astype(jnp.float32), cond.astype(jnp.float32), params)
    grad_x, grad_cond, grad_params = pullback(grad_out.astype(jnp.float32).reshape(dest_count, tok_rows, feat_dim))
    return (y_blocks.reshape(dest_count * tok_rows, feat_dim).astype(jnp.bfloat16), grad_x.astype(jnp.bfloat16), grad_cond.astype(jnp.bfloat16), grad_params[0], grad_params[1], grad_params[2], grad_params[3], grad_params[4], grad_params[5], grad_params[6], grad_params[7], grad_params[8], grad_params[9])
```

```python
import functools
import math

import jax
import jax.numpy as jnp
from jax import lax
from jax.experimental import pallas as pl
from jax.experimental.pallas import tpu as pltpu
from jax.sharding import PartitionSpec as P

HEADS = 16
HEAD_DIM = 64
EPS = 1e-06
MASKED = -1000000000.0
LOG2E = 1.4426950408889634
BLK = 256
TILE = 16
VMEM_LIMIT = 58 * 2**20
BF16 = jnp.bfloat16
F32 = jnp.float32


def params(**more):
    return pltpu.CompilerParams(vmem_limit_bytes=VMEM_LIMIT, **more)


def dot(left, right, left_dim, right_dim):
    return lax.dot_general(
        left, right, (((left_dim,), (right_dim,)), ((), ())), preferred_element_type=F32
    )


def norm_parts(values):
    centre = values - jnp.mean(values, axis=1, keepdims=True)
    spread = jnp.mean(centre * centre, axis=1, keepdims=True)
    inverse = lax.rsqrt(spread + EPS)
    return centre * inverse, inverse


def norm_back(grad, normed, inverse):
    return (
        grad
        - jnp.mean(grad, axis=1, keepdims=True)
        - normed * jnp.mean(grad * normed, axis=1, keepdims=True)
    ) * inverse


def regroup_kernel(
    len_ref, buck_ref, me_ref, x_ref, cond_ref,
    send_ref, scond_ref, seg_ref, src_ref, cidx_ref,
    off_ref, slot_ref, cond_in, cond_out, *, wide, slots,
):
    places = len_ref.shape[0]
    cells = send_ref.shape[1]
    send_ref[...] = jnp.zeros_like(send_ref)
    cond_out[...] = jnp.zeros_like(cond_out)
    cond_in[...] = cond_ref[...].astype(F32)
    for i in range(wide):
        off_ref[i] = 0
        slot_ref[i] = 0
    for i in range(seg_ref.shape[0]):
        seg_ref[i] = -1

    @pl.loop(0, src_ref.shape[0])
    def _(i):
        src_ref[i] = -1

    def place(j, offset):
        units = len_ref[j] // wide
        b = buck_ref[j]
        cidx_ref[j] = -1

        @pl.when(units > 0)
        def _():
            start = off_ref[b]
            slot = slot_ref[b]
            off_ref[b] = start + units
            slot_ref[b] = slot + 1
            cidx_ref[j] = b * slots + slot
            cond_out[pl.ds(b * slots + slot, 1), :] = cond_in[pl.ds(j, 1), :]

            @pl.loop(0, units // TILE)
            def _(t):
                a = pl.multiple_of(offset + t * TILE, TILE)
                c = pl.multiple_of(start + t * TILE, TILE)
                send_ref[b, pl.ds(c, TILE), :] = x_ref[pl.ds(a, TILE), :]
                src_ref[a // TILE] = (b * cells + c) // TILE

            @pl.when(b == me_ref[0])
            def _():
                @pl.loop(0, units * wide // BLK)
                def _(t):
                    seg_ref[start * wide // BLK + t] = slot

        return offset + units

    lax.fori_loop(0, places, place, 0)
    scond_ref[...] = cond_out[...].astype(BF16)


def regroup(x_src, cond, lens, buck, me, wide):
    rows, feat = x_src.shape
    places, part = cond.shape
    slots = places // wide
    smem = pl.BlockSpec(memory_space=pltpu.SMEM)
    vmem = pl.BlockSpec(memory_space=pltpu.VMEM)
    return pl.pallas_call(
        functools.partial(regroup_kernel, wide=wide, slots=slots),
        in_specs=[smem, smem, smem, vmem, vmem],
        out_specs=[vmem, vmem, smem, smem, smem],
        out_shape=[
            jax.ShapeDtypeStruct((wide, rows // wide, feat), BF16),
            jax.ShapeDtypeStruct((places, part), BF16),
            jax.ShapeDtypeStruct((rows // BLK,), jnp.int32),
            jax.ShapeDtypeStruct((rows // TILE,), jnp.int32),
            jax.ShapeDtypeStruct((places,), jnp.int32),
        ],
        scratch_shapes=[
            pltpu.SMEM((wide,), jnp.int32),
            pltpu.SMEM((wide,), jnp.int32),
            pltpu.VMEM((places, part), F32),
            pltpu.VMEM((places, part), F32),
        ],
        compiler_params=params(),
    )(lens, buck, me, x_src, cond)


def restore_kernel(src_ref, cidx_ref, back_ref, bcond_ref, dx_ref, dcond_ref, cond_in, cond_out):
    cond_in[...] = bcond_ref[...].astype(F32)

    @pl.loop(0, src_ref.shape[0])
    def _(i):
        at = src_ref[i]
        rows = back_ref[pl.ds(pl.multiple_of(jnp.maximum(at, 0) * TILE, TILE), TILE), :]
        dx_ref[pl.ds(pl.multiple_of(i * TILE, TILE), TILE), :] = jnp.where(
            at >= 0, rows, jnp.zeros_like(rows)
        )

    @pl.loop(0, cidx_ref.shape[0])
    def _(j):
        at = cidx_ref[j]
        row = cond_in[pl.ds(jnp.maximum(at, 0), 1), :]
        cond_out[pl.ds(j, 1), :] = jnp.where(at >= 0, row, 0.0)

    dcond_ref[...] = cond_out[...].astype(BF16)


def restore(src, cidx, back, bcond):
    smem = pl.BlockSpec(memory_space=pltpu.SMEM)
    vmem = pl.BlockSpec(memory_space=pltpu.VMEM)
    return pl.pallas_call(
        restore_kernel,
        in_specs=[smem, smem, vmem, vmem],
        out_specs=[vmem, vmem],
        out_shape=[
            jax.ShapeDtypeStruct(back.shape, BF16),
            jax.ShapeDtypeStruct(bcond.shape, BF16),
        ],
        scratch_shapes=[pltpu.VMEM(bcond.shape, F32), pltpu.VMEM(bcond.shape, F32)],
        compiler_params=params(),
    )(src, cidx, back, bcond)


def regroup_any(x_src, cond, lens, buck, me, wide):
    rows, feat = x_src.shape
    places = lens.shape[0]
    slots, cells = places // wide, rows // wide
    units = lens // wide
    order = jnp.arange(places, dtype=jnp.int32)
    earlier = (order[:, None] < order[None, :]) & (buck[:, None] == buck[None, :])
    live = (lens > 0).astype(jnp.int32)
    offset = jnp.cumsum(units) - units
    start = jnp.sum(jnp.where(earlier, units[:, None], 0), axis=0)
    slot = jnp.sum(jnp.where(earlier, live[:, None], 0), axis=0)
    cell = jnp.arange(cells, dtype=jnp.int32)[None, :, None]
    to_target = (buck[None, :] == jnp.arange(wide, dtype=jnp.int32)[:, None]) & (live[None, :] > 0)
    hit = (
        to_target[:, None, :]
        & (cell >= start[None, None, :])
        & (cell < (start + units)[None, None, :])
    ).astype(jnp.int32)
    valid = jnp.sum(hit, axis=2)
    source = jnp.sum(hit * (offset - start)[None, None, :], axis=2) + cell[:, :, 0]
    source = jnp.where(valid > 0, source, 0)
    picked = jnp.take(x_src, source.reshape(-1), axis=0).reshape(wide, cells, feat)
    send = jnp.where(valid[:, :, None] > 0, picked, jnp.zeros((), BF16))
    cond_hit = to_target[:, None, :] & (
        slot[None, None, :] == jnp.arange(slots, dtype=jnp.int32)[None, :, None]
    )
    scond = jnp.einsum("wqs,sf->wqf", cond_hit.astype(BF16), cond, preferred_element_type=F32)
    scond = scond.astype(BF16).reshape(cond.shape)
    first = jnp.arange(rows // BLK, dtype=jnp.int32)[:, None] * BLK
    mine = (
        ((buck == me[0]) & (live > 0))[None, :]
        & (first >= (start * wide)[None, :])
        & (first < ((start + units) * wide)[None, :])
    )
    seg = jnp.sum(jnp.where(mine, slot[None, :] + 1, 0), axis=1) - 1
    spot = jnp.arange(rows, dtype=jnp.int32)[:, None]
    inside = (live[None, :] > 0) & (spot >= offset[None, :]) & (spot < (offset + units)[None, :])
    src = jnp.sum(jnp.where(inside, (buck * cells + start - offset)[None, :] + spot + 1, 0), axis=1)
    cidx = jnp.where(live > 0, buck * slots + slot, -1)
    return send, scond, seg.astype(jnp.int32), src - 1, cidx


def restore_any(src, cidx, back, bcond):
    dx = jnp.take(back, jnp.maximum(src, 0), axis=0)
    dcond = jnp.take(bcond, jnp.maximum(cidx, 0), axis=0)
    zero = jnp.zeros((), BF16)
    return jnp.where(src[:, None] >= 0, dx, zero), jnp.where(cidx[:, None] >= 0, dcond, zero)


def qkv_kernel(x_ref, mod_ref, w_ref, b_ref, q_ref, a_ref):
    feat = x_ref.shape[-1]
    x = x_ref[...].reshape(BLK, feat).astype(F32)
    normed, _ = norm_parts(x)
    a1 = (normed * (1.0 + mod_ref[0, 1:2, :]) + mod_ref[0, 0:1, :]).astype(BF16)
    a1_t = a1.T
    a_ref[...] = a1_t
    for i in range(3):
        part = slice(i * feat, (i + 1) * feat)
        q_ref[part, :] = (dot(w_ref[part, :], a1_t, 1, 0) + b_ref[part, :]).astype(BF16)


def row_spec(view):
    return pl.BlockSpec((view[0], 1, view[2], view[3]), lambda k: (0, k, 0, 0))


def whole(*shape):
    return pl.BlockSpec(shape, lambda k: (0,) * len(shape))


def qkv_forward(x_view, mod_blocks, w_t, bias):
    feat = x_view.shape[-1]
    blocks = x_view.shape[1]
    return pl.pallas_call(
        qkv_kernel,
        grid=(blocks,),
        in_specs=[
            row_spec(x_view.shape),
            pl.BlockSpec((1, 6, feat), lambda k: (k, 0, 0)),
            whole(3 * feat, feat),
            whole(3 * feat, 1),
        ],
        out_specs=[
            pl.BlockSpec((3 * feat, BLK), lambda k: (0, k)),
            pl.BlockSpec((feat, BLK), lambda k: (0, k)),
        ],
        out_shape=[
            jax.ShapeDtypeStruct((3 * feat, blocks * BLK), BF16),
            jax.ShapeDtypeStruct((feat, blocks * BLK), BF16),
        ],
        compiler_params=params(),
        cost_estimate=pl.CostEstimate(
            flops=6 * feat * feat * blocks * BLK, bytes_accessed=20 * 2**20, transcendentals=0
        ),
    )(x_view, mod_blocks, w_t, bias)


def masks(seg_ref, query_block, blocks):
    base = LOG2E / math.sqrt(HEAD_DIM)
    same = [seg_ref[query_block] == seg_ref[kb] for kb in range(blocks)]
    scales = [jnp.where(s, base, 0.0) for s in same]
    shifts = [jnp.where(s, 0.0, MASKED * LOG2E) for s in same]
    return scales, shifts


def attend_kernel(seg_ref, q_ref, k_ref, v_ref, o_ref, lse_ref, *, blocks, heads):
    for h in range(heads):
        hs = slice(h * HEAD_DIM, (h + 1) * HEAD_DIM)
        keys = k_ref[hs, :].T
        v_t = v_ref[hs, :]
        for qb in range(blocks):
            qs = slice(qb * BLK, (qb + 1) * BLK)
            q_t = q_ref[hs, qs]
            scales, shifts = masks(seg_ref, qb, blocks)
            scores = [dot(keys[kb * BLK : (kb + 1) * BLK], q_t, 1, 0) for kb in range(blocks)]
            top = None
            for kb in range(blocks):
                peak = jnp.max(scores[kb], axis=0, keepdims=True) * scales[kb] + shifts[kb]
                top = peak if top is None else jnp.maximum(top, peak)
            total = jnp.zeros((1, BLK), F32)
            parts = []
            for kb in range(blocks):
                expo = jnp.exp2(scores[kb] * scales[kb] - (top - shifts[kb]))
                total = total + jnp.sum(expo, axis=0, keepdims=True)
                parts.append(expo.astype(BF16))
            out = dot(v_t, jnp.concatenate(parts, axis=0), 1, 0)
            o_ref[hs, qs] = (out / total).astype(BF16)
            lse_ref[h, :, qs] = top + jnp.log2(total)


def attend(seg, qkv_t, heads=2):
    feat3, rows = qkv_t.shape
    feat = feat3 // 3
    span = heads * HEAD_DIM
    groups = feat // span
    return pl.pallas_call(
        functools.partial(attend_kernel, blocks=rows // BLK, heads=heads),
        grid_spec=pltpu.PrefetchScalarGridSpec(
            num_scalar_prefetch=1,
            grid=(groups,),
            in_specs=[
                pl.BlockSpec((span, rows), lambda g, s: (g, 0)),
                pl.BlockSpec((span, rows), lambda g, s: (groups + g, 0)),
                pl.BlockSpec((span, rows), lambda g, s: (2 * groups + g, 0)),
            ],
            out_specs=[
                pl.BlockSpec((span, rows), lambda g, s: (g, 0)),
                pl.BlockSpec((heads, 1, rows), lambda g, s: (g, 0, 0)),
            ],
        ),
        out_shape=[
            jax.ShapeDtypeStruct((feat, rows), BF16),
            jax.ShapeDtypeStruct((feat // HEAD_DIM, 1, rows), F32),
        ],
        compiler_params=params(),
        cost_estimate=pl.CostEstimate(
            flops=16 * feat * rows * rows, bytes_accessed=8 * 2**20, transcendentals=16 * rows * rows
        ),
    )(seg, qkv_t, qkv_t, qkv_t)


def attend_back_kernel(
    seg_ref, q_ref, k_ref, v_ref, o_ref, do_ref, lse_ref, out_ref, *, blocks, heads
):
    scale = 1.0 / math.sqrt(HEAD_DIM)
    for h in range(heads):
        hs = slice(h * HEAD_DIM, (h + 1) * HEAD_DIM)
        k_t = k_ref[hs, :]
        keys, values = k_t.T, v_ref[hs, :].T
        inner = jnp.sum(
            o_ref[hs, :].astype(F32) * do_ref[hs, :].astype(F32), axis=0, keepdims=True
        )
        grad_k = grad_v = None
        for qb in range(blocks):
            qs = slice(qb * BLK, (qb + 1) * BLK)
            q_t, do_t = q_ref[hs, qs], do_ref[hs, qs]
            scales, shifts = masks(seg_ref, qb, blocks)
            probs, grads = [], []
            for kb in range(blocks):
                ks = slice(kb * BLK, (kb + 1) * BLK)
                score = dot(keys[ks], q_t, 1, 0)
                grad_p = dot(values[ks], do_t, 1, 0)
                prob = jnp.exp2(score * scales[kb] - (lse_ref[h, :, qs] - shifts[kb]))
                probs.append(prob.astype(BF16))
                grads.append((prob * (grad_p - inner[:, qs])).astype(BF16))
            probs = jnp.concatenate(probs, axis=0)
            grads = jnp.concatenate(grads, axis=0)
            out_ref[0, hs, qs] = (dot(k_t, grads, 1, 0) * scale).astype(BF16)
            more_k, more_v = dot(q_t, grads, 1, 1), dot(do_t, probs, 1, 1)
            grad_k = more_k if grad_k is None else grad_k + more_k
            grad_v = more_v if grad_v is None else grad_v + more_v
        out_ref[1, hs, :] = (grad_k * scale).astype(BF16)
        out_ref[2, hs, :] = grad_v.astype(BF16)


def attend_back(seg, qkv_t, o_t, do_t, lse, heads=2):
    feat3, rows = qkv_t.shape
    feat = feat3 // 3
    span = heads * HEAD_DIM
    groups = feat // span
    return pl.pallas_call(
        functools.partial(attend_back_kernel, blocks=rows // BLK, heads=heads),
        grid_spec=pltpu.PrefetchScalarGridSpec(
            num_scalar_prefetch=1,
            grid=(groups,),
            in_specs=[
                pl.BlockSpec((span, rows), lambda g, s: (g, 0)),
                pl.BlockSpec((span, rows), lambda g, s: (groups + g, 0)),
                pl.BlockSpec((span, rows), lambda g, s: (2 * groups + g, 0)),
                pl.BlockSpec((span, rows), lambda g, s: (g, 0)),
                pl.BlockSpec((span, rows), lambda g, s: (g, 0)),
                pl.BlockSpec((heads, 1, rows), lambda g, s: (g, 0, 0)),
            ],
            out_specs=pl.BlockSpec((3, span, rows), lambda g, s: (0, g, 0)),
        ),
        out_shape=jax.ShapeDtypeStruct((3, feat, rows), BF16),
        compiler_params=params(),
        cost_estimate=pl.CostEstimate(
            flops=24 * feat * rows * rows, bytes_accessed=16 * 2**20, transcendentals=16 * rows * rows
        ),
    )(seg, qkv_t, qkv_t, qkv_t, o_t, do_t, lse)


def proj_kernel(o_ref, w_ref, b_ref, x_ref, mod_ref, attn_ref, x1_ref, a_ref, at_ref):
    feat = x_ref.shape[-1]
    attn = dot(o_ref[...], w_ref[...], 0, 0) + b_ref[...]
    attn_ref[...] = attn
    x1 = x_ref[...].reshape(BLK, feat).astype(F32) + mod_ref[0, 2:3, :] * attn
    x1_ref[...] = x1
    normed, _ = norm_parts(x1)
    a2 = (normed * (1.0 + mod_ref[0, 4:5, :]) + mod_ref[0, 3:4, :]).astype(BF16)
    a_ref[...] = a2
    at_ref[...] = a2.T


def proj_forward(o_t, w_proj, b_proj, x_view, mod_blocks):
    feat = x_view.shape[-1]
    blocks = x_view.shape[1]
    rows = blocks * BLK
    by_row = pl.BlockSpec((BLK, feat), lambda k: (k, 0))
    by_column = pl.BlockSpec((feat, BLK), lambda k: (0, k))
    return pl.pallas_call(
        proj_kernel,
        grid=(blocks,),
        in_specs=[
            by_column,
            whole(feat, feat),
            whole(1, feat),
            row_spec(x_view.shape),
            pl.BlockSpec((1, 6, feat), lambda k: (k, 0, 0)),
        ],
        out_specs=[by_row, by_row, by_row, by_column],
        out_shape=[
            jax.ShapeDtypeStruct((rows, feat), F32),
            jax.ShapeDtypeStruct((rows, feat), F32),
            jax.ShapeDtypeStruct((rows, feat), BF16),
            jax.ShapeDtypeStruct((feat, rows), BF16),
        ],
        compiler_params=params(),
        cost_estimate=pl.CostEstimate(
            flops=2 * feat * feat * rows, bytes_accessed=20 * 2**20, transcendentals=0
        ),
    )(o_t, w_proj, b_proj, x_view, mod_blocks)


def gelu_both(u):
    c = math.sqrt(2.0 / math.pi)
    square = u * u
    t = jnp.tanh(u * (c + (c * 0.044715) * square))
    half = 0.5 + 0.5 * t
    slope = half + (0.5 * u) * (1.0 - t * t) * (c + (3.0 * c * 0.044715) * square)
    return u * half, slope


def mlp_kernel(
    a_ref, at_ref, df_ref, dg_ref, w1_ref, w2_ref, b1_ref,
    f_ref, da_ref, d1_ref, d2_ref, db_ref, g_ref, du_ref,
):
    step = pl.program_id(0)
    rows = a_ref.shape[0]

    @pl.when(step == 0)
    def _():
        f_ref[...] = jnp.zeros_like(f_ref)
        da_ref[...] = jnp.zeros_like(da_ref)

    w1, w2 = w1_ref[...], w2_ref[...]
    bias = jnp.zeros((1, w1.shape[1]), F32)
    for r in range(rows // BLK):
        rs = slice(r * BLK, (r + 1) * BLK)
        u = dot(a_ref[rs, :], w1, 1, 0) + b1_ref[...]
        g, slope = gelu_both(u)
        g = g.astype(BF16)
        du = (dg_ref[rs, :] * slope).astype(BF16)
        g_ref[rs, :] = g
        du_ref[rs, :] = du
        bias = bias + jnp.sum(du.astype(F32), axis=0, keepdims=True)
        f_ref[rs, :] += dot(g, w2, 1, 0)
        da_ref[rs, :] += dot(du, w1, 1, 1)
    db_ref[...] = bias
    du = du_ref[...]
    d1_ref[0] = dot(at_ref[...], du, 1, 0).astype(BF16)
    d2_ref[...] = dot(g_ref[...], df_ref[...], 0, 0).astype(BF16)


def mlp(a2, a2_t, df, dg, w1, w2, b1, width=512):
    rows, feat = a2.shape
    hidden = w1.shape[1]
    per = feat // width
    one = pl.Buffered(1)

    def fixed(*shape):
        return pl.BlockSpec(shape, lambda j: (0,) * len(shape), pipeline_mode=one)

    return pl.pallas_call(
        mlp_kernel,
        grid=(hidden // width,),
        in_specs=[
            fixed(rows, feat),
            fixed(feat, rows),
            fixed(rows, feat),
            pl.BlockSpec((rows, width), lambda j: (0, j)),
            pl.BlockSpec((feat, width), lambda j: (0, j)),
            pl.BlockSpec((width, feat), lambda j: (j, 0)),
            pl.BlockSpec((1, width), lambda j: (0, j)),
        ],
        out_specs=[
            whole(rows, feat),
            whole(rows, feat),
            pl.BlockSpec((1, feat, width), lambda j: (j // per, 0, j % per)),
            pl.BlockSpec((width, feat), lambda j: (j, 0)),
            pl.BlockSpec((1, width), lambda j: (0, j)),
        ],
        out_shape=[
            jax.ShapeDtypeStruct((rows, feat), F32),
            jax.ShapeDtypeStruct((rows, feat), F32),
            jax.ShapeDtypeStruct((hidden // feat, feat, feat), BF16),
            jax.ShapeDtypeStruct((hidden, feat), BF16),
            jax.ShapeDtypeStruct((1, hidden), F32),
        ],
        scratch_shapes=[pltpu.VMEM((rows, width), BF16), pltpu.VMEM((rows, width), BF16)],
        compiler_params=params(),
        cost_estimate=pl.CostEstimate(
            flops=10 * rows * feat * hidden, bytes_accessed=64 * 2**20, transcendentals=rows * hidden
        ),
    )(a2, a2_t, df, dg, w1, w2, b1)


def middle_kernel(
    f_ref, b2_ref, x1_ref, attn_ref, dy_ref, da_ref, mod_ref, o_ref, w_ref,
    y_ref, dx_ref, do_ref, dw_ref, db_ref, sums_ref, acc_ref,
):
    k = pl.program_id(0)

    @pl.when(k == 0)
    def _():
        acc_ref[...] = jnp.zeros_like(acc_ref)
        db_ref[...] = jnp.zeros_like(db_ref)

    f = f_ref[...] + b2_ref[...]
    x1 = x1_ref[...]
    dy = dy_ref[...].astype(F32)
    y_ref[...] = (x1 + mod_ref[0, 5:6, :] * f).astype(BF16)
    normed, inverse = norm_parts(x1)
    da = da_ref[...]
    dx1 = dy + norm_back(da * (1.0 + mod_ref[0, 4:5, :]), normed, inverse)
    dx_ref[...] = dx1
    dattn = (mod_ref[0, 2:3, :] * dx1).astype(BF16)
    db_ref[...] += jnp.sum(dattn.astype(F32), axis=0, keepdims=True)
    sums_ref[0, 0:1, :] = jnp.sum(dx1 * attn_ref[...], axis=0, keepdims=True)
    sums_ref[0, 1:2, :] = jnp.sum(da, axis=0, keepdims=True)
    sums_ref[0, 2:3, :] = jnp.sum(da * normed, axis=0, keepdims=True)
    sums_ref[0, 3:4, :] = jnp.sum(dy * f, axis=0, keepdims=True)
    do_ref[...] = dot(w_ref[...], dattn, 1, 1).astype(BF16)
    acc_ref[...] += dot(o_ref[...], dattn, 1, 0)

    @pl.when(k == pl.num_programs(0) - 1)
    def _():
        dw_ref[...] = acc_ref[...].astype(BF16)


def middle(f, b2, x1, attn, dy, da2, mod_blocks, o_t, w_proj):
    rows, feat = x1.shape
    by_row = pl.BlockSpec((BLK, feat), lambda k: (k, 0))
    by_column = pl.BlockSpec((feat, BLK), lambda k: (0, k))
    blocks = rows // BLK
    return pl.pallas_call(
        middle_kernel,
        grid=(blocks,),
        in_specs=[
            by_row, whole(1, feat), by_row, by_row, by_row, by_row,
            pl.BlockSpec((1, 6, feat), lambda k: (k, 0, 0)),
            by_column, whole(feat, feat),
        ],
        out_specs=[
            by_row, by_row, by_column, whole(feat, feat), whole(1, feat),
            pl.BlockSpec((1, 4, feat), lambda k: (k, 0, 0)),
        ],
        out_shape=[
            jax.ShapeDtypeStruct((rows, feat), BF16),
            jax.ShapeDtypeStruct((rows, feat), F32),
            jax.ShapeDtypeStruct((feat, rows), BF16),
            jax.ShapeDtypeStruct((feat, feat), BF16),
            jax.ShapeDtypeStruct((1, feat), F32),
            jax.ShapeDtypeStruct((blocks, 4, feat), F32),
        ],
        scratch_shapes=[pltpu.VMEM((feat, feat), F32)],
        compiler_params=params(),
        cost_estimate=pl.CostEstimate(
            flops=4 * feat * feat * rows, bytes_accessed=32 * 2**20, transcendentals=0
        ),
    )(f, b2, x1, attn, dy, da2, mod_blocks, o_t, w_proj)


def rows_back_kernel(dq_ref, w_ref, x_ref, dx_ref, mod_ref, out_ref, sums_ref):
    feat = x_ref.shape[-1]
    da = dot(dq_ref[0], w_ref[0:feat, :], 0, 0)
    for i in (1, 2):
        da = da + dot(dq_ref[i], w_ref[i * feat : (i + 1) * feat, :], 0, 0)
    normed, inverse = norm_parts(x_ref[...].reshape(BLK, feat).astype(F32))
    out = dx_ref[...] + norm_back(da * (1.0 + mod_ref[0, 1:2, :]), normed, inverse)
    out_ref[...] = out.astype(BF16).reshape(out_ref.shape)
    sums_ref[0, 0:1, :] = jnp.sum(da, axis=0, keepdims=True)
    sums_ref[0, 1:2, :] = jnp.sum(da * normed, axis=0, keepdims=True)


def rows_back(dqkv_t, w_t, x_view, dx1, mod_blocks):
    rows, feat = dx1.shape
    blocks = rows // BLK
    return pl.pallas_call(
        rows_back_kernel,
        grid=(blocks,),
        in_specs=[
            pl.BlockSpec((3, feat, BLK), lambda k: (0, 0, k)),
            whole(3 * feat, feat),
            row_spec(x_view.shape),
            pl.BlockSpec((BLK, feat), lambda k: (k, 0)),
            pl.BlockSpec((1, 6, feat), lambda k: (k, 0, 0)),
        ],
        out_specs=[row_spec(x_view.shape), pl.BlockSpec((1, 2, feat), lambda k: (k, 0, 0))],
        out_shape=[
            jax.ShapeDtypeStruct(x_view.shape, BF16),
            jax.ShapeDtypeStruct((blocks, 2, feat), F32),
        ],
        compiler_params=params(),
        cost_estimate=pl.CostEstimate(
            flops=6 * feat * feat * rows, bytes_accessed=20 * 2**20, transcendentals=0
        ),
    )(dqkv_t, w_t, x_view, dx1, mod_blocks)


def swap(values, axis, bit):
    count = lax.axis_size(axis)
    return lax.ppermute(values, axis, [(i, i ^ bit) for i in range(count)])


def add_low(left, right):
    return (left.astype(F32) + right.astype(F32)).astype(BF16)


def pick(values, index, dim):
    return lax.dynamic_index_in_dim(values, index, dim, keepdims=False)


def bits_of(wide):
    return [1 << i for i in range(wide.bit_length() - 1)]


def chain_orders(wide):
    bits = bits_of(wide)
    near, far = bits[:3], bits[3:]
    return [near[i:] + near[:i] + far for i in range(3)]


def scatter_chain(values, order):
    wide = values.shape[0]
    bits = bits_of(wide)
    values = values.reshape((2,) * len(bits) + values.shape[1:])
    dims = list(reversed(bits))
    me = lax.axis_index("wide")
    for bit in order:
        dim = dims.index(bit)
        own = (me // bit) % 2
        got = swap(pick(values, 1 - own, dim), "wide", bit)
        values = add_low(pick(values, own, dim), got)
        dims.pop(dim)
    return values


def scatter_sum(send, keep):
    got = swap(send, "narrow", 1)
    wide, rows = keep.shape[:2]
    third = rows // 3 // TILE * TILE
    cuts = [0, third, 2 * third, rows]
    parts = []
    for i, order in enumerate(chain_orders(wide)):
        cut = slice(cuts[i], cuts[i + 1])
        parts.append(scatter_chain(add_low(keep[:, cut], got[:, cut]), order))
    return jnp.concatenate(parts, axis=0)


def gather_slots(values):
    for bit in reversed(bits_of(lax.axis_size("wide"))):
        values = jnp.concatenate([values, swap(values, "wide", bit)], axis=0)
    return jnp.concatenate([values, swap(values, "narrow", 1)], axis=0)


def local(
    x_src,
    cond,
    lengths,
    bucket,
    w_mod,
    b_mod,
    w_qkv,
    b_qv,
    w_proj,
    b_proj,
    w_fc1,
    b_fc1,
    w_fc2,
    b_fc2,
    grad_out,
):
    wide = lax.axis_size("wide")
    halves = lax.axis_size("narrow")
    devices = wide * halves
    group = lax.axis_index("wide")
    half = lax.axis_index("narrow")
    rows, feat = x_src.shape
    hidden = w_fc1.shape[1]
    places = lengths.shape[0] // halves
    slots = places // wide
    blocks = rows // BLK
    per_block = BLK // wide
    tiled = per_block % TILE == 0

    lens = lax.dynamic_slice_in_dim(lengths, half * places, places)
    buck = lax.dynamic_slice_in_dim(bucket, half * places, places)
    split = regroup if tiled else regroup_any
    send, scond, seg, src, cidx = split(x_src, cond, lens, buck, group.reshape(1), wide)
    exchange = functools.partial(
        lax.all_to_all, axis_name="wide", split_axis=0, concat_axis=0, tiled=True
    )
    came = exchange(send)
    came_cond = exchange(scond.reshape(wide, slots, feat // wide))
    cond_in = came_cond.transpose(1, 0, 2).reshape(slots, feat)
    x_view = came.reshape(wide, blocks, per_block, feat)
    if not tiled:
        x_view = x_view.transpose(1, 0, 2, 3).reshape(1, blocks, BLK, feat)

    act, silu_back = jax.vjp(jax.nn.silu, cond_in.astype(F32))
    act_low = act.astype(BF16)
    modulate = jnp.dot(act_low, w_mod, preferred_element_type=F32) + b_mod.astype(F32)
    slot_ids = jnp.arange(slots, dtype=jnp.int32)
    in_slot = seg[:, None] == slot_ids[None, :]
    mod_blocks = jnp.sum(
        jnp.where(in_slot[:, :, None], modulate[None], 0.0), axis=1
    ).reshape(blocks, 6, feat)

    dy = (
        grad_out.reshape(blocks, per_block, wide, feat)
        .transpose(0, 2, 1, 3)
        .reshape(rows, feat)
    )
    gate_two = mod_blocks[:, 5:6, :]
    df = (
        (gate_two * dy.reshape(blocks, BLK, feat).astype(F32)).astype(BF16).reshape(rows, feat)
    )
    grad_b_fc2 = jnp.sum(df.astype(F32), axis=0)
    dg = dot(df, w_fc2, 1, 1)
    w_qkv_t = w_qkv.T
    bias_qkv = jnp.concatenate(
        [b_qv[:feat].astype(F32), jnp.zeros((feat,), F32), b_qv[feat:].astype(F32)]
    ).reshape(3 * feat, 1)

    qkv_t, a1_t = qkv_forward(x_view, mod_blocks, w_qkv_t, bias_qkv)
    o_t, lse = attend(seg, qkv_t)
    attn, x1, a2, a2_t = proj_forward(
        o_t, w_proj, b_proj.astype(F32).reshape(1, feat), x_view, mod_blocks
    )
    f, da2, d_fc1, d_fc2, grad_b_fc1 = mlp(
        a2, a2_t, df, dg, w_fc1, w_fc2, b_fc1.astype(F32).reshape(1, hidden)
    )

    part = feat // devices
    d_fc1 = d_fc1.reshape(hidden // feat, wide, halves, part, feat)
    d_fc2 = d_fc2.reshape(wide, halves, hidden // devices, feat)

    def mlp_half(which):
        one = pick(d_fc1, which, 2).transpose(1, 0, 2, 3).reshape(wide, -1, feat)
        return jnp.concatenate([pick(d_fc2, which, 1), one], axis=1)

    mlp_sum = scatter_sum(mlp_half(1 - half), mlp_half(half))

    y, dx1, do_t, d_proj, grad_b_proj, sums_two = middle(
        f, b_fc2.astype(F32).reshape(1, feat), x1, attn, dy, da2, mod_blocks, o_t, w_proj
    )
    y_dest = (
        y.reshape(blocks, wide, per_block, feat).transpose(0, 2, 1, 3).reshape(rows, feat)
    )
    dqkv_t = attend_back(seg, qkv_t, o_t, do_t, lse)

    a1_parts = a1_t.reshape(wide, halves, part, rows)
    d_proj = d_proj.reshape(wide, halves, part, feat)

    def qkv_half(which):
        mine = pick(a1_parts, which, 1).reshape(wide * part, rows)
        three = lax.dot_general(
            mine, dqkv_t, (((1,), (2,)), ((), ())), preferred_element_type=F32
        )
        three = three.reshape(wide, part, 3, feat).transpose(0, 2, 1, 3)
        return jnp.concatenate(
            [three.astype(BF16).reshape(wide, 3 * part, feat), pick(d_proj, which, 1)], axis=1
        )

    qkv_sum = scatter_sum(qkv_half(1 - half), qkv_half(half))
    sums_q = jnp.sum(dqkv_t.astype(F32), axis=2)
    grad_b_qv = jnp.concatenate([sums_q[0], sums_q[2]])

    drows, sums_one = rows_back(dqkv_t, w_qkv_t, x_view, dx1, mod_blocks)
    back = drows
    if not tiled:
        back = back.reshape(blocks, wide, per_block, feat).transpose(1, 0, 2, 3)
    back = exchange(back.reshape(wide, rows // wide, feat)).reshape(rows, feat)

    by_slot = in_slot.astype(F32)

    def slot_sums(sums):
        count = sums.shape[1]
        picked = jnp.where(in_slot[:, :, None, None], sums[:, None], 0.0)
        return jnp.sum(picked, axis=0).reshape(slots, count * feat).astype(BF16)

    dmod_two, dmod_one = slot_sums(sums_two), slot_sums(sums_one)
    dact = dot(dmod_two, w_mod[:, 2 * feat :], 1, 1) + dot(dmod_one, w_mod[:, : 2 * feat], 1, 1)
    dcond_in = silu_back(dact)[0].astype(BF16)
    back_cond = exchange(
        dcond_in.reshape(slots, wide, feat // wide).transpose(1, 0, 2)
    ).reshape(places, feat // wide)
    merge = restore if tiled else restore_any
    dx_src, dcond = merge(src, cidx, back, back_cond)

    me = group * halves + half
    two_all = gather_slots(jnp.concatenate([act_low, dmod_two], axis=1))
    one_all = gather_slots(dmod_one)
    act_mine = lax.dynamic_slice_in_dim(two_all[:, :feat], me * part, part, axis=1)
    dmod_all = jnp.concatenate([one_all, two_all[:, feat:]], axis=1)
    grad_w_mod = dot(act_mine, dmod_all, 0, 0)
    grad_b_mod = jnp.sum(
        lax.dynamic_slice_in_dim(dmod_all, me * 6 * part, 6 * part, axis=1).astype(F32), axis=0
    )

    biases = jnp.concatenate(
        [
            grad_b_fc1.reshape(devices, -1),
            grad_b_fc2.reshape(devices, -1),
            grad_b_proj.reshape(devices, -1),
            grad_b_qv.reshape(devices, -1),
        ],
        axis=1,
    )
    biases = jnp.sum(
        lax.all_to_all(biases, ("wide", "narrow"), split_axis=0, concat_axis=0, tiled=True), axis=0
    )
    at_two, at_proj, at_qv = 4 * part, 5 * part, 6 * part

    fc2_rows = hidden // devices
    grad_w_fc2 = mlp_sum[:fc2_rows].astype(F32)
    grad_w_fc1 = (
        mlp_sum[fc2_rows:]
        .reshape(hidden // feat, part, feat)
        .transpose(1, 0, 2)
        .reshape(part, hidden)
        .astype(F32)
    )
    grad_w_qkv = (
        qkv_sum[: 3 * part]
        .reshape(3, part, feat)
        .transpose(1, 0, 2)
        .reshape(part, 3 * feat)
        .astype(F32)
    )
    grad_w_proj = qkv_sum[3 * part :].astype(F32)
    return (
        y_dest,
        dx_src,
        dcond,
        grad_w_mod,
        grad_b_mod,
        grad_w_qkv,
        biases[at_qv:],
        grad_w_proj,
        biases[at_proj:at_qv],
        grad_w_fc1,
        biases[:at_two],
        grad_w_fc2,
        biases[at_two:at_proj],
    )


def solution(mesh):
    both = ("wide", "narrow")
    placed = (P("narrow", "wide"), P("narrow", "wide")) + (P(),) * 12 + (P(both, None),)
    matrix, vector = P(both, None), P(both)
    return jax.shard_map(
        local,
        mesh=mesh,
        in_specs=placed,
        out_specs=(
            matrix,
            P("narrow", "wide"),
            P("narrow", "wide"),
            matrix,
            vector,
            matrix,
            vector,
            matrix,
            vector,
            matrix,
            vector,
            matrix,
            vector,
        ),
        check_vma=False,
    )
```

```python
import functools
import math

import jax
import jax.numpy as jnp
from jax import lax
from jax.experimental import pallas as pl
from jax.experimental.pallas import tpu as pltpu
from jax.sharding import PartitionSpec as P

HEADS = 16
HEAD_DIM = 64
EPS = 1e-06
MASKED = -1000000000.0
LOG2E = 1.4426950408889634
BLK = 256
TILE = 16
VMEM_LIMIT = 58 * 2**20
BACK_ROUNDS = 3
BF16 = jnp.bfloat16
F32 = jnp.float32


def params(**more):
    return pltpu.CompilerParams(vmem_limit_bytes=VMEM_LIMIT, **more)


def dot(left, right, left_dim, right_dim):
    return lax.dot_general(
        left, right, (((left_dim,), (right_dim,)), ((), ())), preferred_element_type=F32
    )


def norm_parts(values):
    centre = values - jnp.mean(values, axis=1, keepdims=True)
    spread = jnp.mean(centre * centre, axis=1, keepdims=True)
    inverse = lax.rsqrt(spread + EPS)
    return centre * inverse, inverse


def norm_back(grad, normed, inverse):
    return (
        grad
        - jnp.mean(grad, axis=1, keepdims=True)
        - normed * jnp.mean(grad * normed, axis=1, keepdims=True)
    ) * inverse


def each_place(len_ref, buck_ref, off_ref, slot_ref, wide, visit):
    for i in range(wide):
        off_ref[i] = 0
        slot_ref[i] = 0

    def place(j, offset):
        units = len_ref[j] // wide
        b = buck_ref[j]

        @pl.when(units > 0)
        def _():
            start = off_ref[b]
            slot = slot_ref[b]
            off_ref[b] = start + units
            slot_ref[b] = slot + 1
            visit(j, b, units, offset, start, slot)

        return offset + units

    lax.fori_loop(0, len_ref.shape[0], place, 0)


def regroup_rows_kernel(len_ref, buck_ref, x_ref, send_ref, src_ref, off_ref, slot_ref, *, wide):
    cells = send_ref.shape[1]
    send_ref[...] = jnp.zeros_like(send_ref)

    @pl.loop(0, src_ref.shape[0])
    def _(i):
        src_ref[i] = -1

    def visit(j, b, units, offset, start, slot):
        @pl.loop(0, units // TILE)
        def _(t):
            a = pl.multiple_of(offset + t * TILE, TILE)
            c = pl.multiple_of(start + t * TILE, TILE)
            send_ref[b, pl.ds(c, TILE), :] = x_ref[pl.ds(a, TILE), :]
            src_ref[a // TILE] = (b * cells + c) // TILE

    each_place(len_ref, buck_ref, off_ref, slot_ref, wide, visit)


def regroup_cond_kernel(
    len_ref, buck_ref, me_ref, cond_ref, scond_ref, seg_ref, cidx_ref,
    off_ref, slot_ref, cond_in, cond_out, *, wide, slots,
):
    cond_out[...] = jnp.zeros_like(cond_out)
    cond_in[...] = cond_ref[...].astype(F32)
    for i in range(seg_ref.shape[0]):
        seg_ref[i] = -1

    @pl.loop(0, cidx_ref.shape[0])
    def _(j):
        cidx_ref[j] = -1

    def visit(j, b, units, offset, start, slot):
        cidx_ref[j] = b * slots + slot
        cond_out[pl.ds(b * slots + slot, 1), :] = cond_in[pl.ds(j, 1), :]

        @pl.when(b == me_ref[0])
        def _():
            @pl.loop(0, units * wide // BLK)
            def _(t):
                seg_ref[start * wide // BLK + t] = slot

    each_place(len_ref, buck_ref, off_ref, slot_ref, wide, visit)
    scond_ref[...] = cond_out[...].astype(BF16)


def regroup(x_src, cond, lens, buck, me, wide):
    rows, feat = x_src.shape
    places, part = cond.shape
    slots = places // wide
    smem = pl.BlockSpec(memory_space=pltpu.SMEM)
    vmem = pl.BlockSpec(memory_space=pltpu.VMEM)
    counters = [pltpu.SMEM((wide,), jnp.int32), pltpu.SMEM((wide,), jnp.int32)]
    scond, seg, cidx = pl.pallas_call(
        functools.partial(regroup_cond_kernel, wide=wide, slots=slots),
        in_specs=[smem, smem, smem, vmem],
        out_specs=[vmem, smem, smem],
        out_shape=[
            jax.ShapeDtypeStruct((places, part), BF16),
            jax.ShapeDtypeStruct((rows // BLK,), jnp.int32),
            jax.ShapeDtypeStruct((places,), jnp.int32),
        ],
        scratch_shapes=counters + [pltpu.VMEM((places, part), F32), pltpu.VMEM((places, part), F32)],
        compiler_params=params(),
    )(lens, buck, me, cond)
    send, src = pl.pallas_call(
        functools.partial(regroup_rows_kernel, wide=wide),
        in_specs=[smem, smem, vmem],
        out_specs=[vmem, smem],
        out_shape=[
            jax.ShapeDtypeStruct((wide, rows // wide, feat), BF16),
            jax.ShapeDtypeStruct((rows // TILE,), jnp.int32),
        ],
        scratch_shapes=counters,
        compiler_params=params(),
        cost_estimate=pl.CostEstimate(flops=0, bytes_accessed=16 * 2**20, transcendentals=0),
    )(lens, buck, x_src)
    return send, scond, seg, src, cidx


def restore_kernel(src_ref, back_ref, dx_ref):
    @pl.loop(0, src_ref.shape[0])
    def _(i):
        at = src_ref[i]
        rows = back_ref[pl.ds(pl.multiple_of(jnp.maximum(at, 0) * TILE, TILE), TILE), :]
        dx_ref[pl.ds(pl.multiple_of(i * TILE, TILE), TILE), :] = jnp.where(
            at >= 0, rows, jnp.zeros_like(rows)
        )


def restore(src, back):
    vmem = pl.BlockSpec(memory_space=pltpu.VMEM)
    return pl.pallas_call(
        restore_kernel,
        in_specs=[pl.BlockSpec(memory_space=pltpu.SMEM), vmem],
        out_specs=vmem,
        out_shape=jax.ShapeDtypeStruct(back.shape, BF16),
        compiler_params=params(),
    )(src, back)


def regroup_any(x_src, cond, lens, buck, me, wide):
    rows, feat = x_src.shape
    places = lens.shape[0]
    slots, cells = places // wide, rows // wide
    units = lens // wide
    order = jnp.arange(places, dtype=jnp.int32)
    earlier = (order[:, None] < order[None, :]) & (buck[:, None] == buck[None, :])
    live = (lens > 0).astype(jnp.int32)
    offset = jnp.cumsum(units) - units
    start = jnp.sum(jnp.where(earlier, units[:, None], 0), axis=0)
    slot = jnp.sum(jnp.where(earlier, live[:, None], 0), axis=0)
    cell = jnp.arange(cells, dtype=jnp.int32)[None, :, None]
    to_target = (buck[None, :] == jnp.arange(wide, dtype=jnp.int32)[:, None]) & (live[None, :] > 0)
    hit = (
        to_target[:, None, :]
        & (cell >= start[None, None, :])
        & (cell < (start + units)[None, None, :])
    ).astype(jnp.int32)
    valid = jnp.sum(hit, axis=2)
    source = jnp.sum(hit * (offset - start)[None, None, :], axis=2) + cell[:, :, 0]
    source = jnp.where(valid > 0, source, 0)
    picked = jnp.take(x_src, source.reshape(-1), axis=0).reshape(wide, cells, feat)
    send = jnp.where(valid[:, :, None] > 0, picked, jnp.zeros((), BF16))
    cond_hit = to_target[:, None, :] & (
        slot[None, None, :] == jnp.arange(slots, dtype=jnp.int32)[None, :, None]
    )
    scond = jnp.einsum("wqs,sf->wqf", cond_hit.astype(BF16), cond, preferred_element_type=F32)
    scond = scond.astype(BF16).reshape(cond.shape)
    first = jnp.arange(rows // BLK, dtype=jnp.int32)[:, None] * BLK
    mine = (
        ((buck == me[0]) & (live > 0))[None, :]
        & (first >= (start * wide)[None, :])
        & (first < ((start + units) * wide)[None, :])
    )
    seg = jnp.sum(jnp.where(mine, slot[None, :] + 1, 0), axis=1) - 1
    spot = jnp.arange(rows, dtype=jnp.int32)[:, None]
    inside = (live[None, :] > 0) & (spot >= offset[None, :]) & (spot < (offset + units)[None, :])
    src = jnp.sum(jnp.where(inside, (buck * cells + start - offset)[None, :] + spot + 1, 0), axis=1)
    cidx = jnp.where(live > 0, buck * slots + slot, -1)
    return send, scond, seg.astype(jnp.int32), src - 1, cidx


def restore_any(src, back):
    dx = jnp.take(back, jnp.maximum(src, 0), axis=0)
    return jnp.where(src[:, None] >= 0, dx, jnp.zeros((), BF16))


def qkv_kernel(x_ref, mod_ref, w_ref, b_ref, q_ref, a_ref):
    feat = x_ref.shape[-1]
    x = x_ref[...].reshape(BLK, feat).astype(F32)
    normed, _ = norm_parts(x)
    a1 = (normed * (1.0 + mod_ref[0, 1:2, :]) + mod_ref[0, 0:1, :]).astype(BF16)
    a1_t = a1.T
    a_ref[...] = a1_t
    for i in range(3):
        part = slice(i * feat, (i + 1) * feat)
        q_ref[part, :] = (dot(w_ref[part, :], a1_t, 1, 0) + b_ref[part, :]).astype(BF16)


def row_spec(view):
    return pl.BlockSpec((view[0], 1, view[2], view[3]), lambda k: (0, k, 0, 0))


def whole(*shape):
    return pl.BlockSpec(shape, lambda k: (0,) * len(shape))


def qkv_forward(x_view, mod_blocks, w_t, bias):
    feat = x_view.shape[-1]
    blocks = x_view.shape[1]
    return pl.pallas_call(
        qkv_kernel,
        grid=(blocks,),
        in_specs=[
            row_spec(x_view.shape),
            pl.BlockSpec((1, 6, feat), lambda k: (k, 0, 0)),
            whole(3 * feat, feat),
            whole(3 * feat, 1),
        ],
        out_specs=[
            pl.BlockSpec((3 * feat, BLK), lambda k: (0, k)),
            pl.BlockSpec((feat, BLK), lambda k: (0, k)),
        ],
        out_shape=[
            jax.ShapeDtypeStruct((3 * feat, blocks * BLK), BF16),
            jax.ShapeDtypeStruct((feat, blocks * BLK), BF16),
        ],
        compiler_params=params(),
        cost_estimate=pl.CostEstimate(
            flops=6 * feat * feat * blocks * BLK, bytes_accessed=20 * 2**20, transcendentals=0
        ),
    )(x_view, mod_blocks, w_t, bias)


def masks(seg_ref, query_block, blocks):
    base = LOG2E / math.sqrt(HEAD_DIM)
    same = [seg_ref[query_block] == seg_ref[kb] for kb in range(blocks)]
    scales = [jnp.where(s, base, 0.0) for s in same]
    shifts = [jnp.where(s, 0.0, MASKED * LOG2E) for s in same]
    return scales, shifts


def attend_kernel(seg_ref, q_ref, k_ref, v_ref, o_ref, lse_ref, *, blocks, heads):
    for h in range(heads):
        hs = slice(h * HEAD_DIM, (h + 1) * HEAD_DIM)
        keys = k_ref[hs, :].T
        v_t = v_ref[hs, :]
        for qb in range(blocks):
            qs = slice(qb * BLK, (qb + 1) * BLK)
            q_t = q_ref[hs, qs]
            scales, shifts = masks(seg_ref, qb, blocks)
            scores = [dot(keys[kb * BLK : (kb + 1) * BLK], q_t, 1, 0) for kb in range(blocks)]
            top = None
            for kb in range(blocks):
                peak = jnp.max(scores[kb], axis=0, keepdims=True) * scales[kb] + shifts[kb]
                top = peak if top is None else jnp.maximum(top, peak)
            total = jnp.zeros((1, BLK), F32)
            parts = []
            for kb in range(blocks):
                expo = jnp.exp2(scores[kb] * scales[kb] - (top - shifts[kb]))
                total = total + jnp.sum(expo, axis=0, keepdims=True)
                parts.append(expo.astype(BF16))
            out = dot(v_t, jnp.concatenate(parts, axis=0), 1, 0)
            o_ref[hs, qs] = (out / total).astype(BF16)
            lse_ref[h, :, qs] = top + jnp.log2(total)


def attend(seg, qkv_t, heads=2):
    feat3, rows = qkv_t.shape
    feat = feat3 // 3
    span = heads * HEAD_DIM
    groups = feat // span
    return pl.pallas_call(
        functools.partial(attend_kernel, blocks=rows // BLK, heads=heads),
        grid_spec=pltpu.PrefetchScalarGridSpec(
            num_scalar_prefetch=1,
            grid=(groups,),
            in_specs=[
                pl.BlockSpec((span, rows), lambda g, s: (g, 0)),
                pl.BlockSpec((span, rows), lambda g, s: (groups + g, 0)),
                pl.BlockSpec((span, rows), lambda g, s: (2 * groups + g, 0)),
            ],
            out_specs=[
                pl.BlockSpec((span, rows), lambda g, s: (g, 0)),
                pl.BlockSpec((heads, 1, rows), lambda g, s: (g, 0, 0)),
            ],
        ),
        out_shape=[
            jax.ShapeDtypeStruct((feat, rows), BF16),
            jax.ShapeDtypeStruct((feat // HEAD_DIM, 1, rows), F32),
        ],
        compiler_params=params(),
        cost_estimate=pl.CostEstimate(
            flops=16 * feat * rows * rows, bytes_accessed=8 * 2**20, transcendentals=16 * rows * rows
        ),
    )(seg, qkv_t, qkv_t, qkv_t)


def attend_back_kernel(
    seg_ref, q_ref, k_ref, v_ref, o_ref, do_ref, lse_ref, out_ref, *, blocks, heads
):
    scale = 1.0 / math.sqrt(HEAD_DIM)
    for h in range(heads):
        hs = slice(h * HEAD_DIM, (h + 1) * HEAD_DIM)
        k_t = k_ref[hs, :]
        keys, values = k_t.T, v_ref[hs, :].T
        inner = jnp.sum(
            o_ref[hs, :].astype(F32) * do_ref[hs, :].astype(F32), axis=0, keepdims=True
        )
        grad_k = grad_v = None
        for qb in range(blocks):
            qs = slice(qb * BLK, (qb + 1) * BLK)
            q_t, do_t = q_ref[hs, qs], do_ref[hs, qs]
            scales, shifts = masks(seg_ref, qb, blocks)
            probs, grads = [], []
            for kb in range(blocks):
                ks = slice(kb * BLK, (kb + 1) * BLK)
                score = dot(keys[ks], q_t, 1, 0)
                grad_p = dot(values[ks], do_t, 1, 0)
                prob = jnp.exp2(score * scales[kb] - (lse_ref[h, :, qs] - shifts[kb]))
                probs.append(prob.astype(BF16))
                grads.append((prob * (grad_p - inner[:, qs])).astype(BF16))
            probs = jnp.concatenate(probs, axis=0)
            grads = jnp.concatenate(grads, axis=0)
            out_ref[0, hs, qs] = (dot(k_t, grads, 1, 0) * scale).astype(BF16)
            more_k, more_v = dot(q_t, grads, 1, 1), dot(do_t, probs, 1, 1)
            grad_k = more_k if grad_k is None else grad_k + more_k
            grad_v = more_v if grad_v is None else grad_v + more_v
        out_ref[1, hs, :] = (grad_k * scale).astype(BF16)
        out_ref[2, hs, :] = grad_v.astype(BF16)


def attend_back(seg, qkv_t, o_t, do_t, lse, first, count, heads=2):
    feat3, rows = qkv_t.shape
    feat = feat3 // 3
    span = heads * HEAD_DIM
    groups = feat // span
    at = first // heads
    return pl.pallas_call(
        functools.partial(attend_back_kernel, blocks=rows // BLK, heads=heads),
        grid_spec=pltpu.PrefetchScalarGridSpec(
            num_scalar_prefetch=1,
            grid=(count // heads,),
            in_specs=[
                pl.BlockSpec((span, rows), lambda g, s: (at + g, 0)),
                pl.BlockSpec((span, rows), lambda g, s: (groups + at + g, 0)),
                pl.BlockSpec((span, rows), lambda g, s: (2 * groups + at + g, 0)),
                pl.BlockSpec((span, rows), lambda g, s: (at + g, 0)),
                pl.BlockSpec((span, rows), lambda g, s: (at + g, 0)),
                pl.BlockSpec((heads, 1, rows), lambda g, s: (at + g, 0, 0)),
            ],
            out_specs=pl.BlockSpec((3, span, rows), lambda g, s: (0, g, 0)),
        ),
        out_shape=jax.ShapeDtypeStruct((3, count * HEAD_DIM, rows), BF16),
        compiler_params=params(),
        cost_estimate=pl.CostEstimate(
            flops=24 * count * HEAD_DIM * rows * rows,
            bytes_accessed=count * 2**20,
            transcendentals=count * rows * rows,
        ),
    )(seg, qkv_t, qkv_t, qkv_t, o_t, do_t, lse)


class Halves:
    def __init__(self, wide, part):
        self.wide, self.part = wide, part
        self.split = part % TILE == 0

    def shapes(self, between, columns):
        if self.split:
            shape = (self.wide,) + between + (self.part, columns)
            return [jax.ShapeDtypeStruct(shape, BF16)] * 2
        return [jax.ShapeDtypeStruct(between + (2 * self.wide * self.part, columns), BF16)]

    def specs(self, between, columns, index):
        ones = (1,) * between
        if self.split:
            return [
                pl.BlockSpec(
                    (self.wide,) + ones + (self.part, columns),
                    lambda *g: (0,) + index(*g)[:-1] + (0, index(*g)[-1]),
                )
            ] * 2
        return [
            pl.BlockSpec(
                ones + (2 * self.wide * self.part, columns),
                lambda *g: index(*g)[:-1] + (0, index(*g)[-1]),
            )
        ]

    def store(self, half, value, refs):
        if not self.split:
            refs[0][...] = value.astype(BF16).reshape(refs[0].shape)
            return
        value = value.reshape(value.shape[0] // (2 * self.part), 2, self.part, value.shape[1])
        even, odd = value[:, 0], value[:, 1]
        refs[0][...] = jnp.where(half == 0, odd, even).astype(BF16).reshape(refs[0].shape)
        refs[1][...] = jnp.where(half == 0, even, odd).astype(BF16).reshape(refs[1].shape)

    def finish(self, arrays):
        if self.split:
            return [a.reshape(self.wide, -1, a.shape[-1]) for a in arrays]
        return arrays


def qkv_grad_kernel(half_ref, a_ref, *refs, pieces, halves):
    ins, outs, sums_ref = refs[:pieces], refs[pieces:-1], refs[-1]
    ones = jnp.ones((8, a_ref.shape[1]), BF16)
    value = jnp.concatenate([dot(a_ref[...], r[0], 1, 1) for r in ins], axis=1)
    halves.store(half_ref[0], value, outs)
    sums_ref[0] = jnp.concatenate([dot(ones, r[0], 1, 1) for r in ins], axis=1)


def qkv_grad(half, a1_t, dqkv, halves):
    feat, rows = a1_t.shape
    span = dqkv[0].shape[1]
    columns = span * len(dqkv)
    out = pl.pallas_call(
        functools.partial(qkv_grad_kernel, pieces=len(dqkv), halves=halves),
        grid=(3,),
        in_specs=[pl.BlockSpec(memory_space=pltpu.SMEM), whole(feat, rows)]
        + [pl.BlockSpec((1, span, rows), lambda i: (i, 0, 0))] * len(dqkv),
        out_specs=halves.specs(1, columns, lambda i: (i, 0))
        + [pl.BlockSpec((1, 8, columns), lambda i: (i, 0, 0))],
        out_shape=halves.shapes((3,), columns) + [jax.ShapeDtypeStruct((3, 8, columns), F32)],
        compiler_params=params(),
        cost_estimate=pl.CostEstimate(
            flops=6 * feat * rows * columns, bytes_accessed=12 * 2**20, transcendentals=0
        ),
    )(half, a1_t, *dqkv)
    return halves.finish(out[:-1]), out[-1][:, 0, :]


def proj_kernel(o_ref, w_ref, b_ref, x_ref, mod_ref, attn_ref, x1_ref, a_ref, at_ref):
    feat = x_ref.shape[-1]
    attn = dot(o_ref[...], w_ref[...], 0, 0) + b_ref[...]
    attn_ref[...] = attn
    x1 = x_ref[...].reshape(BLK, feat).astype(F32) + mod_ref[0, 2:3, :] * attn
    x1_ref[...] = x1
    normed, _ = norm_parts(x1)
    a2 = (normed * (1.0 + mod_ref[0, 4:5, :]) + mod_ref[0, 3:4, :]).astype(BF16)
    a_ref[...] = a2
    at_ref[...] = a2.T


def proj_forward(o_t, w_proj, b_proj, x_view, mod_blocks):
    feat = x_view.shape[-1]
    blocks = x_view.shape[1]
    rows = blocks * BLK
    by_row = pl.BlockSpec((BLK, feat), lambda k: (k, 0))
    by_column = pl.BlockSpec((feat, BLK), lambda k: (0, k))
    return pl.pallas_call(
        proj_kernel,
        grid=(blocks,),
        in_specs=[
            by_column,
            whole(feat, feat),
            whole(1, feat),
            row_spec(x_view.shape),
            pl.BlockSpec((1, 6, feat), lambda k: (k, 0, 0)),
        ],
        out_specs=[by_row, by_row, by_row, by_column],
        out_shape=[
            jax.ShapeDtypeStruct((rows, feat), F32),
            jax.ShapeDtypeStruct((rows, feat), F32),
            jax.ShapeDtypeStruct((rows, feat), BF16),
            jax.ShapeDtypeStruct((feat, rows), BF16),
        ],
        compiler_params=params(),
        cost_estimate=pl.CostEstimate(
            flops=2 * feat * feat * rows, bytes_accessed=20 * 2**20, transcendentals=0
        ),
    )(o_t, w_proj, b_proj, x_view, mod_blocks)


def gelu_both(u):
    c = math.sqrt(2.0 / math.pi)
    square = u * u
    t = jnp.tanh(u * (c + (c * 0.044715) * square))
    half = 0.5 + 0.5 * t
    slope = half + (0.5 * u) * (1.0 - t * t) * (c + (3.0 * c * 0.044715) * square)
    return u * half, slope


def mlp_kernel(
    half_ref, a_ref, at_ref, df_ref, dg_ref, w1_ref, w2_ref, b1_ref, *refs, first, second
):
    f_ref, da_ref, db_ref = refs[:3]
    g_ref, du_ref = refs[-2:]
    outs = refs[3:-2]
    outs_one, outs_two = outs[: len(outs) // 2], outs[len(outs) // 2 :]
    step = pl.program_id(0)
    rows = a_ref.shape[0]

    @pl.when(step == 0)
    def _():
        f_ref[...] = jnp.zeros_like(f_ref)
        da_ref[...] = jnp.zeros_like(da_ref)

    w1, w2 = w1_ref[...], w2_ref[...]
    bias = jnp.zeros((1, w1.shape[1]), F32)
    for r in range(rows // BLK):
        rs = slice(r * BLK, (r + 1) * BLK)
        u = dot(a_ref[rs, :], w1, 1, 0) + b1_ref[...]
        g, slope = gelu_both(u)
        g = g.astype(BF16)
        du = (dg_ref[rs, :] * slope).astype(BF16)
        g_ref[rs, :] = g
        du_ref[rs, :] = du
        bias = bias + jnp.sum(du.astype(F32), axis=0, keepdims=True)
        f_ref[rs, :] += dot(g, w2, 1, 0)
        da_ref[rs, :] += dot(du, w1, 1, 1)
    db_ref[...] = bias
    first.store(half_ref[0], dot(at_ref[...], du_ref[...], 1, 0), outs_one)
    second.store(half_ref[0], dot(g_ref[...], df_ref[...], 0, 0), outs_two)


def mlp(half, a2, a2_t, df, dg, w1, w2, b1, halves, width=512):
    rows, feat = a2.shape
    hidden = w1.shape[1]
    per = feat // width
    wide = halves.wide
    part = hidden // (2 * wide)
    first = halves
    second = Halves(wide, part)
    second.split = halves.split
    one = pl.Buffered(1)

    def fixed(*shape):
        return pl.BlockSpec(shape, lambda j: (0,) * len(shape), pipeline_mode=one)

    if halves.split:
        two_specs = [pl.BlockSpec((width // (2 * part), part, feat), lambda j: (j, 0, 0))] * 2
        two_shapes = [jax.ShapeDtypeStruct((wide, part, feat), BF16)] * 2
    else:
        two_specs = [pl.BlockSpec((width, feat), lambda j: (j, 0))]
        two_shapes = [jax.ShapeDtypeStruct((hidden, feat), BF16)]
    out = pl.pallas_call(
        functools.partial(mlp_kernel, first=first, second=second),
        grid=(hidden // width,),
        in_specs=[
            pl.BlockSpec(memory_space=pltpu.SMEM),
            fixed(rows, feat),
            fixed(feat, rows),
            fixed(rows, feat),
            pl.BlockSpec((rows, width), lambda j: (0, j)),
            pl.BlockSpec((feat, width), lambda j: (0, j)),
            pl.BlockSpec((width, feat), lambda j: (j, 0)),
            pl.BlockSpec((1, width), lambda j: (0, j)),
        ],
        out_specs=[whole(rows, feat), whole(rows, feat), pl.BlockSpec((1, width), lambda j: (0, j))]
        + halves.specs(1, width, lambda j: (j // per, j % per))
        + two_specs,
        out_shape=[
            jax.ShapeDtypeStruct((rows, feat), F32),
            jax.ShapeDtypeStruct((rows, feat), F32),
            jax.ShapeDtypeStruct((1, hidden), F32),
        ]
        + halves.shapes((hidden // feat,), feat)
        + two_shapes,
        scratch_shapes=[pltpu.VMEM((rows, width), BF16), pltpu.VMEM((rows, width), BF16)],
        compiler_params=params(),
        cost_estimate=pl.CostEstimate(
            flops=10 * rows * feat * hidden, bytes_accessed=64 * 2**20, transcendentals=rows * hidden
        ),
    )(half, a2, a2_t, df, dg, w1, w2, b1)
    f, da2, bias = out[:3]
    rest = out[3:]
    count = len(rest) // 2
    return f, da2, bias, first.finish(rest[:count]), second.finish(rest[count:])


def middle_kernel(
    half_ref, f_ref, b2_ref, x1_ref, attn_ref, dy_ref, da_ref, mod_ref, o_ref, w_ref,
    y_ref, dx_ref, do_ref, db_ref, sums_ref, *rest, halves,
):
    k = pl.program_id(0)
    outs, acc_ref = rest[:-1], rest[-1]

    @pl.when(k == 0)
    def _():
        acc_ref[...] = jnp.zeros_like(acc_ref)
        db_ref[...] = jnp.zeros_like(db_ref)

    f = f_ref[...] + b2_ref[...]
    x1 = x1_ref[...]
    dy = dy_ref[...].astype(F32)
    y_ref[...] = (x1 + mod_ref[0, 5:6, :] * f).astype(BF16)
    normed, inverse = norm_parts(x1)
    da = da_ref[...]
    dx1 = dy + norm_back(da * (1.0 + mod_ref[0, 4:5, :]), normed, inverse)
    dx_ref[...] = dx1
    dattn = (mod_ref[0, 2:3, :] * dx1).astype(BF16)
    db_ref[...] += jnp.sum(dattn.astype(F32), axis=0, keepdims=True)
    sums_ref[0, 0:1, :] = jnp.sum(dx1 * attn_ref[...], axis=0, keepdims=True)
    sums_ref[0, 1:2, :] = jnp.sum(da, axis=0, keepdims=True)
    sums_ref[0, 2:3, :] = jnp.sum(da * normed, axis=0, keepdims=True)
    sums_ref[0, 3:4, :] = jnp.sum(dy * f, axis=0, keepdims=True)
    do_ref[...] = dot(w_ref[...], dattn, 1, 1).astype(BF16)
    acc_ref[...] += dot(o_ref[...], dattn, 1, 0)

    @pl.when(k == pl.num_programs(0) - 1)
    def _():
        halves.store(half_ref[0], acc_ref[...], outs)


def middle(half, f, b2, x1, attn, dy, da2, mod_blocks, o_t, w_proj, halves):
    rows, feat = x1.shape
    by_row = pl.BlockSpec((BLK, feat), lambda k: (k, 0))
    by_column = pl.BlockSpec((feat, BLK), lambda k: (0, k))
    blocks = rows // BLK
    out = pl.pallas_call(
        functools.partial(middle_kernel, halves=halves),
        grid=(blocks,),
        in_specs=[
            pl.BlockSpec(memory_space=pltpu.SMEM),
            by_row, whole(1, feat), by_row, by_row, by_row, by_row,
            pl.BlockSpec((1, 6, feat), lambda k: (k, 0, 0)),
            by_column, whole(feat, feat),
        ],
        out_specs=[
            by_row, by_row, by_column, whole(1, feat),
            pl.BlockSpec((1, 4, feat), lambda k: (k, 0, 0)),
        ] + halves.specs(0, feat, lambda k: (0,)),
        out_shape=[
            jax.ShapeDtypeStruct((rows, feat), BF16),
            jax.ShapeDtypeStruct((rows, feat), F32),
            jax.ShapeDtypeStruct((feat, rows), BF16),
            jax.ShapeDtypeStruct((1, feat), F32),
            jax.ShapeDtypeStruct((blocks, 4, feat), F32),
        ]
        + halves.shapes((), feat),
        scratch_shapes=[pltpu.VMEM((feat, feat), F32)],
        compiler_params=params(),
        cost_estimate=pl.CostEstimate(
            flops=4 * feat * feat * rows, bytes_accessed=32 * 2**20, transcendentals=0
        ),
    )(half, f, b2, x1, attn, dy, da2, mod_blocks, o_t, w_proj)
    return tuple(out[:5]) + (halves.finish(out[5:]),)


def rows_back_kernel(w_ref, x_ref, dx_ref, mod_ref, *refs):
    out_ref, sums_ref = refs[-2:]
    feat = x_ref.shape[-1]
    span = refs[0].shape[1]
    da = None
    for i in range(3):
        for g, ref in enumerate(refs[:-2]):
            at = i * feat + g * span
            more = dot(ref[i], w_ref[at : at + span, :], 0, 0)
            da = more if da is None else da + more
    normed, inverse = norm_parts(x_ref[...].reshape(BLK, feat).astype(F32))
    out = dx_ref[...] + norm_back(da * (1.0 + mod_ref[0, 1:2, :]), normed, inverse)
    out_ref[...] = out.astype(BF16).reshape(out_ref.shape)
    sums_ref[0, 0:1, :] = jnp.sum(da, axis=0, keepdims=True)
    sums_ref[0, 1:2, :] = jnp.sum(da * normed, axis=0, keepdims=True)


def rows_back(dqkv, w_t, x_view, dx1, mod_blocks):
    rows, feat = dx1.shape
    blocks = rows // BLK
    span = dqkv[0].shape[1]
    return pl.pallas_call(
        rows_back_kernel,
        grid=(blocks,),
        in_specs=[
            whole(3 * feat, feat),
            row_spec(x_view.shape),
            pl.BlockSpec((BLK, feat), lambda k: (k, 0)),
            pl.BlockSpec((1, 6, feat), lambda k: (k, 0, 0)),
        ]
        + [pl.BlockSpec((3, span, BLK), lambda k: (0, 0, k))] * len(dqkv),
        out_specs=[row_spec(x_view.shape), pl.BlockSpec((1, 2, feat), lambda k: (k, 0, 0))],
        out_shape=[
            jax.ShapeDtypeStruct(x_view.shape, BF16),
            jax.ShapeDtypeStruct((blocks, 2, feat), F32),
        ],
        compiler_params=params(),
        cost_estimate=pl.CostEstimate(
            flops=6 * feat * feat * rows, bytes_accessed=20 * 2**20, transcendentals=0
        ),
    )(w_t, x_view, dx1, mod_blocks, *dqkv)


def mod_grad_kernel(
    ids_ref, one_ref, two_ref, w_ref, gw_ref, gb_ref, dact_ref, bias_ref, act_ref, *, part, slots
):
    early = one_ref.shape[1]
    feat = early // 2
    rows = one_ref.shape[0]
    first = lax.broadcasted_iota(jnp.int32, (rows, 1), 0) % (2 * slots) < slots
    act = pltpu.roll(two_ref[:, :feat].astype(F32), rows - slots, 0)
    act_ref[...] = jnp.where(first, act, 0.0).T
    act = act_ref[pl.ds(pl.multiple_of(ids_ref[1] * part, 8), part), :].astype(BF16)
    one, two = one_ref[...], two_ref[...]
    gw_ref[:, :early] = dot(act, one, 1, 0)
    gw_ref[:, early:] = dot(act, two, 1, 0)
    one_wide = one.astype(F32)
    gb_ref[:, :early] = jnp.sum(jnp.where(first, one_wide, 0.0), axis=0, keepdims=True)
    gb_ref[:, early:] = jnp.sum(jnp.where(first, two.astype(F32), 0.0), axis=0, keepdims=True)
    dact_ref[...] = dot(one, w_ref[:, :early], 1, 1) + dot(two, w_ref[:, early:], 1, 1)
    bias_ref[...] = jnp.sum(one_wide.reshape(rows // (2 * slots), 2 * slots, early), axis=0)


def mod_grad(group, me, one, two, w_mod, part, share, slots):
    count, early = one.shape
    feat, columns = w_mod.shape

    def fixed(i, ids):
        return (0, 0)

    return pl.pallas_call(
        functools.partial(mod_grad_kernel, part=part, slots=slots),
        grid_spec=pltpu.PrefetchScalarGridSpec(
            num_scalar_prefetch=1,
            grid=(1,),
            in_specs=[
                pl.BlockSpec(one.shape, fixed),
                pl.BlockSpec(two.shape, fixed),
                pl.BlockSpec((share, columns), lambda i, ids: (ids[0], 0)),
            ],
            out_specs=[
                pl.BlockSpec((part, columns), fixed),
                pl.BlockSpec((1, columns), fixed),
                pl.BlockSpec((count, share), fixed),
                pl.BlockSpec((2 * slots, early), fixed),
            ],
            scratch_shapes=[pltpu.VMEM((feat, count), F32)],
        ),
        out_shape=[
            jax.ShapeDtypeStruct((part, columns), F32),
            jax.ShapeDtypeStruct((1, columns), F32),
            jax.ShapeDtypeStruct((count, share), F32),
            jax.ShapeDtypeStruct((2 * slots, early), F32),
        ],
        compiler_params=params(),
    )(jnp.stack([group, me]), one, two, w_mod)


def swap(values, axis, bit):
    count = lax.axis_size(axis)
    return lax.ppermute(values, axis, [(i, i ^ bit) for i in range(count)])


def bits_of(wide):
    return [1 << i for i in range(wide.bit_length() - 1)]


def chain_orders(wide):
    bits = bits_of(wide)
    near, far = bits[:3], bits[3:]
    return [near[i:] + near[:i] + far for i in range(3)]


class Part:
    def __init__(self, keep, got, start, rows, order):
        wide, stride, columns = keep.shape
        self.keep = (keep.reshape(wide * stride, columns), start, stride)
        self.got = (got.reshape(wide * stride, columns), start, stride)
        self.rows = rows
        self.dims = list(reversed(bits_of(wide)))
        self.order = list(order)


def relay_kernel(me_ref, *refs, plan, inputs):
    ins, outs = refs[:inputs], refs[inputs:]
    for keep, got, rows, bit, inner, count, targets in plan:
        k_ref, g_ref = ins[keep[0]], ins[got[0]]

        def total(entry, keep=keep, got=got, rows=rows, k_ref=k_ref, g_ref=g_ref):
            left = k_ref[pl.ds(pl.multiple_of(keep[1] + entry * keep[2], TILE), rows), :]
            right = g_ref[pl.ds(pl.multiple_of(got[1] + entry * got[2], TILE), rows), :]
            return left.astype(F32) + right.astype(F32)

        if bit is None:
            outs[targets[0][0]][...] = total(0)
            continue
        own = (me_ref[0] // bit) % 2

        @pl.loop(0, count // 2)
        def _(i, own=own, rows=rows, inner=inner, targets=targets, total=total):
            outer = (i // inner) * 2 * inner + i % inner
            for which, (out, base) in zip((1 - own, own), targets, strict=True):
                to = pl.multiple_of(base + i * rows, TILE)
                outs[out][pl.ds(to, rows), :] = total(outer + which * inner).astype(BF16)


def relay(me, parts):
    arrays, plan, shapes, buffers = [], [], [], {}

    def index(array):
        for i, known in enumerate(arrays):
            if known is array:
                return i
        arrays.append(array)
        return len(arrays) - 1

    columns = parts[0].keep[0].shape[1]
    bits = sorted({p.order[0] for p in parts if p.order})
    sizes = {b: 0 for b in bits}
    for p in parts:
        keep, got = (index(p.keep[0]),) + p.keep[1:], (index(p.got[0]),) + p.got[1:]
        count = 1 << len(p.dims)
        if not p.order:
            plan.append([keep, got, p.rows, None, 1, 1, [(len(bits) + len(shapes), 0)]])
            shapes.append(jax.ShapeDtypeStruct((p.rows, columns), F32))
            continue
        bit = p.order[0]
        at = p.dims.index(bit)
        inner = 1 << (len(p.dims) - 1 - at)
        targets = [(bits.index(bit), sizes[bit]), (len(bits) + len(shapes), 0)]
        plan.append([keep, got, p.rows, bit, inner, count, targets])
        p.got = (None, sizes[bit], p.rows)
        sizes[bit] += count // 2 * p.rows
        shapes.append(jax.ShapeDtypeStruct((count // 2 * p.rows, columns), BF16))
        p.dims.pop(at)
    sends = [jax.ShapeDtypeStruct((sizes[b], columns), BF16) for b in bits]
    vmem = pl.BlockSpec(memory_space=pltpu.VMEM)
    out = pl.pallas_call(
        functools.partial(relay_kernel, plan=plan, inputs=len(arrays)),
        in_specs=[pl.BlockSpec(memory_space=pltpu.SMEM)] + [vmem] * len(arrays),
        out_specs=[vmem] * (len(sends) + len(shapes)),
        out_shape=sends + shapes,
        compiler_params=params(),
    )(me, *arrays)
    for p, kept in zip(parts, out[len(bits) :], strict=True):
        p.keep = (kept, 0, p.rows)
    return dict(zip(bits, out))


class Sums:
    def __init__(self, me, parts):
        self.me, self.parts = me, parts
        self.going = relay(me, parts)

    def step(self):
        came = {bit: swap(send, "wide", bit) for bit, send in self.going.items()}
        for p in self.parts:
            bit = p.order.pop(0)
            p.got = (came[bit],) + p.got[1:]
        self.going = relay(self.me, self.parts)

    def arrays(self):
        return tuple(self.going.values()) + tuple(p.keep[0] for p in self.parts)

    def put(self, arrays):
        count = len(self.going)
        self.going = dict(zip(self.going, arrays[:count], strict=True))
        for p, kept in zip(self.parts, arrays[count:], strict=True):
            p.keep = (kept,) + p.keep[1:]


class Gather:
    def __init__(self, values):
        self.values = values
        self.done = []

    def step(self, bit):
        got = swap(self.values, "narrow", 1) if bit is None else swap(self.values, "wide", bit)
        self.values = jnp.concatenate([self.values, got], axis=0)
        self.done.append(bit)

    def place(self, difference):
        at = jnp.zeros_like(difference)
        for i, bit in enumerate(self.done):
            if bit is not None:
                at = at + ((difference // bit) % 2) * (1 << i)
        return at

    def arrays(self):
        return (self.values,)

    def put(self, arrays):
        (self.values,) = arrays


def tie(values, moving):
    out = lax.optimization_barrier((tuple(values), tuple(m.arrays() for m in moving)))
    for one, kept in zip(moving, out[1], strict=True):
        one.put(kept)
    return out[0]


def local(
    x_src,
    cond,
    lengths,
    bucket,
    w_mod,
    b_mod,
    w_qkv,
    b_qv,
    w_proj,
    b_proj,
    w_fc1,
    b_fc1,
    w_fc2,
    b_fc2,
    grad_out,
):
    wide = lax.axis_size("wide")
    halves = lax.axis_size("narrow")
    devices = wide * halves
    group = lax.axis_index("wide")
    half = lax.axis_index("narrow")
    rows, feat = x_src.shape
    hidden = w_fc1.shape[1]
    places = lengths.shape[0] // halves
    slots = places // wide
    blocks = rows // BLK
    per_block = BLK // wide
    tiled = per_block % TILE == 0

    lens = lax.dynamic_slice_in_dim(lengths, half * places, places)
    buck = lax.dynamic_slice_in_dim(bucket, half * places, places)
    split = regroup if tiled else regroup_any
    send, scond, seg, src, cidx = split(x_src, cond, lens, buck, group.reshape(1), wide)
    exchange = functools.partial(
        lax.all_to_all, axis_name="wide", split_axis=0, concat_axis=0, tiled=True
    )
    came = exchange(send)
    came_cond = exchange(scond.reshape(wide, slots, feat // wide))
    cond_in = came_cond.transpose(1, 0, 2).reshape(slots, feat)
    x_view = came.reshape(wide, blocks, per_block, feat)
    if not tiled:
        x_view = x_view.transpose(1, 0, 2, 3).reshape(1, blocks, BLK, feat)

    act_low = jax.nn.silu(cond_in.astype(F32)).astype(BF16)
    modulate = jnp.dot(act_low, w_mod, preferred_element_type=F32) + b_mod.astype(F32)
    slot_ids = jnp.arange(slots, dtype=jnp.int32)
    in_slot = seg[:, None] == slot_ids[None, :]
    mod_blocks = jnp.sum(
        jnp.where(in_slot[:, :, None], modulate[None], 0.0), axis=1
    ).reshape(blocks, 6, feat)

    dy = (
        grad_out.reshape(blocks, per_block, wide, feat)
        .transpose(0, 2, 1, 3)
        .reshape(rows, feat)
    )
    gate_two = mod_blocks[:, 5:6, :]
    df = (
        (gate_two * dy.reshape(blocks, BLK, feat).astype(F32)).astype(BF16).reshape(rows, feat)
    )
    grad_b_fc2 = jnp.sum(df.astype(F32), axis=0)
    dg = dot(df, w_fc2, 1, 1)
    w_qkv_t = w_qkv.T
    bias_qkv = jnp.concatenate(
        [b_qv[:feat].astype(F32), jnp.zeros((feat,), F32), b_qv[feat:].astype(F32)]
    ).reshape(3 * feat, 1)

    qkv_t, a1_t = qkv_forward(x_view, mod_blocks, w_qkv_t, bias_qkv)
    o_t, lse = attend(seg, qkv_t)
    attn, x1, a2, a2_t = proj_forward(
        o_t, w_proj, b_proj.astype(F32).reshape(1, feat), x_view, mod_blocks
    )
    own, place = half.reshape(1), group.reshape(1)
    part = feat // devices
    halved = Halves(wide, part)
    both = ("wide", "narrow")
    f, da2, grad_b_fc1, d_fc1, d_fc2 = mlp(
        own, a2, a2_t, df, dg, w_fc1, w_fc2, b_fc1.astype(F32).reshape(1, hidden), halved
    )

    if halved.split:
        fc2_got, fc1_got = swap(d_fc2[0], "narrow", 1), swap(d_fc1[0], "narrow", 1)
    y, dx1, do_t, grad_b_proj, sums_two, d_proj = middle(
        own, f, b_fc2.astype(F32).reshape(1, feat), x1, attn, dy, da2, mod_blocks, o_t, w_proj,
        halved,
    )
    y_dest = (
        y.reshape(blocks, wide, per_block, feat).transpose(0, 2, 1, 3).reshape(rows, feat)
    )
    in_slot_wide = in_slot[:, :, None, None]

    def padded(by_slot):
        return jnp.pad(by_slot, ((0, 0), (0, -slots % 8), (0, 0)))

    def slot_sums(sums):
        picked = jnp.where(in_slot_wide, sums[:, None], 0.0)
        return jnp.sum(picked, axis=0).reshape(slots, -1).astype(BF16)

    two = Gather(
        jnp.concatenate(
            [slot_sums(sums_two), jnp.pad(act_low, ((0, 0), (0, 3 * feat)))], axis=0
        )[None]
    )
    near, far = bits_of(wide)[:3], bits_of(wide)[3:]
    quarter = HEADS // 4
    back_piece = functools.partial(attend_back, seg, qkv_t, o_t, lse=lse, count=quarter)
    orders = chain_orders(wide)
    if halved.split:
        proj_got = swap(d_proj[0], "narrow", 1)
        fc2_rows, fc1_rows = d_fc2[1].shape[1], d_fc1[1].shape[1]
        cut = (fc2_rows + fc1_rows + part) // 3 // TILE * TILE
        sums = Sums(
            place,
            [
                Part(d_fc2[1], fc2_got, 0, cut, orders[0]),
                Part(d_fc1[1], fc1_got, 0, cut, orders[1]),
                Part(d_fc2[1], fc2_got, cut, fc2_rows - cut, orders[2]),
                Part(d_fc1[1], fc1_got, cut, fc1_rows - cut, orders[2]),
                Part(d_proj[1], proj_got, 0, part, orders[2]),
            ],
        )
        (do_t,) = tie((do_t,), [sums, two])
        two.step(None)
        pieces = [back_piece(do_t, first=i * quarter) for i in range(3)]
        sums.step()
        (do_t, *pieces) = tie((do_t, *pieces), [sums, two])
        for bit in far:
            two.step(bit)
        pieces.append(back_piece(do_t, first=3 * quarter))
        sums.step()
        (a1_t, *pieces) = tie((a1_t, *pieces), [sums, two])
        d_qkv, sums_q = qkv_grad(own, a1_t, pieces, halved)
        sums.step()
        qkv_got = swap(d_qkv[0], "narrow", 1)
        (dx1, *pieces) = tie((dx1, *pieces), [sums, two])
    else:
        for bit in [None] + far:
            two.step(bit)
        pieces = [back_piece(do_t, first=i * quarter) for i in range(4)]
        d_qkv, sums_q = qkv_grad(own, a1_t, pieces, halved)
    for bit in near:
        two.step(bit)
    drows, sums_one = rows_back(pieces, w_qkv_t, x_view, dx1, mod_blocks)
    back = drows
    if not tiled:
        back = back.reshape(blocks, wide, per_block, feat).transpose(1, 0, 2, 3)
    back = exchange(back.reshape(wide, rows // wide, feat))
    biases = jnp.concatenate(
        [
            grad_b_fc1.reshape(devices, -1),
            grad_b_fc2.reshape(devices, -1),
            grad_b_proj.reshape(devices, -1),
            jnp.concatenate([sums_q[0], sums_q[2]]).reshape(devices, -1),
        ],
        axis=1,
    )
    per_device = biases.shape[1]
    one = Gather(
        jnp.concatenate(
            [slot_sums(sums_one), biases.astype(BF16).reshape(slots, 2 * feat)], axis=0
        )[None]
    )
    one.step(None)
    if halved.split:
        late = Sums(
            place, [Part(d_qkv[1], qkv_got, i * part, part, orders[i]) for i in range(3)]
        )
        tie((), [late, one])
        for i in range(len(orders[0])):
            late.step()
            if i == 0:
                for bit in far:
                    one.step(bit)
            if i == BACK_ROUNDS:
                (back,) = tie((back,), [late, one])
            else:
                tie((), [late, one])
        sums.step()
        for bit in near:
            one.step(bit)
        fc2_a, fc1_a, fc2_b, fc1_b, grad_w_proj = (p.keep[0] for p in sums.parts)
        grad_w_fc2 = jnp.concatenate([fc2_a, fc2_b], axis=0)
        grad_w_fc1 = jnp.concatenate([fc1_a, fc1_b], axis=0)
        grad_w_fc1 = (
            grad_w_fc1.reshape(hidden // feat, part, feat).transpose(1, 0, 2).reshape(part, hidden)
        )
        grad_w_qkv = jnp.concatenate([p.keep[0] for p in late.parts], axis=1)
    else:
        for bit in far + near:
            one.step(bit)

        def scattered(full):
            return lax.psum_scatter(full, both, scatter_dimension=0, tiled=True).astype(F32)

        grad_w_fc2 = scattered(d_fc2[0])
        grad_w_fc1 = scattered(d_fc1[0].transpose(1, 0, 2).reshape(feat, hidden))
        grad_w_proj = scattered(d_proj[0])
        grad_w_qkv = scattered(d_qkv[0].transpose(1, 0, 2).reshape(feat, 3 * feat))
    merge = restore if tiled else restore_any
    dx_src = merge(src, back.reshape(rows, feat))

    me = group * halves + half
    count = 2 * slots * devices
    grad_w_mod, grad_b_mod, dact, biases = mod_grad(
        group, me, one.values.reshape(count, -1), two.values.reshape(count, -1), w_mod, part,
        feat // wide, slots,
    )
    grad_b_mod = lax.dynamic_slice_in_dim(grad_b_mod[0], me * 6 * part, 6 * part)
    biases = lax.dynamic_slice_in_dim(biases[slots:].reshape(-1), me * per_device, per_device)
    spot = jnp.maximum(cidx, 0)
    spot = one.place((spot // slots) ^ group) * 2 * slots + spot % slots
    _, silu_back = jax.vjp(jax.nn.silu, cond.astype(F32))
    dcond = silu_back(jnp.take(dact, spot, axis=0))[0].astype(BF16)
    dcond = jnp.where(cidx[:, None] >= 0, dcond, jnp.zeros((), BF16))

    at_two, at_proj, at_qv = hidden // devices, hidden // devices + part, hidden // devices + 2 * part
    return (
        y_dest,
        dx_src,
        dcond,
        grad_w_mod,
        grad_b_mod,
        grad_w_qkv,
        biases[at_qv:],
        grad_w_proj,
        biases[at_proj:at_qv],
        grad_w_fc1,
        biases[:at_two],
        grad_w_fc2,
        biases[at_two:at_proj],
    )


def solution(mesh):
    both = ("wide", "narrow")
    placed = (P("narrow", "wide"), P("narrow", "wide")) + (P(),) * 12 + (P(both, None),)
    matrix, vector = P(both, None), P(both)
    return jax.shard_map(
        local,
        mesh=mesh,
        in_specs=placed,
        out_specs=(
            matrix,
            P("narrow", "wide"),
            P("narrow", "wide"),
            matrix,
            vector,
            matrix,
            vector,
            matrix,
            vector,
            matrix,
            vector,
            matrix,
            vector,
        ),
        check_vma=False,
    )
```

```python
import functools
import math

import jax
import jax.numpy as jnp
from jax import lax
from jax.experimental import pallas as pl
from jax.experimental.pallas import tpu as pltpu
from jax.sharding import PartitionSpec as P

HEADS = 16
HEAD_DIM = 64
EPS = 1e-06
MASKED = -1000000000.0
LOG2E = 1.4426950408889634
BLK = 256
TILE = 16
VMEM_LIMIT = 58 * 2**20
BRIEF = pl.CostEstimate(flops=1, bytes_accessed=1, transcendentals=0)
BF16 = jnp.bfloat16
F32 = jnp.float32


def params(**more):
    return pltpu.CompilerParams(vmem_limit_bytes=VMEM_LIMIT, **more)


def dot(left, right, left_dim, right_dim):
    return lax.dot_general(
        left, right, (((left_dim,), (right_dim,)), ((), ())), preferred_element_type=F32
    )


def norm_parts(values):
    centre = values - jnp.mean(values, axis=1, keepdims=True)
    spread = jnp.mean(centre * centre, axis=1, keepdims=True)
    inverse = lax.rsqrt(spread + EPS)
    return centre * inverse, inverse


def norm_back(grad, normed, inverse):
    return (
        grad
        - jnp.mean(grad, axis=1, keepdims=True)
        - normed * jnp.mean(grad * normed, axis=1, keepdims=True)
    ) * inverse


def each_place(len_ref, buck_ref, off_ref, slot_ref, wide, visit):
    for i in range(wide):
        off_ref[i] = 0
        slot_ref[i] = 0

    def place(j, offset):
        units = len_ref[j] // wide
        b = buck_ref[j]

        @pl.when(units > 0)
        def _():
            start = off_ref[b]
            slot = slot_ref[b]
            off_ref[b] = start + units
            slot_ref[b] = slot + 1
            visit(j, b, units, offset, start, slot)

        return offset + units

    lax.fori_loop(0, len_ref.shape[0], place, 0)


def regroup_rows_kernel(len_ref, buck_ref, x_ref, send_ref, src_ref, off_ref, slot_ref, *, wide):
    cells = send_ref.shape[1]
    send_ref[...] = jnp.zeros_like(send_ref)

    @pl.loop(0, src_ref.shape[0])
    def _(i):
        src_ref[i] = -1

    def visit(j, b, units, offset, start, slot):
        @pl.loop(0, units // TILE)
        def _(t):
            a = pl.multiple_of(offset + t * TILE, TILE)
            c = pl.multiple_of(start + t * TILE, TILE)
            send_ref[b, pl.ds(c, TILE), :] = x_ref[pl.ds(a, TILE), :]
            src_ref[a // TILE] = (b * cells + c) // TILE

    each_place(len_ref, buck_ref, off_ref, slot_ref, wide, visit)


def regroup_cond_kernel(
    len_ref, buck_ref, me_ref, cond_ref, scond_ref, seg_ref, cidx_ref,
    off_ref, slot_ref, cond_in, cond_out, *, wide, slots,
):
    cond_out[...] = jnp.zeros_like(cond_out)
    cond_in[...] = cond_ref[...].astype(F32)
    for i in range(seg_ref.shape[0]):
        seg_ref[i] = -1

    @pl.loop(0, cidx_ref.shape[0])
    def _(j):
        cidx_ref[j] = -1

    def visit(j, b, units, offset, start, slot):
        cidx_ref[j] = b * slots + slot
        cond_out[pl.ds(b * slots + slot, 1), :] = cond_in[pl.ds(j, 1), :]

        @pl.when(b == me_ref[0])
        def _():
            @pl.loop(0, units * wide // BLK)
            def _(t):
                seg_ref[start * wide // BLK + t] = slot

    each_place(len_ref, buck_ref, off_ref, slot_ref, wide, visit)
    scond_ref[...] = cond_out[...].astype(BF16)


def regroup(x_src, cond, lens, buck, me, wide):
    rows, feat = x_src.shape
    places, part = cond.shape
    slots = places // wide
    smem = pl.BlockSpec(memory_space=pltpu.SMEM)
    vmem = pl.BlockSpec(memory_space=pltpu.VMEM)
    counters = [pltpu.SMEM((wide,), jnp.int32), pltpu.SMEM((wide,), jnp.int32)]
    scond, seg, cidx = pl.pallas_call(
        functools.partial(regroup_cond_kernel, wide=wide, slots=slots),
        in_specs=[smem, smem, smem, vmem],
        out_specs=[vmem, smem, smem],
        out_shape=[
            jax.ShapeDtypeStruct((places, part), BF16),
            jax.ShapeDtypeStruct((rows // BLK,), jnp.int32),
            jax.ShapeDtypeStruct((places,), jnp.int32),
        ],
        scratch_shapes=counters + [pltpu.VMEM((places, part), F32), pltpu.VMEM((places, part), F32)],
        compiler_params=params(),
        cost_estimate=BRIEF,
    )(lens, buck, me, cond)
    send, src = pl.pallas_call(
        functools.partial(regroup_rows_kernel, wide=wide),
        in_specs=[smem, smem, vmem],
        out_specs=[vmem, smem],
        out_shape=[
            jax.ShapeDtypeStruct((wide, rows // wide, feat), BF16),
            jax.ShapeDtypeStruct((rows // TILE,), jnp.int32),
        ],
        scratch_shapes=counters,
        compiler_params=params(),
        cost_estimate=BRIEF,
    )(lens, buck, x_src)
    return send, scond, seg, src, cidx


def restore_kernel(src_ref, back_ref, dx_ref):
    @pl.loop(0, src_ref.shape[0])
    def _(i):
        at = src_ref[i]
        rows = back_ref[pl.ds(pl.multiple_of(jnp.maximum(at, 0) * TILE, TILE), TILE), :]
        dx_ref[pl.ds(pl.multiple_of(i * TILE, TILE), TILE), :] = jnp.where(
            at >= 0, rows, jnp.zeros_like(rows)
        )


def restore(src, back):
    vmem = pl.BlockSpec(memory_space=pltpu.VMEM)
    return pl.pallas_call(
        restore_kernel,
        in_specs=[pl.BlockSpec(memory_space=pltpu.SMEM), vmem],
        out_specs=vmem,
        out_shape=jax.ShapeDtypeStruct(back.shape, BF16),
        compiler_params=params(),
        cost_estimate=BRIEF,
    )(src, back)


def regroup_any(x_src, cond, lens, buck, me, wide):
    rows, feat = x_src.shape
    places = lens.shape[0]
    slots, cells = places // wide, rows // wide
    units = lens // wide
    order = jnp.arange(places, dtype=jnp.int32)
    earlier = (order[:, None] < order[None, :]) & (buck[:, None] == buck[None, :])
    live = (lens > 0).astype(jnp.int32)
    offset = jnp.cumsum(units) - units
    start = jnp.sum(jnp.where(earlier, units[:, None], 0), axis=0)
    slot = jnp.sum(jnp.where(earlier, live[:, None], 0), axis=0)
    cell = jnp.arange(cells, dtype=jnp.int32)[None, :, None]
    to_target = (buck[None, :] == jnp.arange(wide, dtype=jnp.int32)[:, None]) & (live[None, :] > 0)
    hit = (
        to_target[:, None, :]
        & (cell >= start[None, None, :])
        & (cell < (start + units)[None, None, :])
    ).astype(jnp.int32)
    valid = jnp.sum(hit, axis=2)
    source = jnp.sum(hit * (offset - start)[None, None, :], axis=2) + cell[:, :, 0]
    source = jnp.where(valid > 0, source, 0)
    picked = jnp.take(x_src, source.reshape(-1), axis=0).reshape(wide, cells, feat)
    send = jnp.where(valid[:, :, None] > 0, picked, jnp.zeros((), BF16))
    cond_hit = to_target[:, None, :] & (
        slot[None, None, :] == jnp.arange(slots, dtype=jnp.int32)[None, :, None]
    )
    scond = jnp.einsum("wqs,sf->wqf", cond_hit.astype(BF16), cond, preferred_element_type=F32)
    scond = scond.astype(BF16).reshape(cond.shape)
    first = jnp.arange(rows // BLK, dtype=jnp.int32)[:, None] * BLK
    mine = (
        ((buck == me[0]) & (live > 0))[None, :]
        & (first >= (start * wide)[None, :])
        & (first < ((start + units) * wide)[None, :])
    )
    seg = jnp.sum(jnp.where(mine, slot[None, :] + 1, 0), axis=1) - 1
    spot = jnp.arange(rows, dtype=jnp.int32)[:, None]
    inside = (live[None, :] > 0) & (spot >= offset[None, :]) & (spot < (offset + units)[None, :])
    src = jnp.sum(jnp.where(inside, (buck * cells + start - offset)[None, :] + spot + 1, 0), axis=1)
    cidx = jnp.where(live > 0, buck * slots + slot, -1)
    return send, scond, seg.astype(jnp.int32), src - 1, cidx


def restore_any(src, back):
    dx = jnp.take(back, jnp.maximum(src, 0), axis=0)
    return jnp.where(src[:, None] >= 0, dx, jnp.zeros((), BF16))


def qkv_kernel(x_ref, mod_ref, w_ref, b_ref, q_ref, a_ref):
    feat = x_ref.shape[-1]
    x = x_ref[...].reshape(BLK, feat).astype(F32)
    normed, _ = norm_parts(x)
    a1 = (normed * (1.0 + mod_ref[0, 1:2, :]) + mod_ref[0, 0:1, :]).astype(BF16)
    a1_t = a1.T
    a_ref[...] = a1_t
    for i in range(3):
        part = slice(i * feat, (i + 1) * feat)
        q_ref[part, :] = (dot(w_ref[part, :], a1_t, 1, 0) + b_ref[part, :]).astype(BF16)


def row_spec(view):
    return pl.BlockSpec((view[0], 1, view[2], view[3]), lambda k: (0, k, 0, 0))


def whole(*shape):
    return pl.BlockSpec(shape, lambda k: (0,) * len(shape))


def qkv_forward(x_view, mod_blocks, w_t, bias):
    feat = x_view.shape[-1]
    blocks = x_view.shape[1]
    return pl.pallas_call(
        qkv_kernel,
        grid=(blocks,),
        in_specs=[
            row_spec(x_view.shape),
            pl.BlockSpec((1, 6, feat), lambda k: (k, 0, 0)),
            whole(3 * feat, feat),
            whole(3 * feat, 1),
        ],
        out_specs=[
            pl.BlockSpec((3 * feat, BLK), lambda k: (0, k)),
            pl.BlockSpec((feat, BLK), lambda k: (0, k)),
        ],
        out_shape=[
            jax.ShapeDtypeStruct((3 * feat, blocks * BLK), BF16),
            jax.ShapeDtypeStruct((feat, blocks * BLK), BF16),
        ],
        compiler_params=params(),
        cost_estimate=BRIEF,
    )(x_view, mod_blocks, w_t, bias)


def masks(seg_ref, query_block, blocks):
    base = LOG2E / math.sqrt(HEAD_DIM)
    same = [seg_ref[query_block] == seg_ref[kb] for kb in range(blocks)]
    scales = [jnp.where(s, base, 0.0) for s in same]
    shifts = [jnp.where(s, 0.0, MASKED * LOG2E) for s in same]
    return scales, shifts


def attend_kernel(seg_ref, q_ref, k_ref, v_ref, o_ref, lse_ref, *, blocks, heads):
    for h in range(heads):
        hs = slice(h * HEAD_DIM, (h + 1) * HEAD_DIM)
        keys = k_ref[hs, :].T
        v_t = v_ref[hs, :]
        for qb in range(blocks):
            qs = slice(qb * BLK, (qb + 1) * BLK)
            q_t = q_ref[hs, qs]
            scales, shifts = masks(seg_ref, qb, blocks)
            scores = [dot(keys[kb * BLK : (kb + 1) * BLK], q_t, 1, 0) for kb in range(blocks)]
            top = None
            for kb in range(blocks):
                peak = jnp.max(scores[kb], axis=0, keepdims=True) * scales[kb] + shifts[kb]
                top = peak if top is None else jnp.maximum(top, peak)
            total = jnp.zeros((1, BLK), F32)
            parts = []
            for kb in range(blocks):
                expo = jnp.exp2(scores[kb] * scales[kb] - (top - shifts[kb]))
                total = total + jnp.sum(expo, axis=0, keepdims=True)
                parts.append(expo.astype(BF16))
            out = dot(v_t, jnp.concatenate(parts, axis=0), 1, 0)
            o_ref[hs, qs] = (out / total).astype(BF16)
            lse_ref[h, :, qs] = top + jnp.log2(total)


def attend(seg, qkv_t, heads=2):
    feat3, rows = qkv_t.shape
    feat = feat3 // 3
    span = heads * HEAD_DIM
    groups = feat // span
    return pl.pallas_call(
        functools.partial(attend_kernel, blocks=rows // BLK, heads=heads),
        grid_spec=pltpu.PrefetchScalarGridSpec(
            num_scalar_prefetch=1,
            grid=(groups,),
            in_specs=[
                pl.BlockSpec((span, rows), lambda g, s: (g, 0)),
                pl.BlockSpec((span, rows), lambda g, s: (groups + g, 0)),
                pl.BlockSpec((span, rows), lambda g, s: (2 * groups + g, 0)),
            ],
            out_specs=[
                pl.BlockSpec((span, rows), lambda g, s: (g, 0)),
                pl.BlockSpec((heads, 1, rows), lambda g, s: (g, 0, 0)),
            ],
        ),
        out_shape=[
            jax.ShapeDtypeStruct((feat, rows), BF16),
            jax.ShapeDtypeStruct((feat // HEAD_DIM, 1, rows), F32),
        ],
        compiler_params=params(),
        cost_estimate=BRIEF,
    )(seg, qkv_t, qkv_t, qkv_t)


def attend_back_kernel(
    seg_ref, q_ref, k_ref, v_ref, o_ref, do_ref, lse_ref, out_ref, *, blocks, heads
):
    scale = 1.0 / math.sqrt(HEAD_DIM)
    for h in range(heads):
        hs = slice(h * HEAD_DIM, (h + 1) * HEAD_DIM)
        k_t = k_ref[hs, :]
        keys, values = k_t.T, v_ref[hs, :].T
        inner = jnp.sum(
            o_ref[hs, :].astype(F32) * do_ref[hs, :].astype(F32), axis=0, keepdims=True
        )
        grad_k = grad_v = None
        for qb in range(blocks):
            qs = slice(qb * BLK, (qb + 1) * BLK)
            q_t, do_t = q_ref[hs, qs], do_ref[hs, qs]
            scales, shifts = masks(seg_ref, qb, blocks)
            probs, grads = [], []
            for kb in range(blocks):
                ks = slice(kb * BLK, (kb + 1) * BLK)
                score = dot(keys[ks], q_t, 1, 0)
                grad_p = dot(values[ks], do_t, 1, 0)
                prob = jnp.exp2(score * scales[kb] - (lse_ref[h, :, qs] - shifts[kb]))
                probs.append(prob.astype(BF16))
                grads.append((prob * (grad_p - inner[:, qs])).astype(BF16))
            probs = jnp.concatenate(probs, axis=0)
            grads = jnp.concatenate(grads, axis=0)
            out_ref[0, hs, qs] = (dot(k_t, grads, 1, 0) * scale).astype(BF16)
            more_k, more_v = dot(q_t, grads, 1, 1), dot(do_t, probs, 1, 1)
            grad_k = more_k if grad_k is None else grad_k + more_k
            grad_v = more_v if grad_v is None else grad_v + more_v
        out_ref[1, hs, :] = (grad_k * scale).astype(BF16)
        out_ref[2, hs, :] = grad_v.astype(BF16)


def attend_back(seg, qkv_t, o_t, do_t, lse, first, count, heads=2):
    feat3, rows = qkv_t.shape
    feat = feat3 // 3
    span = heads * HEAD_DIM
    groups = feat // span
    at = first // heads
    return pl.pallas_call(
        functools.partial(attend_back_kernel, blocks=rows // BLK, heads=heads),
        grid_spec=pltpu.PrefetchScalarGridSpec(
            num_scalar_prefetch=1,
            grid=(count // heads,),
            in_specs=[
                pl.BlockSpec((span, rows), lambda g, s: (at + g, 0)),
                pl.BlockSpec((span, rows), lambda g, s: (groups + at + g, 0)),
                pl.BlockSpec((span, rows), lambda g, s: (2 * groups + at + g, 0)),
                pl.BlockSpec((span, rows), lambda g, s: (at + g, 0)),
                pl.BlockSpec((span, rows), lambda g, s: (at + g, 0)),
                pl.BlockSpec((heads, 1, rows), lambda g, s: (at + g, 0, 0)),
            ],
            out_specs=pl.BlockSpec((3, span, rows), lambda g, s: (0, g, 0)),
        ),
        out_shape=jax.ShapeDtypeStruct((3, count * HEAD_DIM, rows), BF16),
        compiler_params=params(),
        cost_estimate=BRIEF,
    )(seg, qkv_t, qkv_t, qkv_t, o_t, do_t, lse)


class Halves:
    def __init__(self, wide, part):
        self.wide, self.part = wide, part
        self.split = part % TILE == 0

    def shapes(self, between, columns):
        if self.split:
            shape = (self.wide,) + between + (self.part, columns)
            return [jax.ShapeDtypeStruct(shape, BF16)] * 2
        return [jax.ShapeDtypeStruct(between + (2 * self.wide * self.part, columns), BF16)]

    def specs(self, between, columns, index):
        ones = (1,) * between
        if self.split:
            return [
                pl.BlockSpec(
                    (self.wide,) + ones + (self.part, columns),
                    lambda *g: (0,) + index(*g)[:-1] + (0, index(*g)[-1]),
                )
            ] * 2
        return [
            pl.BlockSpec(
                ones + (2 * self.wide * self.part, columns),
                lambda *g: index(*g)[:-1] + (0, index(*g)[-1]),
            )
        ]

    def store(self, half, value, refs):
        if not self.split:
            refs[0][...] = value.astype(BF16).reshape(refs[0].shape)
            return
        value = value.reshape(value.shape[0] // (2 * self.part), 2, self.part, value.shape[1])
        even, odd = value[:, 0], value[:, 1]
        refs[0][...] = jnp.where(half == 0, odd, even).astype(BF16).reshape(refs[0].shape)
        refs[1][...] = jnp.where(half == 0, even, odd).astype(BF16).reshape(refs[1].shape)

    def finish(self, arrays):
        if self.split:
            return [a.reshape(self.wide, -1, a.shape[-1]) for a in arrays]
        return arrays


def qkv_grad_kernel(half_ref, a_ref, *refs, pieces, halves):
    ins, outs, sums_ref = refs[:pieces], refs[pieces:-1], refs[-1]
    ones = jnp.ones((8, a_ref.shape[1]), BF16)
    value = jnp.concatenate([dot(a_ref[...], r[0], 1, 1) for r in ins], axis=1)
    halves.store(half_ref[0], value, outs)
    sums_ref[0] = jnp.concatenate([dot(ones, r[0], 1, 1) for r in ins], axis=1)


def qkv_grad(half, a1_t, dqkv, halves):
    feat, rows = a1_t.shape
    columns = sum(d.shape[1] for d in dqkv)
    out = pl.pallas_call(
        functools.partial(qkv_grad_kernel, pieces=len(dqkv), halves=halves),
        grid=(3,),
        in_specs=[pl.BlockSpec(memory_space=pltpu.SMEM), whole(feat, rows)]
        + [pl.BlockSpec((1, d.shape[1], rows), lambda i: (i, 0, 0)) for d in dqkv],
        out_specs=halves.specs(1, columns, lambda i: (i, 0))
        + [pl.BlockSpec((1, 8, columns), lambda i: (i, 0, 0))],
        out_shape=halves.shapes((3,), columns) + [jax.ShapeDtypeStruct((3, 8, columns), F32)],
        compiler_params=params(),
        cost_estimate=BRIEF,
    )(half, a1_t, *dqkv)
    return halves.finish(out[:-1]), out[-1][:, 0, :]


def proj_kernel(o_ref, w_ref, b_ref, x_ref, mod_ref, attn_ref, x1_ref, a_ref, at_ref):
    feat = x_ref.shape[-1]
    attn = dot(o_ref[...], w_ref[...], 0, 0) + b_ref[...]
    attn_ref[...] = attn
    x1 = x_ref[...].reshape(BLK, feat).astype(F32) + mod_ref[0, 2:3, :] * attn
    x1_ref[...] = x1
    normed, _ = norm_parts(x1)
    a2 = (normed * (1.0 + mod_ref[0, 4:5, :]) + mod_ref[0, 3:4, :]).astype(BF16)
    a_ref[...] = a2
    at_ref[...] = a2.T


def proj_forward(o_t, w_proj, b_proj, x_view, mod_blocks):
    feat = x_view.shape[-1]
    blocks = x_view.shape[1]
    rows = blocks * BLK
    by_row = pl.BlockSpec((BLK, feat), lambda k: (k, 0))
    by_column = pl.BlockSpec((feat, BLK), lambda k: (0, k))
    return pl.pallas_call(
        proj_kernel,
        grid=(blocks,),
        in_specs=[
            by_column,
            whole(feat, feat),
            whole(1, feat),
            row_spec(x_view.shape),
            pl.BlockSpec((1, 6, feat), lambda k: (k, 0, 0)),
        ],
        out_specs=[by_row, by_row, by_row, by_column],
        out_shape=[
            jax.ShapeDtypeStruct((rows, feat), F32),
            jax.ShapeDtypeStruct((rows, feat), F32),
            jax.ShapeDtypeStruct((rows, feat), BF16),
            jax.ShapeDtypeStruct((feat, rows), BF16),
        ],
        compiler_params=params(),
        cost_estimate=BRIEF,
    )(o_t, w_proj, b_proj, x_view, mod_blocks)


def gelu_both(u):
    c = math.sqrt(2.0 / math.pi)
    square = u * u
    half = 0.5 + 0.5 * jnp.tanh(u * (c + (c * 0.044715) * square))
    g = u * half
    return g, half + (g - g * half) * (2.0 * c + (6.0 * c * 0.044715) * square)


def mlp_kernel(
    half_ref, a_ref, at_ref, df_ref, dg_ref, w1_ref, w2_ref, b1_ref, *refs, first, second
):
    f_ref, da_ref, db_ref = refs[:3]
    g_ref, du_ref = refs[-2:]
    outs = refs[3:-2]
    outs_one, outs_two = outs[: len(outs) // 2], outs[len(outs) // 2 :]
    step = pl.program_id(0)
    rows = a_ref.shape[0]

    @pl.when(step == 0)
    def _():
        f_ref[...] = jnp.zeros_like(f_ref)
        da_ref[...] = jnp.zeros_like(da_ref)

    w1, w2 = w1_ref[...], w2_ref[...]
    bias = jnp.zeros((1, w1.shape[1]), F32)
    cuts = [slice(r, r + BLK) for r in range(0, rows, BLK)]
    u = dot(a_ref[cuts[0], :], w1, 1, 0)
    for r, rs in enumerate(cuts):
        later = dot(a_ref[cuts[r + 1], :], w1, 1, 0) if r + 1 < len(cuts) else None
        g, slope = gelu_both(u + b1_ref[...])
        du = dg_ref[rs, :] * slope
        bias = bias + jnp.sum(du, axis=0, keepdims=True)
        g_ref[rs, :] = g.astype(BF16)
        du_ref[rs, :] = du.astype(BF16)
        u = later
        for past in cuts[r - 1 : r] if r + 1 < len(cuts) else cuts[max(r - 1, 0) :]:
            f_ref[past, :] += dot(g_ref[past, :], w2, 1, 0)
            da_ref[past, :] += dot(du_ref[past, :], w1, 1, 1)
    db_ref[...] = bias
    first.store(half_ref[0], dot(at_ref[...], du_ref[...], 1, 0), outs_one)
    second.store(half_ref[0], dot(g_ref[...], df_ref[...], 0, 0), outs_two)


def mlp(half, a2, a2_t, df, dg, w1, w2, b1, halves, width=512):
    rows, feat = a2.shape
    hidden = w1.shape[1]
    per = feat // width
    wide = halves.wide
    part = hidden // (2 * wide)
    first = halves
    second = Halves(wide, part)
    second.split = halves.split
    one = pl.Buffered(1)

    def fixed(*shape):
        return pl.BlockSpec(shape, lambda j: (0,) * len(shape), pipeline_mode=one)

    if halves.split:
        two_specs = [pl.BlockSpec((width // (2 * part), part, feat), lambda j: (j, 0, 0))] * 2
        two_shapes = [jax.ShapeDtypeStruct((wide, part, feat), BF16)] * 2
    else:
        two_specs = [pl.BlockSpec((width, feat), lambda j: (j, 0))]
        two_shapes = [jax.ShapeDtypeStruct((hidden, feat), BF16)]
    out = pl.pallas_call(
        functools.partial(mlp_kernel, first=first, second=second),
        grid=(hidden // width,),
        in_specs=[
            pl.BlockSpec(memory_space=pltpu.SMEM),
            fixed(rows, feat),
            fixed(feat, rows),
            fixed(rows, feat),
            pl.BlockSpec((rows, width), lambda j: (0, j)),
            pl.BlockSpec((feat, width), lambda j: (0, j)),
            pl.BlockSpec((width, feat), lambda j: (j, 0)),
            pl.BlockSpec((1, width), lambda j: (0, j)),
        ],
        out_specs=[whole(rows, feat), whole(rows, feat), pl.BlockSpec((1, width), lambda j: (0, j))]
        + halves.specs(1, width, lambda j: (j // per, j % per))
        + two_specs,
        out_shape=[
            jax.ShapeDtypeStruct((rows, feat), F32),
            jax.ShapeDtypeStruct((rows, feat), F32),
            jax.ShapeDtypeStruct((1, hidden), F32),
        ]
        + halves.shapes((hidden // feat,), feat)
        + two_shapes,
        scratch_shapes=[pltpu.VMEM((rows, width), BF16), pltpu.VMEM((rows, width), BF16)],
        compiler_params=params(),
        cost_estimate=BRIEF,
    )(half, a2, a2_t, df, dg, w1, w2, b1)
    f, da2, bias = out[:3]
    rest = out[3:]
    count = len(rest) // 2
    return f, da2, bias, first.finish(rest[:count]), second.finish(rest[count:])


def to_slot(ref, slot, slots, terms):
    @pl.when(slot >= 0)
    def _():
        for i, term in enumerate(terms):
            ref[pl.ds(2 * slots * i + slot, 1), :] += jnp.sum(term, axis=0, keepdims=True)


def middle_kernel(
    half_ref, seg_ref, f_ref, b2_ref, x1_ref, attn_ref, dy_ref, da_ref, mod_ref, o_ref, w_ref, act_ref,
    y_ref, dx_ref, do_ref, db_ref, sums_ref, *rest, halves,
):
    k = pl.program_id(0)
    outs, acc_ref, slot_ref = rest[:-2], rest[-2], rest[-1]
    slots = act_ref.shape[0]

    @pl.when(k == 0)
    def _():
        acc_ref[...] = jnp.zeros_like(acc_ref)
        db_ref[...] = jnp.zeros_like(db_ref)
        slot_ref[...] = jnp.zeros_like(slot_ref)
        slot_ref[slots : 2 * slots, :] = act_ref[...].astype(F32)

    f = f_ref[...] + b2_ref[...]
    x1 = x1_ref[...]
    dy = dy_ref[...].astype(F32)
    y_ref[...] = (x1 + mod_ref[0, 5:6, :] * f).astype(BF16)
    normed, inverse = norm_parts(x1)
    da = da_ref[...]
    dx1 = dy + norm_back(da * (1.0 + mod_ref[0, 4:5, :]), normed, inverse)
    dx_ref[...] = dx1
    dattn = (mod_ref[0, 2:3, :] * dx1).astype(BF16)
    db_ref[...] += jnp.sum(dattn.astype(F32), axis=0, keepdims=True)
    to_slot(slot_ref, seg_ref[k], slots, [dx1 * attn_ref[...], da, da * normed, dy * f])
    do_ref[...] = dot(w_ref[...], dattn, 1, 1).astype(BF16)
    acc_ref[...] += dot(o_ref[...], dattn, 1, 0)

    @pl.when(k == pl.num_programs(0) - 1)
    def _():
        halves.store(half_ref[0], acc_ref[...], outs)
        sums_ref[0] = slot_ref[...].astype(BF16)


def middle(half, seg, act, f, b2, x1, attn, dy, da2, mod_blocks, o_t, w_proj, halves):
    rows, feat = x1.shape
    by_row = pl.BlockSpec((BLK, feat), lambda k: (k, 0))
    by_column = pl.BlockSpec((feat, BLK), lambda k: (0, k))
    blocks = rows // BLK
    slots = act.shape[0]
    out = pl.pallas_call(
        functools.partial(middle_kernel, halves=halves),
        grid=(blocks,),
        in_specs=[
            pl.BlockSpec(memory_space=pltpu.SMEM),
            pl.BlockSpec(memory_space=pltpu.SMEM),
            by_row, whole(1, feat), by_row, by_row, by_row, by_row,
            pl.BlockSpec((1, 6, feat), lambda k: (k, 0, 0)),
            by_column, whole(feat, feat), whole(slots, feat),
        ],
        out_specs=[
            by_row, by_row, by_column, whole(1, feat),
            whole(1, 8 * slots, feat),
        ] + halves.specs(0, feat, lambda k: (0,)),
        out_shape=[
            jax.ShapeDtypeStruct((rows, feat), BF16),
            jax.ShapeDtypeStruct((rows, feat), F32),
            jax.ShapeDtypeStruct((feat, rows), BF16),
            jax.ShapeDtypeStruct((1, feat), F32),
            jax.ShapeDtypeStruct((1, 8 * slots, feat), BF16),
        ]
        + halves.shapes((), feat),
        scratch_shapes=[pltpu.VMEM((feat, feat), F32), pltpu.VMEM((8 * slots, feat), F32)],
        compiler_params=params(),
        cost_estimate=BRIEF,
    )(half, seg, f, b2, x1, attn, dy, da2, mod_blocks, o_t, w_proj, act)
    return tuple(out[:5]) + (halves.finish(out[5:]),)


def rows_back_kernel(seg_ref, w_ref, x_ref, dx_ref, mod_ref, bias_ref, *refs):
    out_ref, sums_ref, slot_ref = refs[-3:]
    slots = bias_ref.shape[0] // 2

    @pl.when(pl.program_id(0) == 0)
    def _():
        slot_ref[...] = jnp.zeros_like(slot_ref)
        slot_ref[slots : 2 * slots, :] = bias_ref[:slots, :]
        slot_ref[3 * slots :, :] = bias_ref[slots:, :]

    feat = x_ref.shape[-1]
    da = None
    for i in range(3):
        at = i * feat
        for ref in refs[:-3]:
            more = dot(ref[i], w_ref[at : at + ref.shape[1], :], 0, 0)
            da = more if da is None else da + more
            at += ref.shape[1]
    normed, inverse = norm_parts(x_ref[...].reshape(BLK, feat).astype(F32))
    out = dx_ref[...] + norm_back(da * (1.0 + mod_ref[0, 1:2, :]), normed, inverse)
    out_ref[...] = out.astype(BF16).reshape(out_ref.shape)
    to_slot(slot_ref, seg_ref[pl.program_id(0)], slots, [da, da * normed])
    sums_ref[0] = slot_ref[...].astype(BF16)


def rows_back(seg, dqkv, w_t, x_view, dx1, mod_blocks, biases):
    rows, feat = dx1.shape
    blocks = rows // BLK
    return pl.pallas_call(
        rows_back_kernel,
        grid=(blocks,),
        in_specs=[
            pl.BlockSpec(memory_space=pltpu.SMEM),
            whole(3 * feat, feat),
            row_spec(x_view.shape),
            pl.BlockSpec((BLK, feat), lambda k: (k, 0)),
            pl.BlockSpec((1, 6, feat), lambda k: (k, 0, 0)),
            whole(*biases.shape),
        ]
        + [pl.BlockSpec((3, d.shape[1], BLK), lambda k: (0, 0, k)) for d in dqkv],
        out_specs=[row_spec(x_view.shape), whole(1, 2 * biases.shape[0], feat)],
        out_shape=[
            jax.ShapeDtypeStruct(x_view.shape, BF16),
            jax.ShapeDtypeStruct((1, 2 * biases.shape[0], feat), BF16),
        ],
        scratch_shapes=[pltpu.VMEM((2 * biases.shape[0], feat), F32)],
        compiler_params=params(),
        cost_estimate=BRIEF,
    )(seg, w_t, x_view, dx1, mod_blocks, biases, *dqkv)


def mod_grad_kernel(
    ids_ref, one_ref, two_ref, w_ref, gw_ref, gb_ref, dact_ref, bias_ref, act_ref, *, part, slots
):
    feat = one_ref.shape[-1]

    def columns(ref):
        wide = ref[...].astype(F32)
        wide = wide.reshape(wide.shape[0], -1, 2 * slots, feat)
        return [wide[:, i].reshape(-1, feat) for i in range(wide.shape[1])]

    one, two = columns(one_ref), columns(two_ref)
    rows = one[0].shape[0]
    first = lax.broadcasted_iota(jnp.int32, (rows, 1), 0) % (2 * slots) < slots
    act_ref[...] = jnp.where(first, pltpu.roll(two[0], rows - slots, 0), 0.0).T
    act = act_ref[pl.ds(pl.multiple_of(ids_ref[1] * part, 8), part), :].astype(BF16)
    dact = None
    for i, values in enumerate(one + two):
        at = slice(i * feat, (i + 1) * feat)
        low = values.astype(BF16)
        gw_ref[:, at] = dot(act, low, 1, 0)
        gb_ref[:, at] = jnp.sum(jnp.where(first, values, 0.0), axis=0, keepdims=True)
        more = dot(low, w_ref[:, at], 1, 1)
        dact = more if dact is None else dact + more
    dact_ref[...] = dact
    for i, values in enumerate(one):
        sums = jnp.sum(values.reshape(-1, 2 * slots, feat), axis=0)
        bias_ref[i * slots : (i + 1) * slots, :] = sums[slots:, :]


def mod_grad(group, me, one, two, w_mod, part, share, slots):
    feat, columns = w_mod.shape
    count = 2 * slots * one.shape[0]

    def fixed(*shape):
        return pl.BlockSpec(shape, lambda i, ids: (0,) * len(shape))

    return pl.pallas_call(
        functools.partial(mod_grad_kernel, part=part, slots=slots),
        grid_spec=pltpu.PrefetchScalarGridSpec(
            num_scalar_prefetch=1,
            grid=(1,),
            in_specs=[
                fixed(*one.shape),
                fixed(*two.shape),
                pl.BlockSpec((share, columns), lambda i, ids: (ids[0], 0)),
            ],
            out_specs=[
                fixed(part, columns),
                fixed(1, columns),
                fixed(count, share),
                fixed(2 * slots, feat),
            ],
            scratch_shapes=[pltpu.VMEM((feat, count), F32)],
        ),
        out_shape=[
            jax.ShapeDtypeStruct((part, columns), F32),
            jax.ShapeDtypeStruct((1, columns), F32),
            jax.ShapeDtypeStruct((count, share), F32),
            jax.ShapeDtypeStruct((2 * slots, feat), F32),
        ],
        compiler_params=params(),
        cost_estimate=BRIEF,
    )(jnp.stack([group, me]), one, two, w_mod)


def swap(values, axis, bit):
    count = lax.axis_size(axis)
    return lax.ppermute(values, axis, [(i, i ^ bit) for i in range(count)])


def bits_of(wide):
    return [1 << i for i in range(wide.bit_length() - 1)]


def chain_orders(wide):
    bits = bits_of(wide)
    near, far = bits[:3], bits[3:]
    return [near[i:] + near[:i] + far for i in range(3)]


class Part:
    def __init__(self, keep, got, start, rows, order):
        self.keep, self.got = (keep, start), (got, start)
        self.rows = rows
        self.dims = list(reversed(bits_of(keep.shape[0])))
        self.order = list(order)


class Rider:
    def __init__(self, values, order):
        self.keep, self.got = (values, 0), (None, 0)
        self.rows = values.shape[1]
        self.order, self.done = list(order), []

    def place(self, difference):
        at = jnp.zeros_like(difference)
        for i, bit in enumerate(self.done):
            at = at + ((difference // bit) % 2) * (1 << i)
        return at


def relay_kernel(me_ref, *refs, plan, inputs, outputs, streamed):
    ins, outs, scratch = refs[:inputs], refs[inputs : inputs + outputs], refs[inputs + outputs :]
    arriving, leaving = [], []
    if streamed:
        for i, (_, addends, rows, *_) in enumerate(plan):
            for k, (source, start) in enumerate(addends):
                copy = pltpu.make_async_copy(
                    ins[source].at[:, pl.ds(start, rows), :], scratch[4 * i + k], scratch[-1].at[4 * i + k]
                )
                copy.start()
                arriving.append(copy)
    for i, (ride, addends, rows, bit, inner, count, targets) in enumerate(plan):
        if ride:
            for k, (source, start) in enumerate(addends):
                piece = ins[source][0, start : start + rows, :]
                for out, base in targets:
                    outs[out][0, base + k * rows : base + (k + 1) * rows, :] = piece
            continue
        if bit is None:
            left, right = (ins[a][0, start : start + rows, :] for a, start in addends)
            outs[targets[0][0]][...] = left.astype(F32) + right.astype(F32)
            continue
        if streamed:
            arriving[2 * i].wait()
            arriving[2 * i + 1].wait()
            reads = [(scratch[4 * i], 0), (scratch[4 * i + 1], 0)]
            writes = [(scratch[4 * i + 2], 0), (scratch[4 * i + 3], 0)]
        else:
            reads = [(ins[a], start) for a, start in addends]
            writes = [(outs[out], base) for out, base in targets]
        own = (me_ref[0] // bit) % 2

        @pl.loop(0, count // 2)
        def _(e, own=own, rows=rows, inner=inner, reads=reads, writes=writes):
            outer = (e // inner) * 2 * inner + e % inner
            for which, (out, base) in zip((1 - own, own), writes, strict=True):
                left, right = (r[outer + which * inner, a : a + rows, :] for r, a in reads)
                out[e, base : base + rows, :] = left + right

        if streamed:
            for k, (out, base) in enumerate(targets):
                copy = pltpu.make_async_copy(
                    scratch[4 * i + 2 + k],
                    outs[out].at[:, pl.ds(base, rows), :],
                    scratch[-1].at[4 * i + 2 + k],
                )
                copy.start()
                leaving.append(copy)
    for copy in leaving:
        copy.wait()


def relay(me, moving, streamed=False):
    arrays, plan, shapes, sends, keeps = [], [], [], {}, []
    columns = moving[0].keep[0].shape[2]

    def index(array):
        for i, known in enumerate(arrays):
            if known is array:
                return i
        arrays.append(array)
        return len(arrays) - 1

    def out(*shape, dtype=BF16):
        shapes.append(jax.ShapeDtypeStruct(shape, dtype))
        return len(shapes) - 1

    bits = [m.order[0] if m.order else None for m in moving]
    for m, bit in zip(moving, bits, strict=True):
        addends = [(index(a), start) for a, start in (m.keep, m.got) if a is not None]
        ride = isinstance(m, Rider)
        if ride:
            keeps.append(out(1, m.rows * len(addends), m.keep[0].shape[2]))
            plan.append((ride, addends, m.rows, None, 1, 1, [(keeps[-1], 0)]))
            m.rows *= len(addends)
            if bit is not None:
                sends[ride, bit] = keeps[-1]
        elif bit is None:
            keeps.append(out(m.rows, columns, dtype=F32))
            plan.append((ride, addends, m.rows, None, 1, 1, [(keeps[-1], 0)]))
        else:
            at = m.dims.index(bit)
            count, inner = 1 << len(m.dims), 1 << (len(m.dims) - 1 - at)
            same = [o for o, b in zip(moving, bits, strict=True) if b == bit and isinstance(o, Part)]
            if (ride, bit) not in sends:
                sends[ride, bit] = out(count // 2, sum(o.rows for o in same), columns)
            base = sum(o.rows for o in same[: same.index(m)])
            keeps.append(out(count // 2, m.rows, columns))
            targets = [(sends[ride, bit], base), (keeps[-1], 0)]
            plan.append((ride, addends, m.rows, bit, inner, count, targets))
            m.got = (None, base)
            m.dims.pop(at)
    scratch = []
    if streamed:
        for _, _, rows, _, _, count, _ in plan:
            scratch += [pltpu.VMEM((n, rows, columns), BF16) for n in (count, count, count // 2, count // 2)]
        scratch.append(pltpu.SemaphoreType.DMA((len(scratch),)))
    place = pl.BlockSpec(memory_space=pl.ANY if streamed else pltpu.VMEM)
    out_arrays = pl.pallas_call(
        functools.partial(
            relay_kernel, plan=plan, inputs=len(arrays), outputs=len(shapes), streamed=streamed
        ),
        in_specs=[pl.BlockSpec(memory_space=pltpu.SMEM)] + [place] * len(arrays),
        out_specs=[place] * len(shapes),
        out_shape=shapes,
        scratch_shapes=scratch,
        compiler_params=params(),
        cost_estimate=BRIEF,
    )(me, *arrays)
    for m, kept in zip(moving, keeps, strict=True):
        m.keep = (out_arrays[kept], 0)
    return {key: out_arrays[at] for key, at in sends.items()}


class Sums:
    def __init__(self, me, moving, streamed=False):
        self.me, self.moving = me, list(moving)
        self.going = relay(me, moving, streamed)

    def join(self, rider):
        self.moving.append(rider)
        self.going[True, rider.order[0]] = rider.keep[0]

    def step(self):
        came = {key: swap(send, "wide", key[1]) for key, send in self.going.items()}
        going = [m for m in self.moving if m.order]
        for m in going:
            bit = m.order.pop(0)
            ride = isinstance(m, Rider)
            m.got = (came[ride, bit], 0 if ride else m.got[1])
            if ride:
                m.done.append(bit)
        self.going = relay(self.me, going)

    def arrays(self):
        return tuple(self.going.values()) + tuple(m.keep[0] for m in self.moving)

    def put(self, arrays):
        count = len(self.going)
        self.going = dict(zip(self.going, arrays[:count], strict=True))
        for m, kept in zip(self.moving, arrays[count:], strict=True):
            m.keep = (kept,) + m.keep[1:]


def tie(values, moving):
    out = lax.optimization_barrier((tuple(values), tuple(m.arrays() for m in moving)))
    for one, kept in zip(moving, out[1], strict=True):
        one.put(kept)
    return out[0]


def local(
    x_src,
    cond,
    lengths,
    bucket,
    w_mod,
    b_mod,
    w_qkv,
    b_qv,
    w_proj,
    b_proj,
    w_fc1,
    b_fc1,
    w_fc2,
    b_fc2,
    grad_out,
):
    wide = lax.axis_size("wide")
    halves = lax.axis_size("narrow")
    devices = wide * halves
    group = lax.axis_index("wide")
    half = lax.axis_index("narrow")
    rows, feat = x_src.shape
    hidden = w_fc1.shape[1]
    places = lengths.shape[0] // halves
    slots = places // wide
    blocks = rows // BLK
    per_block = BLK // wide
    tiled = per_block % TILE == 0

    lens = lax.dynamic_slice_in_dim(lengths, half * places, places)
    buck = lax.dynamic_slice_in_dim(bucket, half * places, places)
    split = regroup if tiled else regroup_any
    send, scond, seg, src, cidx = split(x_src, cond, lens, buck, group.reshape(1), wide)
    exchange = functools.partial(
        lax.all_to_all, axis_name="wide", split_axis=0, concat_axis=0, tiled=True
    )
    came = exchange(send)
    came_cond = exchange(scond.reshape(wide, slots, feat // wide))
    cond_in = came_cond.transpose(1, 0, 2).reshape(slots, feat)
    x_view = came.reshape(wide, blocks, per_block, feat)
    if not tiled:
        x_view = x_view.transpose(1, 0, 2, 3).reshape(1, blocks, BLK, feat)

    act_low = jax.nn.silu(cond_in.astype(F32)).astype(BF16)
    modulate = jnp.dot(act_low, w_mod, preferred_element_type=F32) + b_mod.astype(F32)
    slot_ids = jnp.arange(slots, dtype=jnp.int32)
    in_slot = seg[:, None] == slot_ids[None, :]
    mod_blocks = jnp.sum(
        jnp.where(in_slot[:, :, None], modulate[None], 0.0), axis=1
    ).reshape(blocks, 6, feat)

    dy = (
        grad_out.reshape(blocks, per_block, wide, feat)
        .transpose(0, 2, 1, 3)
        .reshape(rows, feat)
    )
    gate_two = mod_blocks[:, 5:6, :]
    df = (
        (gate_two * dy.reshape(blocks, BLK, feat).astype(F32)).astype(BF16).reshape(rows, feat)
    )
    grad_b_fc2 = jnp.sum(df.astype(F32), axis=0)
    dg = dot(df, w_fc2, 1, 1)
    w_qkv_t = w_qkv.T
    bias_qkv = jnp.concatenate(
        [b_qv[:feat].astype(F32), jnp.zeros((feat,), F32), b_qv[feat:].astype(F32)]
    ).reshape(3 * feat, 1)

    qkv_t, a1_t = qkv_forward(x_view, mod_blocks, w_qkv_t, bias_qkv)
    o_t, lse = attend(seg, qkv_t)
    attn, x1, a2, a2_t = proj_forward(
        o_t, w_proj, b_proj.astype(F32).reshape(1, feat), x_view, mod_blocks
    )
    own, place = half.reshape(1), group.reshape(1)
    part = feat // devices
    halved = Halves(wide, part)
    both = ("wide", "narrow")
    f, da2, grad_b_fc1, d_fc1, d_fc2 = mlp(
        own, a2, a2_t, df, dg, w_fc1, w_fc2, b_fc1.astype(F32).reshape(1, hidden), halved
    )

    if halved.split:
        fc2_got, fc1_got = swap(d_fc2[0], "narrow", 1), swap(d_fc1[0], "narrow", 1)
    y, dx1, do_t, grad_b_proj, two, d_proj = middle(
        own, seg, act_low, f, b_fc2.astype(F32).reshape(1, feat), x1, attn, dy, da2, mod_blocks, o_t, w_proj,
        halved,
    )
    y_dest = (
        y.reshape(blocks, wide, per_block, feat).transpose(0, 2, 1, 3).reshape(rows, feat)
    )
    near, far = bits_of(wide)[:3], bits_of(wide)[3:]
    orders = chain_orders(wide)
    pieces, head = [], 0

    def attention(counts):
        nonlocal head
        for count in counts:
            pieces.append(attend_back(seg, qkv_t, o_t, do_t, lse, first=head, count=count))
            head += count

    def bias_rows(sums_q):
        sums = [grad_b_fc1[0], grad_b_fc2, grad_b_proj[0], sums_q[0], sums_q[2]]
        return jnp.concatenate(sums).reshape(2 * slots, feat)

    if halved.split:
        proj_got = swap(d_proj[0], "narrow", 1)
        fc2_rows, fc1_rows = d_fc2[1].shape[1], d_fc1[1].shape[1]
        cut = (fc2_rows + fc1_rows + part) // 3 // TILE * TILE
        parts = [
            Part(d_fc2[1], fc2_got, 0, cut, orders[0]),
            Part(d_fc1[1], fc1_got, 0, cut, orders[1]),
            Part(d_fc2[1], fc2_got, cut, fc2_rows - cut, orders[2]),
            Part(d_fc1[1], fc1_got, cut, fc1_rows - cut, orders[2]),
            Part(d_proj[1], proj_got, 0, part, orders[2]),
        ]
        two = Rider(two, far + near)
        sums = Sums(place, parts, streamed=True)
        sums.join(two)
        for counts in ((4, 4, 2), (4,), (2,)):
            (do_t, *pieces) = tie((do_t, *pieces), [sums])
            attention(counts)
            sums.step()
        (a1_t, *pieces) = tie((a1_t, *pieces), [sums])
        d_qkv, sums_q = qkv_grad(own, a1_t, pieces, halved)
        qkv_got = swap(d_qkv[0], "narrow", 1)
        biases = bias_rows(sums_q)
        drows, one = rows_back(seg, pieces, w_qkv_t, x_view, dx1, mod_blocks, biases)
        sums.step()
        qkv_parts = [Part(d_qkv[1], qkv_got, i * part, part, orders[i]) for i in range(3)]
        late = Sums(place, qkv_parts)
        (drows,) = tie((drows,), [sums])
    else:
        attention((4, 4, 4, 4))
        d_qkv, sums_q = qkv_grad(own, a1_t, pieces, halved)
        drows, one = rows_back(seg, pieces, w_qkv_t, x_view, dx1, mod_blocks, bias_rows(sums_q))
    back = drows
    if not tiled:
        back = back.reshape(blocks, wide, per_block, feat).transpose(1, 0, 2, 3)
    back = exchange(back.reshape(wide, rows // wide, feat))
    if halved.split:
        one = Rider(one, far + near)
        late.join(one)
        tie((), [late])
        late.step()
        late.step()
        (back,) = tie((back,), [late])
        while late.going:
            late.step()
        one_all, two_all = (
            jnp.concatenate([a, swap(a, "narrow", 1)], axis=0)
            for a in (r.keep[0].reshape(wide, -1, feat) for r in (one, two))
        )
        fc2_a, fc1_a, fc2_b, fc1_b, grad_w_proj = (p.keep[0] for p in parts)
        grad_w_fc2 = jnp.concatenate([fc2_a, fc2_b], axis=0)
        grad_w_fc1 = jnp.concatenate([fc1_a, fc1_b], axis=0)
        grad_w_fc1 = (
            grad_w_fc1.reshape(hidden // feat, part, feat).transpose(1, 0, 2).reshape(part, hidden)
        )
        grad_w_qkv = jnp.concatenate([p.keep[0] for p in qkv_parts], axis=1)
    else:
        one_all, two_all = (lax.all_gather(a, both, axis=0, tiled=True) for a in (one, two))

        def scattered(full):
            return lax.psum_scatter(full, both, scatter_dimension=0, tiled=True).astype(F32)

        grad_w_fc2 = scattered(d_fc2[0])
        grad_w_fc1 = scattered(d_fc1[0].transpose(1, 0, 2).reshape(feat, hidden))
        grad_w_proj = scattered(d_proj[0])
        grad_w_qkv = scattered(d_qkv[0].transpose(1, 0, 2).reshape(feat, 3 * feat))
    merge = restore if tiled else restore_any
    dx_src = merge(src, back.reshape(rows, feat))

    me = group * halves + half
    grad_w_mod, grad_b_mod, dact, biases = mod_grad(
        group, me, one_all, two_all, w_mod, part, feat // wide, slots
    )
    grad_b_mod = lax.dynamic_slice_in_dim(grad_b_mod[0], me * 6 * part, 6 * part)

    def own_part(first, count):
        rows_of = biases[first : first + count].reshape(-1)
        share = rows_of.shape[0] // devices
        return lax.dynamic_slice_in_dim(rows_of, me * share, share)

    fc1_lines = hidden // feat
    s_fc1, s_fc2, s_proj = own_part(0, fc1_lines), own_part(fc1_lines, 1), own_part(fc1_lines + 1, 1)
    s_qv = own_part(fc1_lines + 2, 2)
    spot = jnp.maximum(cidx, 0)
    bucket_of, slot_of = spot // slots, spot % slots
    if halved.split:
        spot = one.place(bucket_of ^ group) * 2 * slots + slot_of
    else:
        spot = (bucket_of * halves + half) * 2 * slots + slot_of
    _, silu_back = jax.vjp(jax.nn.silu, cond.astype(F32))
    dcond = silu_back(jnp.take(dact, spot, axis=0))[0].astype(BF16)
    dcond = jnp.where(cidx[:, None] >= 0, dcond, jnp.zeros((), BF16))

    return (
        y_dest,
        dx_src,
        dcond,
        grad_w_mod,
        grad_b_mod,
        grad_w_qkv,
        s_qv,
        grad_w_proj,
        s_proj,
        grad_w_fc1,
        s_fc1,
        grad_w_fc2,
        s_fc2,
    )


def solution(mesh):
    both = ("wide", "narrow")
    placed = (P("narrow", "wide"), P("narrow", "wide")) + (P(),) * 12 + (P(both, None),)
    matrix, vector = P(both, None), P(both)
    return jax.shard_map(
        local,
        mesh=mesh,
        in_specs=placed,
        out_specs=(
            matrix,
            P("narrow", "wide"),
            P("narrow", "wide"),
            matrix,
            vector,
            matrix,
            vector,
            matrix,
            vector,
            matrix,
            vector,
            matrix,
            vector,
        ),
        check_vma=False,
    )
```

```python
import functools
import math

import jax
import jax.numpy as jnp
from jax import lax
from jax.experimental import pallas as pl
from jax.experimental.pallas import tpu as pltpu
from jax.sharding import PartitionSpec as P

HEADS = 16
HEAD_DIM = 64
EPS = 1e-06
MASKED = -1000000000.0
LOG2E = 1.4426950408889634
BLK = 256
TILE = 16
VMEM_LIMIT = 58 * 2**20
BRIEF = pl.CostEstimate(flops=1, bytes_accessed=1, transcendentals=0)
BF16 = jnp.bfloat16
F32 = jnp.float32


def params(**more):
    return pltpu.CompilerParams(vmem_limit_bytes=VMEM_LIMIT, **more)


def dot(left, right, left_dim, right_dim):
    return lax.dot_general(
        left, right, (((left_dim,), (right_dim,)), ((), ())), preferred_element_type=F32
    )


def norm_parts(values):
    centre = values - jnp.mean(values, axis=1, keepdims=True)
    spread = jnp.mean(centre * centre, axis=1, keepdims=True)
    inverse = lax.rsqrt(spread + EPS)
    return centre * inverse, inverse


def norm_back(grad, normed, inverse):
    return (
        grad
        - jnp.mean(grad, axis=1, keepdims=True)
        - normed * jnp.mean(grad * normed, axis=1, keepdims=True)
    ) * inverse


def each_place(len_ref, buck_ref, base, count, off_ref, slot_ref, wide, visit):
    for i in range(wide):
        off_ref[i] = 0
        slot_ref[i] = 0

    def place(j, offset):
        units = len_ref[base + j] // wide
        b = buck_ref[base + j]

        @pl.when(units > 0)
        def _():
            start = off_ref[b]
            slot = slot_ref[b]
            off_ref[b] = start + units
            slot_ref[b] = slot + 1
            visit(j, b, units, offset, start, slot)

        return offset + units

    lax.fori_loop(0, count, place, 0)


def regroup_rows_kernel(
    len_ref, buck_ref, me_ref, x_ref, send_ref, src_ref, off_ref, slot_ref, *, wide, places
):
    cells = send_ref.shape[1]
    send_ref[...] = jnp.zeros_like(send_ref)

    @pl.loop(0, src_ref.shape[0])
    def _(i):
        src_ref[i] = -1

    def visit(j, b, units, offset, start, slot):
        @pl.loop(0, units // TILE)
        def _(t):
            a = pl.multiple_of(offset + t * TILE, TILE)
            c = pl.multiple_of(start + t * TILE, TILE)
            send_ref[b, pl.ds(c, TILE), :] = x_ref[pl.ds(a, TILE), :]
            src_ref[a // TILE] = (b * cells + c) // TILE

    each_place(len_ref, buck_ref, me_ref[1] * places, places, off_ref, slot_ref, wide, visit)


def regroup_cond_kernel(
    len_ref, buck_ref, me_ref, cond_ref, scond_ref, seg_ref, cidx_ref,
    off_ref, slot_ref, cond_in, cond_out, *, wide, slots,
):
    cond_out[...] = jnp.zeros_like(cond_out)
    cond_in[...] = cond_ref[...].astype(F32)
    for i in range(seg_ref.shape[0]):
        seg_ref[i] = -1

    @pl.loop(0, cidx_ref.shape[0])
    def _(j):
        cidx_ref[j] = -1

    def visit(j, b, units, offset, start, slot):
        cidx_ref[j] = b * slots + slot
        cond_out[pl.ds(b * slots + slot, 1), :] = cond_in[pl.ds(j, 1), :]

        @pl.when(b == me_ref[0])
        def _():
            @pl.loop(0, units * wide // BLK)
            def _(t):
                seg_ref[start * wide // BLK + t] = slot

    places = cidx_ref.shape[0]
    each_place(len_ref, buck_ref, me_ref[1] * places, places, off_ref, slot_ref, wide, visit)
    scond_ref[...] = cond_out[...].astype(BF16)


def regroup(x_src, cond, lens, buck, me, wide):
    rows, feat = x_src.shape
    places, part = cond.shape
    slots = places // wide
    smem = pl.BlockSpec(memory_space=pltpu.SMEM)
    vmem = pl.BlockSpec(memory_space=pltpu.VMEM)
    counters = [pltpu.SMEM((wide,), jnp.int32), pltpu.SMEM((wide,), jnp.int32)]
    scond, seg, cidx = pl.pallas_call(
        functools.partial(regroup_cond_kernel, wide=wide, slots=slots),
        in_specs=[smem, smem, smem, vmem],
        out_specs=[vmem, smem, smem],
        out_shape=[
            jax.ShapeDtypeStruct((places, part), BF16),
            jax.ShapeDtypeStruct((rows // BLK,), jnp.int32),
            jax.ShapeDtypeStruct((places,), jnp.int32),
        ],
        scratch_shapes=counters + [pltpu.VMEM((places, part), F32), pltpu.VMEM((places, part), F32)],
        compiler_params=params(),
        cost_estimate=BRIEF,
    )(lens, buck, me, cond)
    send, src = pl.pallas_call(
        functools.partial(regroup_rows_kernel, wide=wide, places=places),
        in_specs=[smem, smem, smem, vmem],
        out_specs=[vmem, smem],
        out_shape=[
            jax.ShapeDtypeStruct((wide, rows // wide, feat), BF16),
            jax.ShapeDtypeStruct((rows // TILE,), jnp.int32),
        ],
        scratch_shapes=counters,
        compiler_params=params(),
        cost_estimate=BRIEF,
    )(lens, buck, me, x_src)
    return send, scond, seg, src, cidx


def restore_kernel(src_ref, back_ref, dx_ref):
    @pl.loop(0, src_ref.shape[0])
    def _(i):
        at = src_ref[i]
        rows = back_ref[pl.ds(pl.multiple_of(jnp.maximum(at, 0) * TILE, TILE), TILE), :]
        dx_ref[pl.ds(pl.multiple_of(i * TILE, TILE), TILE), :] = jnp.where(
            at >= 0, rows, jnp.zeros_like(rows)
        )


def restore(src, back):
    vmem = pl.BlockSpec(memory_space=pltpu.VMEM)
    return pl.pallas_call(
        restore_kernel,
        in_specs=[pl.BlockSpec(memory_space=pltpu.SMEM), vmem],
        out_specs=vmem,
        out_shape=jax.ShapeDtypeStruct(back.shape, BF16),
        compiler_params=params(),
        cost_estimate=BRIEF,
    )(src, back)


def regroup_any(x_src, cond, lens, buck, me, wide):
    rows, feat = x_src.shape
    places = cond.shape[0]
    lens = lax.dynamic_slice_in_dim(lens, me[1] * places, places)
    buck = lax.dynamic_slice_in_dim(buck, me[1] * places, places)
    slots, cells = places // wide, rows // wide
    units = lens // wide
    order = jnp.arange(places, dtype=jnp.int32)
    earlier = (order[:, None] < order[None, :]) & (buck[:, None] == buck[None, :])
    live = (lens > 0).astype(jnp.int32)
    offset = jnp.cumsum(units) - units
    start = jnp.sum(jnp.where(earlier, units[:, None], 0), axis=0)
    slot = jnp.sum(jnp.where(earlier, live[:, None], 0), axis=0)
    cell = jnp.arange(cells, dtype=jnp.int32)[None, :, None]
    to_target = (buck[None, :] == jnp.arange(wide, dtype=jnp.int32)[:, None]) & (live[None, :] > 0)
    hit = (
        to_target[:, None, :]
        & (cell >= start[None, None, :])
        & (cell < (start + units)[None, None, :])
    ).astype(jnp.int32)
    valid = jnp.sum(hit, axis=2)
    source = jnp.sum(hit * (offset - start)[None, None, :], axis=2) + cell[:, :, 0]
    source = jnp.where(valid > 0, source, 0)
    picked = jnp.take(x_src, source.reshape(-1), axis=0).reshape(wide, cells, feat)
    send = jnp.where(valid[:, :, None] > 0, picked, jnp.zeros((), BF16))
    cond_hit = to_target[:, None, :] & (
        slot[None, None, :] == jnp.arange(slots, dtype=jnp.int32)[None, :, None]
    )
    scond = jnp.einsum("wqs,sf->wqf", cond_hit.astype(BF16), cond, preferred_element_type=F32)
    scond = scond.astype(BF16).reshape(cond.shape)
    first = jnp.arange(rows // BLK, dtype=jnp.int32)[:, None] * BLK
    mine = (
        ((buck == me[0]) & (live > 0))[None, :]
        & (first >= (start * wide)[None, :])
        & (first < ((start + units) * wide)[None, :])
    )
    seg = jnp.sum(jnp.where(mine, slot[None, :] + 1, 0), axis=1) - 1
    spot = jnp.arange(rows, dtype=jnp.int32)[:, None]
    inside = (live[None, :] > 0) & (spot >= offset[None, :]) & (spot < (offset + units)[None, :])
    src = jnp.sum(jnp.where(inside, (buck * cells + start - offset)[None, :] + spot + 1, 0), axis=1)
    cidx = jnp.where(live > 0, buck * slots + slot, -1)
    return send, scond, seg.astype(jnp.int32), src - 1, cidx


def restore_any(src, back):
    dx = jnp.take(back, jnp.maximum(src, 0), axis=0)
    return jnp.where(src[:, None] >= 0, dx, jnp.zeros((), BF16))


def qkv_kernel(x_ref, mod_ref, w_ref, b_ref, q_ref, a_ref):
    feat = x_ref.shape[-1]
    x = x_ref[...].reshape(BLK, feat).astype(F32)
    normed, _ = norm_parts(x)
    a1 = (normed * (1.0 + mod_ref[0, 1:2, :]) + mod_ref[0, 0:1, :]).astype(BF16)
    a1_t = a1.T
    a_ref[...] = a1_t
    for i in range(3):
        part = slice(i * feat, (i + 1) * feat)
        q_ref[part, :] = (dot(w_ref[part, :], a1_t, 1, 0) + b_ref[part, :]).astype(BF16)


def row_spec(view):
    return pl.BlockSpec((view[0], 1, view[2], view[3]), lambda k: (0, k, 0, 0))


def whole(*shape):
    return pl.BlockSpec(shape, lambda k: (0,) * len(shape))


def qkv_forward(x_view, mod_blocks, w_t, bias):
    feat = x_view.shape[-1]
    blocks = x_view.shape[1]
    return pl.pallas_call(
        qkv_kernel,
        grid=(blocks,),
        in_specs=[
            row_spec(x_view.shape),
            pl.BlockSpec((1, 6, feat), lambda k: (k, 0, 0)),
            whole(3 * feat, feat),
            whole(3 * feat, 1),
        ],
        out_specs=[
            pl.BlockSpec((3 * feat, BLK), lambda k: (0, k)),
            pl.BlockSpec((feat, BLK), lambda k: (0, k)),
        ],
        out_shape=[
            jax.ShapeDtypeStruct((3 * feat, blocks * BLK), BF16),
            jax.ShapeDtypeStruct((feat, blocks * BLK), BF16),
        ],
        compiler_params=params(),
        cost_estimate=BRIEF,
    )(x_view, mod_blocks, w_t, bias)


def masks(seg_ref, query_block, blocks):
    base = LOG2E / math.sqrt(HEAD_DIM)
    same = [seg_ref[query_block] == seg_ref[kb] for kb in range(blocks)]
    scales = [jnp.where(s, base, 0.0) for s in same]
    shifts = [jnp.where(s, 0.0, MASKED * LOG2E) for s in same]
    return scales, shifts


def attend_kernel(seg_ref, q_ref, k_ref, v_ref, o_ref, lse_ref, *, blocks, heads):
    units = [(h, qb) for h in range(heads) for qb in range(blocks)]
    keys = [k_ref[h * HEAD_DIM : (h + 1) * HEAD_DIM, :].T for h in range(heads)]

    def spans(h, qb):
        return slice(h * HEAD_DIM, (h + 1) * HEAD_DIM), slice(qb * BLK, (qb + 1) * BLK)

    def scores_of(h, qb):
        q_t = q_ref[spans(h, qb)]
        return [dot(keys[h][kb * BLK : (kb + 1) * BLK], q_t, 1, 0) for kb in range(blocks)]

    def finish(h, qb, probs, total, top):
        hs, qs = spans(h, qb)
        out = dot(v_ref[hs, :], probs, 1, 0)
        o_ref[hs, qs] = (out / total).astype(BF16)
        lse_ref[h, :, qs] = top + jnp.log2(total)

    ahead, behind = scores_of(*units[0]), None
    for i, (h, qb) in enumerate(units):
        scores, ahead = ahead, scores_of(*units[i + 1]) if i + 1 < len(units) else None
        scales, shifts = masks(seg_ref, qb, blocks)
        top = None
        for kb in range(blocks):
            peak = jnp.max(scores[kb], axis=0, keepdims=True) * scales[kb] + shifts[kb]
            top = peak if top is None else jnp.maximum(top, peak)
        if behind is not None:
            finish(*behind)
        total = jnp.zeros((1, BLK), F32)
        parts = []
        for kb in range(blocks):
            expo = jnp.exp2(scores[kb] * scales[kb] - (top - shifts[kb]))
            total = total + jnp.sum(expo, axis=0, keepdims=True)
            parts.append(expo.astype(BF16))
        behind = (h, qb, jnp.concatenate(parts, axis=0), total, top)
    finish(*behind)


def attend(seg, qkv_t, heads=4):
    feat3, rows = qkv_t.shape
    feat = feat3 // 3
    span = heads * HEAD_DIM
    groups = feat // span
    return pl.pallas_call(
        functools.partial(attend_kernel, blocks=rows // BLK, heads=heads),
        grid_spec=pltpu.PrefetchScalarGridSpec(
            num_scalar_prefetch=1,
            grid=(groups,),
            in_specs=[
                pl.BlockSpec((span, rows), lambda g, s: (g, 0)),
                pl.BlockSpec((span, rows), lambda g, s: (groups + g, 0)),
                pl.BlockSpec((span, rows), lambda g, s: (2 * groups + g, 0)),
            ],
            out_specs=[
                pl.BlockSpec((span, rows), lambda g, s: (g, 0)),
                pl.BlockSpec((heads, 1, rows), lambda g, s: (g, 0, 0)),
            ],
        ),
        out_shape=[
            jax.ShapeDtypeStruct((feat, rows), BF16),
            jax.ShapeDtypeStruct((feat // HEAD_DIM, 1, rows), F32),
        ],
        compiler_params=params(),
        cost_estimate=BRIEF,
    )(seg, qkv_t, qkv_t, qkv_t)


def attend_back_kernel(
    seg_ref, q_ref, k_ref, v_ref, o_ref, do_ref, lse_ref, out_ref, sums_ref, *, blocks, heads
):
    scale = 1.0 / math.sqrt(HEAD_DIM)
    units = [(h, qb) for h in range(heads) for qb in range(blocks)]
    keys = [k_ref[h * HEAD_DIM : (h + 1) * HEAD_DIM, :].T for h in range(heads)]
    values = [v_ref[h * HEAD_DIM : (h + 1) * HEAD_DIM, :].T for h in range(heads)]

    def spans(h, qb):
        return slice(h * HEAD_DIM, (h + 1) * HEAD_DIM), slice(qb * BLK, (qb + 1) * BLK)

    def products(h, qb):
        q_t, do_t = q_ref[spans(h, qb)], do_ref[spans(h, qb)]
        cuts = [slice(kb * BLK, (kb + 1) * BLK) for kb in range(blocks)]
        return [(dot(keys[h][c], q_t, 1, 0), dot(values[h][c], do_t, 1, 0)) for c in cuts]

    ahead = products(*units[0])
    grad_k = grad_v = inner = None
    for i, (h, qb) in enumerate(units):
        present, ahead = ahead, products(*units[i + 1]) if i + 1 < len(units) else None
        hs, qs = spans(h, qb)
        if qb == 0:
            inner = jnp.sum(
                o_ref[hs, :].astype(F32) * do_ref[hs, :].astype(F32), axis=0, keepdims=True
            )
        scales, shifts = masks(seg_ref, qb, blocks)
        probs, grads = [], []
        for kb, (score, grad_p) in enumerate(present):
            prob = jnp.exp2(score * scales[kb] - (lse_ref[h, :, qs] - shifts[kb]))
            probs.append(prob.astype(BF16))
            grads.append((prob * (grad_p - inner[:, qs])).astype(BF16))
        probs = jnp.concatenate(probs, axis=0)
        grads = jnp.concatenate(grads, axis=0)
        out_ref[0, hs, qs] = (dot(k_ref[hs, :], grads, 1, 0) * scale).astype(BF16)
        more_k, more_v = dot(q_ref[hs, qs], grads, 1, 1), dot(do_ref[hs, qs], probs, 1, 1)
        grad_k = more_k if qb == 0 else grad_k + more_k
        grad_v = more_v if qb == 0 else grad_v + more_v
        if qb == blocks - 1:
            out_ref[1, hs, :] = (grad_k * scale).astype(BF16)
            out_ref[2, hs, :] = grad_v.astype(BF16)
    ones = jnp.ones((8, out_ref.shape[2]), BF16)
    sums_ref[0] = dot(ones, out_ref[0], 1, 1)
    sums_ref[1] = dot(ones, out_ref[2], 1, 1)


def attend_back(seg, qkv_t, o_t, do_t, lse, first, count, heads=2):
    feat3, rows = qkv_t.shape
    feat = feat3 // 3
    span = heads * HEAD_DIM
    groups = feat // span
    at = first // heads
    return pl.pallas_call(
        functools.partial(attend_back_kernel, blocks=rows // BLK, heads=heads),
        grid_spec=pltpu.PrefetchScalarGridSpec(
            num_scalar_prefetch=1,
            grid=(count // heads,),
            in_specs=[
                pl.BlockSpec((span, rows), lambda g, s: (at + g, 0)),
                pl.BlockSpec((span, rows), lambda g, s: (groups + at + g, 0)),
                pl.BlockSpec((span, rows), lambda g, s: (2 * groups + at + g, 0)),
                pl.BlockSpec((span, rows), lambda g, s: (at + g, 0)),
                pl.BlockSpec((span, rows), lambda g, s: (at + g, 0)),
                pl.BlockSpec((heads, 1, rows), lambda g, s: (at + g, 0, 0)),
            ],
            out_specs=[
                pl.BlockSpec((3, span, rows), lambda g, s: (0, g, 0)),
                pl.BlockSpec((2, 8, span), lambda g, s: (0, 0, g)),
            ],
        ),
        out_shape=[
            jax.ShapeDtypeStruct((3, count * HEAD_DIM, rows), BF16),
            jax.ShapeDtypeStruct((2, 8, count * HEAD_DIM), F32),
        ],
        compiler_params=params(),
        cost_estimate=BRIEF,
    )(seg, qkv_t, qkv_t, qkv_t, o_t, do_t, lse)


class Halves:
    def __init__(self, wide, part, split=None):
        self.wide, self.part = wide, part
        self.split = part % TILE == 0 if split is None else split

    def shapes(self, between, columns):
        if self.split:
            shape = (self.wide,) + between + (self.part, columns)
            return [jax.ShapeDtypeStruct(shape, BF16)] * 2
        return [jax.ShapeDtypeStruct(between + (2 * self.wide * self.part, columns), BF16)]

    def specs(self, between, columns, index):
        ones = (1,) * between
        if self.split:
            return [
                pl.BlockSpec(
                    (self.wide,) + ones + (self.part, columns),
                    lambda *g: (0,) + index(*g)[:-1] + (0, index(*g)[-1]),
                )
            ] * 2
        return [
            pl.BlockSpec(
                ones + (2 * self.wide * self.part, columns),
                lambda *g: index(*g)[:-1] + (0, index(*g)[-1]),
            )
        ]

    def store(self, half, value, refs):
        if not self.split:
            refs[0][...] = value.astype(BF16).reshape(refs[0].shape)
            return
        value = value.reshape(value.shape[0] // (2 * self.part), 2, self.part, value.shape[1])
        even, odd = value[:, 0], value[:, 1]
        folds = refs[0].shape[-1] // value.shape[-1]
        if folds > 1:
            even, odd = (
                jnp.concatenate(jnp.split(half_value, folds, axis=1), axis=2) for half_value in (even, odd)
            )
        refs[0][...] = jnp.where(half == 0, odd, even).astype(BF16).reshape(refs[0].shape)
        refs[1][...] = jnp.where(half == 0, even, odd).astype(BF16).reshape(refs[1].shape)

    def finish(self, arrays):
        if self.split:
            return [a.reshape(self.wide, -1, a.shape[-1]) for a in arrays]
        return arrays


def qkv_grad_kernel(half_ref, a_ref, *refs, pieces, halves):
    ins, outs = refs[:pieces], refs[pieces:]
    value = jnp.concatenate([dot(a_ref[...], r[0], 1, 1) for r in ins], axis=1)
    halves.store(half_ref[0], value, outs)


def qkv_grad(half, a1_t, dqkv, halves):
    feat, rows = a1_t.shape
    columns = sum(d.shape[1] for d in dqkv)
    folds = feat // columns if halves.split else 1
    packed = Halves(halves.wide, halves.part // folds, halves.split)
    packed_columns = folds * columns
    out = pl.pallas_call(
        functools.partial(qkv_grad_kernel, pieces=len(dqkv), halves=halves),
        grid=(3,),
        in_specs=[pl.BlockSpec(memory_space=pltpu.SMEM), whole(feat, rows)]
        + [pl.BlockSpec((1, d.shape[1], rows), lambda i: (i, 0, 0)) for d in dqkv],
        out_specs=packed.specs(1, packed_columns, lambda i: (i, 0)),
        out_shape=packed.shapes((3,), packed_columns),
        compiler_params=params(),
        cost_estimate=BRIEF,
    )(half, a1_t, *dqkv)
    return halves.finish(out)


def proj_kernel(o_ref, w_ref, b_ref, x_ref, mod_ref, attn_ref, x1_ref, a_ref, at_ref):
    feat = x_ref.shape[-1]
    attn = dot(o_ref[...], w_ref[...], 0, 0) + b_ref[...]
    attn_ref[...] = attn
    x1 = x_ref[...].reshape(BLK, feat).astype(F32) + mod_ref[0, 2:3, :] * attn
    x1_ref[...] = x1
    normed, _ = norm_parts(x1)
    a2 = (normed * (1.0 + mod_ref[0, 4:5, :]) + mod_ref[0, 3:4, :]).astype(BF16)
    a_ref[...] = a2
    at_ref[...] = a2.T


def proj_forward(o_t, w_proj, b_proj, x_view, mod_blocks):
    feat = x_view.shape[-1]
    blocks = x_view.shape[1]
    rows = blocks * BLK
    by_row = pl.BlockSpec((BLK, feat), lambda k: (k, 0))
    by_column = pl.BlockSpec((feat, BLK), lambda k: (0, k))
    return pl.pallas_call(
        proj_kernel,
        grid=(blocks,),
        in_specs=[
            by_column,
            whole(feat, feat),
            whole(1, feat),
            row_spec(x_view.shape),
            pl.BlockSpec((1, 6, feat), lambda k: (k, 0, 0)),
        ],
        out_specs=[by_row, by_row, by_row, by_column],
        out_shape=[
            jax.ShapeDtypeStruct((rows, feat), F32),
            jax.ShapeDtypeStruct((rows, feat), F32),
            jax.ShapeDtypeStruct((rows, feat), BF16),
            jax.ShapeDtypeStruct((feat, rows), BF16),
        ],
        compiler_params=params(),
        cost_estimate=BRIEF,
    )(o_t, w_proj, b_proj, x_view, mod_blocks)


def gelu_both(u):
    c = math.sqrt(2.0 / math.pi)
    square = u * u
    half = 0.5 + 0.5 * jnp.tanh(u * (c + (c * 0.044715) * square))
    g = u * half
    return g, half + (g - g * half) * (2.0 * c + (6.0 * c * 0.044715) * square)


def mlp_kernel(
    half_ref, a_ref, at_ref, df_ref, dg_ref, w1_ref, w2_ref, b1_ref, *refs, first, second
):
    f_ref, da_ref, db_ref = refs[:3]
    g_ref, du_ref = refs[-2:]
    outs = refs[3:-2]
    outs_one, outs_two = outs[: len(outs) // 2], outs[len(outs) // 2 :]
    step = pl.program_id(0)
    rows = a_ref.shape[0]

    @pl.when(step == 0)
    def _():
        f_ref[...] = jnp.zeros_like(f_ref)
        da_ref[...] = jnp.zeros_like(da_ref)

    w1, w2 = w1_ref[...], w2_ref[...]
    bias = jnp.zeros((1, w1.shape[1]), F32)
    cuts = [slice(r, r + BLK) for r in range(0, rows, BLK)]
    u = dot(a_ref[cuts[0], :], w1, 1, 0)
    for r, rs in enumerate(cuts):
        later = dot(a_ref[cuts[r + 1], :], w1, 1, 0) if r + 1 < len(cuts) else None
        g, slope = gelu_both(u + b1_ref[...])
        du = dg_ref[rs, :] * slope
        bias = bias + jnp.sum(du, axis=0, keepdims=True)
        g_ref[rs, :] = g.astype(BF16)
        du_ref[rs, :] = du.astype(BF16)
        u = later
        for past in cuts[r - 1 : r] if r + 1 < len(cuts) else cuts[max(r - 1, 0) :]:
            f_ref[past, :] += dot(g_ref[past, :], w2, 1, 0)
            da_ref[past, :] += dot(du_ref[past, :], w1, 1, 1)
    db_ref[...] = bias
    first.store(half_ref[0], dot(at_ref[...], du_ref[...], 1, 0), outs_one)
    second.store(half_ref[0], dot(g_ref[...], df_ref[...], 0, 0), outs_two)


def mlp(half, a2, a2_t, df, dg, w1, w2, b1, halves, width=512):
    rows, feat = a2.shape
    hidden = w1.shape[1]
    per = feat // width
    wide = halves.wide
    part = hidden // (2 * wide)
    first = halves
    second = Halves(wide, part)
    second.split = halves.split
    one = pl.Buffered(1)

    def fixed(*shape):
        return pl.BlockSpec(shape, lambda j: (0,) * len(shape), pipeline_mode=one)

    if halves.split:
        two_specs = [pl.BlockSpec((width // (2 * part), part, feat), lambda j: (j, 0, 0))] * 2
        two_shapes = [jax.ShapeDtypeStruct((wide, part, feat), BF16)] * 2
    else:
        two_specs = [pl.BlockSpec((width, feat), lambda j: (j, 0))]
        two_shapes = [jax.ShapeDtypeStruct((hidden, feat), BF16)]
    out = pl.pallas_call(
        functools.partial(mlp_kernel, first=first, second=second),
        grid=(hidden // width,),
        in_specs=[
            pl.BlockSpec(memory_space=pltpu.SMEM),
            fixed(rows, feat),
            fixed(feat, rows),
            fixed(rows, feat),
            pl.BlockSpec((rows, width), lambda j: (0, j)),
            pl.BlockSpec((feat, width), lambda j: (0, j)),
            pl.BlockSpec((width, feat), lambda j: (j, 0)),
            pl.BlockSpec((1, width), lambda j: (0, j)),
        ],
        out_specs=[whole(rows, feat), whole(rows, feat), pl.BlockSpec((1, width), lambda j: (0, j))]
        + halves.specs(1, width, lambda j: (j // per, j % per))
        + two_specs,
        out_shape=[
            jax.ShapeDtypeStruct((rows, feat), F32),
            jax.ShapeDtypeStruct((rows, feat), F32),
            jax.ShapeDtypeStruct((1, hidden), F32),
        ]
        + halves.shapes((hidden // feat,), feat)
        + two_shapes,
        scratch_shapes=[pltpu.VMEM((rows, width), BF16), pltpu.VMEM((rows, width), BF16)],
        compiler_params=params(),
        cost_estimate=BRIEF,
    )(half, a2, a2_t, df, dg, w1, w2, b1)
    f, da2, bias = out[:3]
    rest = out[3:]
    count = len(rest) // 2
    return f, da2, bias, first.finish(rest[:count]), second.finish(rest[count:])


def to_slot(ref, slot, slots, terms):
    @pl.when(slot >= 0)
    def _():
        for i, term in enumerate(terms):
            ref[pl.ds(2 * slots * i + slot, 1), :] += jnp.sum(term, axis=0, keepdims=True)


def middle_kernel(
    half_ref, seg_ref, f_ref, b2_ref, x1_ref, attn_ref, dy_ref, da_ref, mod_ref, o_ref, w_ref, act_ref,
    y_ref, dx_ref, do_ref, db_ref, sums_ref, *rest, halves,
):
    k = pl.program_id(0)
    outs, acc_ref, slot_ref = rest[:-2], rest[-2], rest[-1]
    slots = act_ref.shape[0]

    @pl.when(k == 0)
    def _():
        acc_ref[...] = jnp.zeros_like(acc_ref)
        db_ref[...] = jnp.zeros_like(db_ref)
        slot_ref[...] = jnp.zeros_like(slot_ref)
        slot_ref[slots : 2 * slots, :] = act_ref[...].astype(F32)

    f = f_ref[...] + b2_ref[...]
    x1 = x1_ref[...]
    dy = dy_ref[...].astype(F32)
    y_ref[...] = (x1 + mod_ref[0, 5:6, :] * f).astype(BF16)
    normed, inverse = norm_parts(x1)
    da = da_ref[...]
    dx1 = dy + norm_back(da * (1.0 + mod_ref[0, 4:5, :]), normed, inverse)
    dx_ref[...] = dx1
    dattn = (mod_ref[0, 2:3, :] * dx1).astype(BF16)
    db_ref[...] += jnp.sum(dattn.astype(F32), axis=0, keepdims=True)
    to_slot(slot_ref, seg_ref[k], slots, [dx1 * attn_ref[...], da, da * normed, dy * f])
    do_ref[...] = dot(w_ref[...], dattn, 1, 1).astype(BF16)
    acc_ref[...] += dot(o_ref[...], dattn, 1, 0)

    @pl.when(k == pl.num_programs(0) - 1)
    def _():
        halves.store(half_ref[0], acc_ref[...], outs)
        sums_ref[0] = slot_ref[...].astype(BF16)


def middle(half, seg, act, f, b2, x1, attn, dy, da2, mod_blocks, o_t, w_proj, halves):
    rows, feat = x1.shape
    by_row = pl.BlockSpec((BLK, feat), lambda k: (k, 0))
    by_column = pl.BlockSpec((feat, BLK), lambda k: (0, k))
    blocks = rows // BLK
    slots = act.shape[0]
    out = pl.pallas_call(
        functools.partial(middle_kernel, halves=halves),
        grid=(blocks,),
        in_specs=[
            pl.BlockSpec(memory_space=pltpu.SMEM),
            pl.BlockSpec(memory_space=pltpu.SMEM),
            by_row, whole(1, feat), by_row, by_row, by_row, by_row,
            pl.BlockSpec((1, 6, feat), lambda k: (k, 0, 0)),
            by_column, whole(feat, feat), whole(slots, feat),
        ],
        out_specs=[
            by_row, by_row, by_column, whole(1, feat),
            whole(1, 8 * slots, feat),
        ] + halves.specs(0, feat, lambda k: (0,)),
        out_shape=[
            jax.ShapeDtypeStruct((rows, feat), BF16),
            jax.ShapeDtypeStruct((rows, feat), F32),
            jax.ShapeDtypeStruct((feat, rows), BF16),
            jax.ShapeDtypeStruct((1, feat), F32),
            jax.ShapeDtypeStruct((1, 8 * slots, feat), BF16),
        ]
        + halves.shapes((), feat),
        scratch_shapes=[pltpu.VMEM((feat, feat), F32), pltpu.VMEM((8 * slots, feat), F32)],
        compiler_params=params(),
        cost_estimate=BRIEF,
    )(half, seg, f, b2, x1, attn, dy, da2, mod_blocks, o_t, w_proj, act)
    return tuple(out[:5]) + (halves.finish(out[5:]),)


def rows_back_kernel(seg_ref, w_ref, x_ref, dx_ref, mod_ref, bias_ref, *refs):
    out_ref, sums_ref, slot_ref = refs[-3:]
    slots = bias_ref.shape[0] // 2

    @pl.when(pl.program_id(0) == 0)
    def _():
        slot_ref[...] = jnp.zeros_like(slot_ref)
        slot_ref[slots : 2 * slots, :] = bias_ref[:slots, :]
        slot_ref[3 * slots :, :] = bias_ref[slots:, :]

    feat = x_ref.shape[-1]
    da = None
    for i in range(3):
        at = i * feat
        for ref in refs[:-3]:
            more = dot(ref[i], w_ref[at : at + ref.shape[1], :], 0, 0)
            da = more if da is None else da + more
            at += ref.shape[1]
    normed, inverse = norm_parts(x_ref[...].reshape(BLK, feat).astype(F32))
    out = dx_ref[...] + norm_back(da * (1.0 + mod_ref[0, 1:2, :]), normed, inverse)
    out_ref[...] = out.astype(BF16).reshape(out_ref.shape)
    to_slot(slot_ref, seg_ref[pl.program_id(0)], slots, [da, da * normed])
    sums_ref[0] = slot_ref[...].astype(BF16)


def rows_back(seg, dqkv, w_t, x_view, dx1, mod_blocks, biases):
    rows, feat = dx1.shape
    blocks = rows // BLK
    return pl.pallas_call(
        rows_back_kernel,
        grid=(blocks,),
        in_specs=[
            pl.BlockSpec(memory_space=pltpu.SMEM),
            whole(3 * feat, feat),
            row_spec(x_view.shape),
            pl.BlockSpec((BLK, feat), lambda k: (k, 0)),
            pl.BlockSpec((1, 6, feat), lambda k: (k, 0, 0)),
            whole(*biases.shape),
        ]
        + [pl.BlockSpec((3, d.shape[1], BLK), lambda k: (0, 0, k)) for d in dqkv],
        out_specs=[row_spec(x_view.shape), whole(1, 2 * biases.shape[0], feat)],
        out_shape=[
            jax.ShapeDtypeStruct(x_view.shape, BF16),
            jax.ShapeDtypeStruct((1, 2 * biases.shape[0], feat), BF16),
        ],
        scratch_shapes=[pltpu.VMEM((2 * biases.shape[0], feat), F32)],
        compiler_params=params(),
        cost_estimate=BRIEF,
    )(seg, w_t, x_view, dx1, mod_blocks, biases, *dqkv)


def mod_grad_kernel(
    ids_ref, dev_ref, spot_ref, one_ref, two_ref, w_ref, cond_ref,
    gw_ref, gb_ref, dcond_ref, bias_ref, act_ref, moved_ref, dact_ref, picked_ref, *, part, slots,
):
    @pl.loop(0, one_ref.shape[0])
    def _(p):
        moved_ref[p] = one_ref[dev_ref[p]]

    feat = one_ref.shape[-1]

    def columns(ref):
        wide = ref[...].astype(F32)
        wide = wide.reshape(wide.shape[0], -1, 2 * slots, feat)
        return [wide[:, i].reshape(-1, feat) for i in range(wide.shape[1])]

    one, two = columns(moved_ref), columns(two_ref)
    rows = one[0].shape[0]
    first = lax.broadcasted_iota(jnp.int32, (rows, 1), 0) % (2 * slots) < slots
    act_ref[...] = jnp.where(first, pltpu.roll(two[0], rows - slots, 0), 0.0).T
    act = act_ref[pl.ds(pl.multiple_of(ids_ref[1] * part, 8), part), :].astype(BF16)
    dact = None
    for i, values in enumerate(one + two):
        at = slice(i * feat, (i + 1) * feat)
        low = values.astype(BF16)
        gw_ref[:, at] = dot(act, low, 1, 0)
        gb_ref[:, at] = jnp.sum(jnp.where(first, values, 0.0), axis=0, keepdims=True)
        more = dot(low, w_ref[:, at], 1, 1)
        dact = more if dact is None else dact + more
    dact_ref[...] = dact

    @pl.loop(0, spot_ref.shape[0])
    def _(j):
        at = spot_ref[j]
        row = dact_ref[pl.ds(jnp.maximum(at, 0), 1), :]
        picked_ref[pl.ds(j, 1), :] = jnp.where(at >= 0, row, 0.0)

    cond = cond_ref[...].astype(F32)
    gate = 1.0 / (1.0 + jnp.exp(-cond))
    dcond_ref[...] = (picked_ref[...] * (gate * (1.0 + cond * (1.0 - gate)))).astype(BF16)
    for i, values in enumerate(one):
        sums = jnp.sum(values.reshape(-1, 2 * slots, feat), axis=0)
        bias_ref[i * slots : (i + 1) * slots, :] = sums[slots:, :]


def mod_grad(group, me, device_of, spot, one, two, w_mod, cond, part, slots):
    feat, columns = w_mod.shape
    places, share = cond.shape
    count = 2 * slots * one.shape[0]

    def fixed(*shape):
        return pl.BlockSpec(shape, lambda i, *scalars: (0,) * len(shape))

    return pl.pallas_call(
        functools.partial(mod_grad_kernel, part=part, slots=slots),
        grid_spec=pltpu.PrefetchScalarGridSpec(
            num_scalar_prefetch=3,
            grid=(1,),
            in_specs=[
                fixed(*one.shape),
                fixed(*two.shape),
                pl.BlockSpec((share, columns), lambda i, ids, *scalars: (ids[0], 0)),
                fixed(places, share),
            ],
            out_specs=[
                fixed(part, columns),
                fixed(1, columns),
                fixed(places, share),
                fixed(2 * slots, feat),
            ],
            scratch_shapes=[pltpu.VMEM((feat, count), F32), pltpu.VMEM(one.shape, BF16), pltpu.VMEM((count, share), F32), pltpu.VMEM((places, share), F32)],
        ),
        out_shape=[
            jax.ShapeDtypeStruct((part, columns), F32),
            jax.ShapeDtypeStruct((1, columns), F32),
            jax.ShapeDtypeStruct((places, share), BF16),
            jax.ShapeDtypeStruct((2 * slots, feat), F32),
        ],
        compiler_params=params(),
        cost_estimate=BRIEF,
    )(jnp.stack([group, me]), device_of, spot, one, two, w_mod, cond)


def swap(values, axis, bit):
    count = lax.axis_size(axis)
    return lax.ppermute(values, axis, [(i, i ^ bit) for i in range(count)])


def bits_of(wide):
    return [1 << i for i in range(wide.bit_length() - 1)]


def chain_orders(wide):
    bits = bits_of(wide)
    near, far = bits[:3], bits[3:]
    return [near[i:] + near[:i] + far for i in range(3)]


class Part:
    def __init__(self, keep, got, start, rows, order):
        self.keep, self.got, self.at = keep, got, start
        self.rows = rows
        self.fresh = True
        self.dims = list(reversed(bits_of(keep.shape[0])))
        self.order = list(order)


class Rider:
    def __init__(self, values, order):
        self.keep, self.got, self.at = values, None, 0
        self.rows = values.shape[1]
        self.fresh = True
        self.order, self.done = list(order), []

    def differences(self):
        return [sum(b for i, b in enumerate(self.done) if p >> i & 1) for p in range(1 << len(self.done))]

    def place(self, difference):
        at = jnp.zeros_like(difference)
        for i, bit in enumerate(self.done):
            at = at + ((difference // bit) % 2) * (1 << i)
        return at


def relay_kernel(me_ref, *refs, plan, inputs, outputs):
    ins, outs, scratch = refs[:inputs], refs[inputs : inputs + outputs], list(refs[inputs + outputs :])
    arriving = {}
    if scratch:
        sems = scratch.pop()
        for i, (kind, keep, got, at, rows, *_) in enumerate(plan):
            if kind == "fresh":
                for source in (keep, got):
                    k = len(arriving)
                    copy = pltpu.make_async_copy(
                        ins[source].at[:, pl.ds(at, rows), :], scratch[k], sems.at[k]
                    )
                    copy.start()
                    arriving[i, source == got] = (copy, scratch[k])
    for i, (kind, keep, got, at, rows, bit, inner, count, targets) in enumerate(plan):
        if kind == "ride":
            pieces = [ins[keep][0]]
            if got is not None:
                pieces.append(ins[got][at : at + rows, :])
            for out, base in targets:
                for k, piece in enumerate(pieces):
                    to = slice(base + k * rows, base + (k + 1) * rows)
                    if len(outs[out].shape) == 3:
                        outs[out][0, to, :] = piece
                    else:
                        outs[out][to, :] = piece
            continue
        if kind == "fresh":
            for copy, _ in (arriving[i, False], arriving[i, True]):
                copy.wait()
            k_ref, g_ref = arriving[i, False][1], arriving[i, True][1]
        else:
            k_ref, g_ref = ins[keep], ins[got]
        if bit is None:
            outs[targets[0][0]][...] = k_ref[0].astype(F32) + g_ref[at : at + rows, :].astype(F32)
            continue
        own = (me_ref[0] // bit) % 2

        @pl.loop(0, count // 2)
        def _(e, kind=kind, at=at, own=own, rows=rows, inner=inner, k_ref=k_ref, g_ref=g_ref, targets=targets):
            outer = (e // inner) * 2 * inner + e % inner
            for which, (out, base) in zip((1 - own, own), targets, strict=True):
                entry = outer + which * inner
                if kind == "fresh":
                    right = g_ref[entry]
                else:
                    right = g_ref[pl.ds(pl.multiple_of(at + entry * rows, TILE), rows), :]
                total = k_ref[entry] + right
                if base is None:
                    outs[out][e] = total
                else:
                    outs[out][pl.ds(pl.multiple_of(base + e * rows, TILE), rows), :] = total


def relay(me, moving):
    arrays, places, plan, shapes, sends = [], [], [], [], {}
    columns = moving[0].keep.shape[2]
    vmem, hbm = pl.BlockSpec(memory_space=pltpu.VMEM), pl.BlockSpec(memory_space=pl.ANY)

    def index(array, place):
        if array is None:
            return None
        for i, known in enumerate(arrays):
            if known is array:
                return i
        arrays.append(array)
        places.append(place)
        return len(arrays) - 1

    bits = sorted({m.order[0] for m in moving if m.order})
    sizes = dict.fromkeys(bits, 0)
    scratch, keeps = [], []
    for m in moving:
        bit = m.order[0] if m.order else None
        ride = isinstance(m, Rider)
        kind = "ride" if ride else "fresh" if m.fresh else "add"
        place = hbm if kind == "fresh" else vmem
        keep, got, at = index(m.keep, place), index(m.got, place), m.at
        rows, inner, count = m.rows, 1, 1
        to = (bits.index(bit), sizes[bit]) if bit is not None else None
        kept = len(bits) + len(shapes)
        keeps.append(kept)
        if ride:
            m.rows *= 1 if got is None else 2
            shapes.append(jax.ShapeDtypeStruct((1, m.rows, columns), BF16))
            targets = [(kept, 0)] + ([] if to is None else [to])
            size = m.rows
        elif bit is None:
            shapes.append(jax.ShapeDtypeStruct((rows, columns), F32))
            targets, size = [(kept, 0)], 0
        else:
            dim = m.dims.index(bit)
            count, inner = 1 << len(m.dims), 1 << (len(m.dims) - 1 - dim)
            m.dims.pop(dim)
            size = count // 2 * rows
            shapes.append(jax.ShapeDtypeStruct((count // 2, rows, columns), BF16))
            targets = [to, (kept, None)]
            if kind == "fresh":
                scratch += [pltpu.VMEM((count, rows, columns), BF16)] * 2
        plan.append((kind, keep, got, at, rows, bit, inner, count, targets))
        if bit is not None:
            m.at = sizes[bit]
            sizes[bit] += size
        m.fresh = False
    if scratch:
        scratch.append(pltpu.SemaphoreType.DMA((len(scratch),)))
    shapes = [jax.ShapeDtypeStruct((sizes[b], columns), BF16) for b in bits] + shapes
    out = pl.pallas_call(
        functools.partial(relay_kernel, plan=plan, inputs=len(arrays), outputs=len(shapes)),
        in_specs=[pl.BlockSpec(memory_space=pltpu.SMEM)] + places,
        out_specs=[vmem] * len(shapes),
        out_shape=shapes,
        scratch_shapes=scratch,
        compiler_params=params(),
        cost_estimate=BRIEF,
    )(me, *arrays)
    for m, kept in zip(moving, keeps, strict=True):
        m.keep = out[kept]
    return dict(zip(bits, out))


class Sums:
    def __init__(self, me):
        self.me, self.moving, self.going = me, [], {}

    def step(self, *joining):
        came = {bit: swap(send, "wide", bit) for bit, send in self.going.items()}
        going = [m for m in self.moving if m.order]
        for m in going:
            bit = m.order.pop(0)
            m.got = came[bit]
            if isinstance(m, Rider):
                m.done.append(bit)
        self.moving += joining
        self.going = relay(self.me, going + list(joining))

    def arrays(self):
        return tuple(self.going.values()) + tuple(m.keep for m in self.moving)

    def put(self, arrays):
        count = len(self.going)
        self.going = dict(zip(self.going, arrays[:count], strict=True))
        for m, kept in zip(self.moving, arrays[count:], strict=True):
            m.keep = kept


def tie(values, moving):
    out = lax.optimization_barrier((tuple(values), tuple(m.arrays() for m in moving)))
    for one, kept in zip(moving, out[1], strict=True):
        one.put(kept)
    return out[0]


def local(
    x_src,
    cond,
    lengths,
    bucket,
    w_mod,
    b_mod,
    w_qkv,
    b_qv,
    w_proj,
    b_proj,
    w_fc1,
    b_fc1,
    w_fc2,
    b_fc2,
    grad_out,
):
    wide = lax.axis_size("wide")
    halves = lax.axis_size("narrow")
    devices = wide * halves
    group = lax.axis_index("wide")
    half = lax.axis_index("narrow")
    rows, feat = x_src.shape
    hidden = w_fc1.shape[1]
    places = lengths.shape[0] // halves
    slots = places // wide
    blocks = rows // BLK
    per_block = BLK // wide
    tiled = per_block % TILE == 0

    split = regroup if tiled else regroup_any
    send, scond, seg, src, cidx = split(x_src, cond, lengths, bucket, jnp.stack([group, half]), wide)
    exchange = functools.partial(
        lax.all_to_all, axis_name="wide", split_axis=0, concat_axis=0, tiled=True
    )
    came = exchange(send)
    came_cond = exchange(scond.reshape(wide, slots, feat // wide))
    cond_in = came_cond.transpose(1, 0, 2).reshape(slots, feat)
    x_view = came.reshape(wide, blocks, per_block, feat)
    if not tiled:
        x_view = x_view.transpose(1, 0, 2, 3).reshape(1, blocks, BLK, feat)

    act_low = jax.nn.silu(cond_in.astype(F32)).astype(BF16)
    modulate = jnp.dot(act_low, w_mod, preferred_element_type=F32) + b_mod.astype(F32)
    slot_ids = jnp.arange(slots, dtype=jnp.int32)
    in_slot = seg[:, None] == slot_ids[None, :]
    mod_blocks = jnp.sum(
        jnp.where(in_slot[:, :, None], modulate[None], 0.0), axis=1
    ).reshape(blocks, 6, feat)

    dy = (
        grad_out.reshape(blocks, per_block, wide, feat)
        .transpose(0, 2, 1, 3)
        .reshape(rows, feat)
    )
    gate_two = mod_blocks[:, 5:6, :]
    df = (
        (gate_two * dy.reshape(blocks, BLK, feat).astype(F32)).astype(BF16).reshape(rows, feat)
    )
    grad_b_fc2 = jnp.sum(df.astype(F32), axis=0)
    dg = dot(df, w_fc2, 1, 1)
    w_qkv_t = w_qkv.T
    bias_qkv = jnp.concatenate(
        [b_qv[:feat].astype(F32), jnp.zeros((feat,), F32), b_qv[feat:].astype(F32)]
    ).reshape(3 * feat, 1)

    qkv_t, a1_t = qkv_forward(x_view, mod_blocks, w_qkv_t, bias_qkv)
    o_t, lse = attend(seg, qkv_t)
    attn, x1, a2, a2_t = proj_forward(
        o_t, w_proj, b_proj.astype(F32).reshape(1, feat), x_view, mod_blocks
    )
    own, place = half.reshape(1), group.reshape(1)
    part = feat // devices
    halved = Halves(wide, part)
    both = ("wide", "narrow")
    orders = chain_orders(wide)
    near, far = bits_of(wide)[:3], bits_of(wide)[3:]
    sums = Sums(place)

    def shares(grad, got, cuts, ways):
        return [
            Part(grad[1], got, a, b - a, way)
            for a, b, way in zip(cuts[:-1], cuts[1:], ways, strict=True)
        ]

    def thirds(rows_of):
        third = -(-rows_of // 3 // TILE) * TILE
        return [0, third, min(2 * third, rows_of - TILE), rows_of]

    f, da2, grad_b_fc1, d_fc1, d_fc2 = mlp(
        own, a2, a2_t, df, dg, w_fc1, w_fc2, b_fc1.astype(F32).reshape(1, hidden), halved
    )

    if halved.split:
        fc2_got, fc1_got = swap(d_fc2[0], "narrow", 1), swap(d_fc1[0], "narrow", 1)
    y, dx1, do_t, grad_b_proj, two, d_proj = middle(
        own, seg, act_low, f, b_fc2.astype(F32).reshape(1, feat), x1, attn, dy, da2, mod_blocks, o_t,
        w_proj, halved,
    )
    y_dest = (
        y.reshape(blocks, wide, per_block, feat).transpose(0, 2, 1, 3).reshape(rows, feat)
    )
    pieces, row_sums, head = [], [], 0

    def attention(counts):
        nonlocal head
        for count in counts:
            piece, piece_sums = attend_back(
                seg, qkv_t, o_t, do_t, lse, first=head, count=count
            )
            pieces.append(piece)
            row_sums.append(piece_sums[:, 0])
            head += count

    def bias_rows():
        of_qv = jnp.concatenate(row_sums, axis=1)
        rows_of = [grad_b_fc1[0], grad_b_fc2, grad_b_proj[0], of_qv[0], of_qv[1]]
        return jnp.concatenate(rows_of).reshape(2 * slots, feat)

    ride_order = far + near[2:] + near[:2]
    if halved.split:
        proj_got = swap(d_proj[0], "narrow", 1)
        third = (d_fc2[1].shape[1] + d_fc1[1].shape[1] + part) // 3 // TILE * TILE
        fc2_parts = shares(d_fc2, fc2_got, [0, third, d_fc2[1].shape[1]], [orders[0], orders[2]])
        fc1_parts = shares(d_fc1, fc1_got, [0, third, d_fc1[1].shape[1]], [orders[1], orders[2]])
        proj_parts = shares(d_proj, proj_got, [0, part], orders[2:])
        two = Rider(two, ride_order)
        sums.step(*fc2_parts, *fc1_parts, *proj_parts, two)
        for counts in ((4, 4, 2), (4,), (2,)):
            (do_t, *pieces) = tie((do_t, *pieces), [sums])
            attention(counts)
            sums.step()
        (dx1, a1_t, *pieces) = tie((dx1, a1_t, *pieces), [sums])
    else:
        attention((4, 4, 4, 4))
    d_qkv = qkv_grad(own, a1_t, pieces, halved)
    if halved.split:
        qkv_got = swap(d_qkv[0], "narrow", 1)
    drows, one = rows_back(seg, pieces, w_qkv_t, x_view, dx1, mod_blocks, bias_rows())
    if halved.split:
        sums.step()
        (drows,) = tie((drows,), [sums])
    back = drows
    if not tiled:
        back = back.reshape(blocks, wide, per_block, feat).transpose(1, 0, 2, 3)
    back = exchange(back.reshape(wide, rows // wide, feat))
    one_all = lax.all_gather(one, both, axis=0, tiled=True)
    if halved.split:
        flat = near[:2] + near[2:] + far
        turned = near[:2][::-1] + near[2:] + far
        qkv_parts = shares(
            d_qkv, qkv_got, [0, part, 2 * part, 2 * part + part // 2, 3 * part], [flat, turned, flat, turned]
        )
        sums = Sums(place)
        sums.step(*qkv_parts)
        tie((), [sums])
        sums.step()
        tie((), [sums])
        sums.step()
        (back,) = tie((back,), [sums])
        sums.step()
        (one_all,) = tie((one_all,), [sums])
        while sums.going:
            sums.step()
        two_all = two.keep.reshape(wide, -1, feat)
        two_all = jnp.concatenate([two_all, swap(two_all, "narrow", 1)], axis=0)
        differs = jnp.asarray(two.differences(), jnp.int32)
        device_of = jnp.concatenate(
            [(differs ^ group) * halves + half, (differs ^ group) * halves + 1 - half]
        )
        grad_w_fc2 = jnp.concatenate([p.keep for p in fc2_parts], axis=0)
        grad_w_fc1 = jnp.concatenate([p.keep for p in fc1_parts], axis=0)
        grad_w_fc1 = (
            grad_w_fc1.reshape(hidden // feat, part, feat).transpose(1, 0, 2).reshape(part, hidden)
        )
        (grad_w_proj,) = (p.keep for p in proj_parts)

        kept = [p.keep for p in qkv_parts]
        grad_w_qkv = jnp.concatenate(kept[:2] + [jnp.concatenate(kept[2:], axis=0)], axis=1)
    else:
        two_all = lax.all_gather(two, both, axis=0, tiled=True)
        device_of = jnp.arange(devices, dtype=jnp.int32)

        def scattered(full):
            return lax.psum_scatter(full, both, scatter_dimension=0, tiled=True).astype(F32)

        grad_w_fc2 = scattered(d_fc2[0])
        grad_w_fc1 = scattered(d_fc1[0].transpose(1, 0, 2).reshape(feat, hidden))
        grad_w_proj = scattered(d_proj[0])
        grad_w_qkv = scattered(d_qkv[0].transpose(1, 0, 2).reshape(feat, 3 * feat))
    merge = restore if tiled else restore_any
    dx_src = merge(src, back.reshape(rows, feat))

    me = group * halves + half
    bucket_of, slot_of = jnp.maximum(cidx, 0) // slots, jnp.maximum(cidx, 0) % slots
    if halved.split:
        spot = two.place(bucket_of ^ group) * 2 * slots + slot_of
    else:
        spot = (bucket_of * halves + half) * 2 * slots + slot_of
    grad_w_mod, grad_b_mod, dcond, biases = mod_grad(
        group, me, device_of, jnp.where(cidx >= 0, spot, -1), one_all, two_all, w_mod, cond, part, slots
    )
    grad_b_mod = lax.dynamic_slice_in_dim(grad_b_mod[0], me * 6 * part, 6 * part)

    def own_part(first, count):
        rows_of = biases[first : first + count].reshape(-1)
        share = rows_of.shape[0] // devices
        return lax.dynamic_slice_in_dim(rows_of, me * share, share)

    fc1_lines = hidden // feat
    s_fc1, s_fc2, s_proj = own_part(0, fc1_lines), own_part(fc1_lines, 1), own_part(fc1_lines + 1, 1)
    s_qv = own_part(fc1_lines + 2, 2)
    return (
        y_dest,
        dx_src,
        dcond,
        grad_w_mod,
        grad_b_mod,
        grad_w_qkv,
        s_qv,
        grad_w_proj,
        s_proj,
        grad_w_fc1,
        s_fc1,
        grad_w_fc2,
        s_fc2,
    )


def solution(mesh):
    both = ("wide", "narrow")
    placed = (P("narrow", "wide"), P("narrow", "wide")) + (P(),) * 12 + (P(both, None),)
    matrix, vector = P(both, None), P(both)
    return jax.shard_map(
        local,
        mesh=mesh,
        in_specs=placed,
        out_specs=(
            matrix,
            P("narrow", "wide"),
            P("narrow", "wide"),
            matrix,
            vector,
            matrix,
            vector,
            matrix,
            vector,
            matrix,
            vector,
            matrix,
            vector,
        ),
        check_vma=False,
    )
```

```python
import functools
import math

import jax
import jax.numpy as jnp
from jax import lax
from jax.experimental import pallas as pl
from jax.experimental.pallas import tpu as pltpu
from jax.sharding import PartitionSpec as P

HEADS = 16
HEAD_DIM = 64
EPS = 1e-06
MASKED = -1000000000.0
LOG2E = 1.4426950408889634
BLK = 256
TILE = 16
VMEM_LIMIT = 58 * 2**20
BRIEF = pl.CostEstimate(flops=1, bytes_accessed=1, transcendentals=0)
BF16 = jnp.bfloat16
F32 = jnp.float32


def params(**more):
    return pltpu.CompilerParams(vmem_limit_bytes=VMEM_LIMIT, **more)


def dot(left, right, left_dim, right_dim):
    return lax.dot_general(
        left, right, (((left_dim,), (right_dim,)), ((), ())), preferred_element_type=F32
    )


def norm_parts(values):
    centre = values - jnp.mean(values, axis=1, keepdims=True)
    spread = jnp.mean(centre * centre, axis=1, keepdims=True)
    inverse = lax.rsqrt(spread + EPS)
    return centre * inverse, inverse


def norm_back(grad, normed, inverse):
    return (
        grad
        - jnp.mean(grad, axis=1, keepdims=True)
        - normed * jnp.mean(grad * normed, axis=1, keepdims=True)
    ) * inverse


def each_place(len_ref, buck_ref, base, count, off_ref, slot_ref, wide, visit):
    for i in range(wide):
        off_ref[i] = 0
        slot_ref[i] = 0

    def place(j, offset):
        units = len_ref[base + j] // wide
        b = buck_ref[base + j]

        @pl.when(units > 0)
        def _():
            start = off_ref[b]
            slot = slot_ref[b]
            off_ref[b] = start + units
            slot_ref[b] = slot + 1
            visit(j, b, units, offset, start, slot)

        return offset + units

    lax.fori_loop(0, count, place, 0)


def regroup_rows_kernel(
    len_ref, buck_ref, me_ref, x_ref, send_ref, src_ref, off_ref, slot_ref, *, wide, places
):
    cells = send_ref.shape[1]
    send_ref[...] = jnp.zeros_like(send_ref)

    @pl.loop(0, src_ref.shape[0])
    def _(i):
        src_ref[i] = -1

    def visit(j, b, units, offset, start, slot):
        @pl.loop(0, units // TILE)
        def _(t):
            a = pl.multiple_of(offset + t * TILE, TILE)
            c = pl.multiple_of(start + t * TILE, TILE)
            send_ref[b, pl.ds(c, TILE), :] = x_ref[pl.ds(a, TILE), :]
            src_ref[a // TILE] = (b * cells + c) // TILE

    each_place(len_ref, buck_ref, me_ref[1] * places, places, off_ref, slot_ref, wide, visit)


def regroup_cond_kernel(
    len_ref, buck_ref, me_ref, cond_ref, scond_ref, seg_ref, cidx_ref,
    off_ref, slot_ref, cond_in, cond_out, *, wide, slots,
):
    cond_out[...] = jnp.zeros_like(cond_out)
    cond_in[...] = cond_ref[...].astype(F32)
    for i in range(seg_ref.shape[0]):
        seg_ref[i] = -1

    @pl.loop(0, cidx_ref.shape[0])
    def _(j):
        cidx_ref[j] = -1

    def visit(j, b, units, offset, start, slot):
        cidx_ref[j] = b * slots + slot
        cond_out[pl.ds(b * slots + slot, 1), :] = cond_in[pl.ds(j, 1), :]

        @pl.when(b == me_ref[0])
        def _():
            @pl.loop(0, units * wide // BLK)
            def _(t):
                seg_ref[start * wide // BLK + t] = slot

    places = cidx_ref.shape[0]
    each_place(len_ref, buck_ref, me_ref[1] * places, places, off_ref, slot_ref, wide, visit)
    scond_ref[...] = cond_out[...].astype(BF16)


def regroup(x_src, cond, lens, buck, me, wide):
    rows, feat = x_src.shape
    places, part = cond.shape
    slots = places // wide
    smem = pl.BlockSpec(memory_space=pltpu.SMEM)
    vmem = pl.BlockSpec(memory_space=pltpu.VMEM)
    counters = [pltpu.SMEM((wide,), jnp.int32), pltpu.SMEM((wide,), jnp.int32)]
    scond, seg, cidx = pl.pallas_call(
        functools.partial(regroup_cond_kernel, wide=wide, slots=slots),
        in_specs=[smem, smem, smem, vmem],
        out_specs=[vmem, smem, smem],
        out_shape=[
            jax.ShapeDtypeStruct((places, part), BF16),
            jax.ShapeDtypeStruct((rows // BLK,), jnp.int32),
            jax.ShapeDtypeStruct((places,), jnp.int32),
        ],
        scratch_shapes=counters + [pltpu.VMEM((places, part), F32), pltpu.VMEM((places, part), F32)],
        compiler_params=params(),
        cost_estimate=BRIEF,
    )(lens, buck, me, cond)
    send, src = pl.pallas_call(
        functools.partial(regroup_rows_kernel, wide=wide, places=places),
        in_specs=[smem, smem, smem, vmem],
        out_specs=[vmem, smem],
        out_shape=[
            jax.ShapeDtypeStruct((wide, rows // wide, feat), BF16),
            jax.ShapeDtypeStruct((rows // TILE,), jnp.int32),
        ],
        scratch_shapes=counters,
        compiler_params=params(),
        cost_estimate=BRIEF,
    )(lens, buck, me, x_src)
    return send, scond, seg, src, cidx


def restore_kernel(src_ref, back_ref, dx_ref):
    @pl.loop(0, src_ref.shape[0])
    def _(i):
        at = src_ref[i]
        rows = back_ref[pl.ds(pl.multiple_of(jnp.maximum(at, 0) * TILE, TILE), TILE), :]
        dx_ref[pl.ds(pl.multiple_of(i * TILE, TILE), TILE), :] = jnp.where(
            at >= 0, rows, jnp.zeros_like(rows)
        )


def restore(src, back):
    vmem = pl.BlockSpec(memory_space=pltpu.VMEM)
    return pl.pallas_call(
        restore_kernel,
        in_specs=[pl.BlockSpec(memory_space=pltpu.SMEM), vmem],
        out_specs=vmem,
        out_shape=jax.ShapeDtypeStruct(back.shape, BF16),
        compiler_params=params(),
        cost_estimate=BRIEF,
    )(src, back)


def regroup_any(x_src, cond, lens, buck, me, wide):
    rows, feat = x_src.shape
    places = cond.shape[0]
    lens = lax.dynamic_slice_in_dim(lens, me[1] * places, places)
    buck = lax.dynamic_slice_in_dim(buck, me[1] * places, places)
    slots, cells = places // wide, rows // wide
    units = lens // wide
    order = jnp.arange(places, dtype=jnp.int32)
    earlier = (order[:, None] < order[None, :]) & (buck[:, None] == buck[None, :])
    live = (lens > 0).astype(jnp.int32)
    offset = jnp.cumsum(units) - units
    start = jnp.sum(jnp.where(earlier, units[:, None], 0), axis=0)
    slot = jnp.sum(jnp.where(earlier, live[:, None], 0), axis=0)
    cell = jnp.arange(cells, dtype=jnp.int32)[None, :, None]
    to_target = (buck[None, :] == jnp.arange(wide, dtype=jnp.int32)[:, None]) & (live[None, :] > 0)
    hit = (
        to_target[:, None, :]
        & (cell >= start[None, None, :])
        & (cell < (start + units)[None, None, :])
    ).astype(jnp.int32)
    valid = jnp.sum(hit, axis=2)
    source = jnp.sum(hit * (offset - start)[None, None, :], axis=2) + cell[:, :, 0]
    source = jnp.where(valid > 0, source, 0)
    picked = jnp.take(x_src, source.reshape(-1), axis=0).reshape(wide, cells, feat)
    send = jnp.where(valid[:, :, None] > 0, picked, jnp.zeros((), BF16))
    cond_hit = to_target[:, None, :] & (
        slot[None, None, :] == jnp.arange(slots, dtype=jnp.int32)[None, :, None]
    )
    scond = jnp.einsum("wqs,sf->wqf", cond_hit.astype(BF16), cond, preferred_element_type=F32)
    scond = scond.astype(BF16).reshape(cond.shape)
    first = jnp.arange(rows // BLK, dtype=jnp.int32)[:, None] * BLK
    mine = (
        ((buck == me[0]) & (live > 0))[None, :]
        & (first >= (start * wide)[None, :])
        & (first < ((start + units) * wide)[None, :])
    )
    seg = jnp.sum(jnp.where(mine, slot[None, :] + 1, 0), axis=1) - 1
    spot = jnp.arange(rows, dtype=jnp.int32)[:, None]
    inside = (live[None, :] > 0) & (spot >= offset[None, :]) & (spot < (offset + units)[None, :])
    src = jnp.sum(jnp.where(inside, (buck * cells + start - offset)[None, :] + spot + 1, 0), axis=1)
    cidx = jnp.where(live > 0, buck * slots + slot, -1)
    return send, scond, seg.astype(jnp.int32), src - 1, cidx


def restore_any(src, back):
    dx = jnp.take(back, jnp.maximum(src, 0), axis=0)
    return jnp.where(src[:, None] >= 0, dx, jnp.zeros((), BF16))


def qkv_kernel(x_ref, mod_ref, w_ref, b_ref, q_ref, a_ref):
    feat = x_ref.shape[-1]
    x = x_ref[...].reshape(BLK, feat).astype(F32)
    normed, _ = norm_parts(x)
    a1 = (normed * (1.0 + mod_ref[0, 1:2, :]) + mod_ref[0, 0:1, :]).astype(BF16)
    a1_t = a1.T
    a_ref[...] = a1_t
    for i in range(3):
        part = slice(i * feat, (i + 1) * feat)
        q_ref[part, :] = (dot(w_ref[part, :], a1_t, 1, 0) + b_ref[part, :]).astype(BF16)


def row_spec(view):
    return pl.BlockSpec((view[0], 1, view[2], view[3]), lambda k: (0, k, 0, 0))


def whole(*shape):
    return pl.BlockSpec(shape, lambda k: (0,) * len(shape))


def qkv_forward(x_view, mod_blocks, w_t, bias):
    feat = x_view.shape[-1]
    blocks = x_view.shape[1]
    return pl.pallas_call(
        qkv_kernel,
        grid=(blocks,),
        in_specs=[
            row_spec(x_view.shape),
            pl.BlockSpec((1, 6, feat), lambda k: (k, 0, 0)),
            whole(3 * feat, feat),
            whole(3 * feat, 1),
        ],
        out_specs=[
            pl.BlockSpec((3 * feat, BLK), lambda k: (0, k)),
            pl.BlockSpec((feat, BLK), lambda k: (0, k)),
        ],
        out_shape=[
            jax.ShapeDtypeStruct((3 * feat, blocks * BLK), BF16),
            jax.ShapeDtypeStruct((feat, blocks * BLK), BF16),
        ],
        compiler_params=params(),
        cost_estimate=BRIEF,
    )(x_view, mod_blocks, w_t, bias)


def masks(seg_ref, query_block, blocks):
    base = LOG2E / math.sqrt(HEAD_DIM)
    same = [seg_ref[query_block] == seg_ref[kb] for kb in range(blocks)]
    scales = [jnp.where(s, base, 0.0) for s in same]
    shifts = [jnp.where(s, 0.0, MASKED * LOG2E) for s in same]
    return scales, shifts


def attend_kernel(seg_ref, q_ref, k_ref, v_ref, o_ref, lse_ref, *, blocks, heads):
    units = [(h, qb) for h in range(heads) for qb in range(blocks)]
    keys = [k_ref[h * HEAD_DIM : (h + 1) * HEAD_DIM, :].T for h in range(heads)]

    def spans(h, qb):
        return slice(h * HEAD_DIM, (h + 1) * HEAD_DIM), slice(qb * BLK, (qb + 1) * BLK)

    def scores_of(h, qb):
        q_t = q_ref[spans(h, qb)]
        return [dot(keys[h][kb * BLK : (kb + 1) * BLK], q_t, 1, 0) for kb in range(blocks)]

    def finish(h, qb, probs, total, top):
        hs, qs = spans(h, qb)
        out = dot(v_ref[hs, :], probs, 1, 0)
        o_ref[hs, qs] = (out / total).astype(BF16)
        lse_ref[h, :, qs] = top + jnp.log2(total)

    ahead, behind = scores_of(*units[0]), None
    for i, (h, qb) in enumerate(units):
        scores, ahead = ahead, scores_of(*units[i + 1]) if i + 1 < len(units) else None
        scales, shifts = masks(seg_ref, qb, blocks)
        top = None
        for kb in range(blocks):
            peak = jnp.max(scores[kb], axis=0, keepdims=True) * scales[kb] + shifts[kb]
            top = peak if top is None else jnp.maximum(top, peak)
        if behind is not None:
            finish(*behind)
        total = jnp.zeros((1, BLK), F32)
        parts = []
        for kb in range(blocks):
            expo = jnp.exp2(scores[kb] * scales[kb] - (top - shifts[kb]))
            total = total + jnp.sum(expo, axis=0, keepdims=True)
            parts.append(expo.astype(BF16))
        behind = (h, qb, jnp.concatenate(parts, axis=0), total, top)
    finish(*behind)


def attend(seg, qkv_t, heads=4):
    feat3, rows = qkv_t.shape
    feat = feat3 // 3
    span = heads * HEAD_DIM
    groups = feat // span
    return pl.pallas_call(
        functools.partial(attend_kernel, blocks=rows // BLK, heads=heads),
        grid_spec=pltpu.PrefetchScalarGridSpec(
            num_scalar_prefetch=1,
            grid=(groups,),
            in_specs=[
                pl.BlockSpec((span, rows), lambda g, s: (g, 0)),
                pl.BlockSpec((span, rows), lambda g, s: (groups + g, 0)),
                pl.BlockSpec((span, rows), lambda g, s: (2 * groups + g, 0)),
            ],
            out_specs=[
                pl.BlockSpec((span, rows), lambda g, s: (g, 0)),
                pl.BlockSpec((heads, 1, rows), lambda g, s: (g, 0, 0)),
            ],
        ),
        out_shape=[
            jax.ShapeDtypeStruct((feat, rows), BF16),
            jax.ShapeDtypeStruct((feat // HEAD_DIM, 1, rows), F32),
        ],
        compiler_params=params(),
        cost_estimate=BRIEF,
    )(seg, qkv_t, qkv_t, qkv_t)


def attend_back_kernel(
    seg_ref, q_ref, k_ref, v_ref, o_ref, do_ref, lse_ref, out_ref, sums_ref, *, blocks, heads
):
    scale = 1.0 / math.sqrt(HEAD_DIM)
    units = [(h, qb) for h in range(heads) for qb in range(blocks)]
    keys = [k_ref[h * HEAD_DIM : (h + 1) * HEAD_DIM, :].T for h in range(heads)]
    values = [v_ref[h * HEAD_DIM : (h + 1) * HEAD_DIM, :].T for h in range(heads)]

    def spans(h, qb):
        return slice(h * HEAD_DIM, (h + 1) * HEAD_DIM), slice(qb * BLK, (qb + 1) * BLK)

    def products(h, qb):
        q_t, do_t = q_ref[spans(h, qb)], do_ref[spans(h, qb)]
        cuts = [slice(kb * BLK, (kb + 1) * BLK) for kb in range(blocks)]
        return [(dot(keys[h][c], q_t, 1, 0), dot(values[h][c], do_t, 1, 0)) for c in cuts]

    ahead = products(*units[0])
    grad_k = grad_v = inner = None
    for i, (h, qb) in enumerate(units):
        present, ahead = ahead, products(*units[i + 1]) if i + 1 < len(units) else None
        hs, qs = spans(h, qb)
        if qb == 0:
            inner = jnp.sum(
                o_ref[hs, :].astype(F32) * do_ref[hs, :].astype(F32), axis=0, keepdims=True
            )
        scales, shifts = masks(seg_ref, qb, blocks)
        probs, grads = [], []
        for kb, (score, grad_p) in enumerate(present):
            prob = jnp.exp2(score * scales[kb] - (lse_ref[h, :, qs] - shifts[kb]))
            probs.append(prob.astype(BF16))
            grads.append((prob * (grad_p - inner[:, qs])).astype(BF16))
        probs = jnp.concatenate(probs, axis=0)
        grads = jnp.concatenate(grads, axis=0)
        out_ref[0, hs, qs] = (dot(k_ref[hs, :], grads, 1, 0) * scale).astype(BF16)
        more_k, more_v = dot(q_ref[hs, qs], grads, 1, 1), dot(do_ref[hs, qs], probs, 1, 1)
        grad_k = more_k if qb == 0 else grad_k + more_k
        grad_v = more_v if qb == 0 else grad_v + more_v
        if qb == blocks - 1:
            out_ref[1, hs, :] = (grad_k * scale).astype(BF16)
            out_ref[2, hs, :] = grad_v.astype(BF16)
    ones = jnp.ones((8, out_ref.shape[2]), BF16)
    sums_ref[0] = dot(ones, out_ref[0], 1, 1)
    sums_ref[1] = dot(ones, out_ref[2], 1, 1)


def attend_back(seg, qkv_t, o_t, do_t, lse, first, count, heads=2):
    feat3, rows = qkv_t.shape
    feat = feat3 // 3
    span = heads * HEAD_DIM
    groups = feat // span
    at = first // heads
    return pl.pallas_call(
        functools.partial(attend_back_kernel, blocks=rows // BLK, heads=heads),
        grid_spec=pltpu.PrefetchScalarGridSpec(
            num_scalar_prefetch=1,
            grid=(count // heads,),
            in_specs=[
                pl.BlockSpec((span, rows), lambda g, s: (at + g, 0)),
                pl.BlockSpec((span, rows), lambda g, s: (groups + at + g, 0)),
                pl.BlockSpec((span, rows), lambda g, s: (2 * groups + at + g, 0)),
                pl.BlockSpec((span, rows), lambda g, s: (at + g, 0)),
                pl.BlockSpec((span, rows), lambda g, s: (at + g, 0)),
                pl.BlockSpec((heads, 1, rows), lambda g, s: (at + g, 0, 0)),
            ],
            out_specs=[
                pl.BlockSpec((3, span, rows), lambda g, s: (0, g, 0)),
                pl.BlockSpec((2, 8, span), lambda g, s: (0, 0, g)),
            ],
        ),
        out_shape=[
            jax.ShapeDtypeStruct((3, count * HEAD_DIM, rows), BF16),
            jax.ShapeDtypeStruct((2, 8, count * HEAD_DIM), F32),
        ],
        compiler_params=params(),
        cost_estimate=BRIEF,
    )(seg, qkv_t, qkv_t, qkv_t, o_t, do_t, lse)


class Halves:
    def __init__(self, wide, part, split=None):
        self.wide, self.part = wide, part
        self.split = part % TILE == 0 if split is None else split

    def shapes(self, between, columns):
        if self.split:
            shape = (self.wide,) + between + (self.part, columns)
            return [jax.ShapeDtypeStruct(shape, BF16)] * 2
        return [jax.ShapeDtypeStruct(between + (2 * self.wide * self.part, columns), BF16)]

    def specs(self, between, columns, index):
        ones = (1,) * between
        if self.split:
            return [
                pl.BlockSpec(
                    (self.wide,) + ones + (self.part, columns),
                    lambda *g: (0,) + index(*g)[:-1] + (0, index(*g)[-1]),
                )
            ] * 2
        return [
            pl.BlockSpec(
                ones + (2 * self.wide * self.part, columns),
                lambda *g: index(*g)[:-1] + (0, index(*g)[-1]),
            )
        ]

    def store(self, half, value, refs):
        if not self.split:
            refs[0][...] = value.astype(BF16).reshape(refs[0].shape)
            return
        value = value.reshape(value.shape[0] // (2 * self.part), 2, self.part, value.shape[1])
        even, odd = value[:, 0], value[:, 1]
        folds = refs[0].shape[-1] // value.shape[-1]
        if folds > 1:
            even, odd = (
                jnp.concatenate(jnp.split(half_value, folds, axis=1), axis=2) for half_value in (even, odd)
            )
        refs[0][...] = jnp.where(half == 0, odd, even).astype(BF16).reshape(refs[0].shape)
        refs[1][...] = jnp.where(half == 0, even, odd).astype(BF16).reshape(refs[1].shape)

    def finish(self, arrays):
        if self.split:
            return [a.reshape(self.wide, -1, a.shape[-1]) for a in arrays]
        return arrays


def qkv_grad_kernel(half_ref, a_ref, *refs, pieces, halves):
    ins, outs = refs[:pieces], refs[pieces:]
    value = jnp.concatenate([dot(a_ref[...], r[0], 1, 1) for r in ins], axis=1)
    halves.store(half_ref[0], value, outs)


def qkv_grad(half, a1_t, dqkv, halves):
    feat, rows = a1_t.shape
    columns = sum(d.shape[1] for d in dqkv)
    folds = feat // columns if halves.split else 1
    packed = Halves(halves.wide, halves.part // folds, halves.split)
    packed_columns = folds * columns
    out = pl.pallas_call(
        functools.partial(qkv_grad_kernel, pieces=len(dqkv), halves=halves),
        grid=(3,),
        in_specs=[pl.BlockSpec(memory_space=pltpu.SMEM), whole(feat, rows)]
        + [pl.BlockSpec((1, d.shape[1], rows), lambda i: (i, 0, 0)) for d in dqkv],
        out_specs=packed.specs(1, packed_columns, lambda i: (i, 0)),
        out_shape=packed.shapes((3,), packed_columns),
        compiler_params=params(),
        cost_estimate=BRIEF,
    )(half, a1_t, *dqkv)
    return halves.finish(out)


def proj_kernel(o_ref, w_ref, b_ref, x_ref, mod_ref, attn_ref, x1_ref, a_ref, at_ref):
    feat = x_ref.shape[-1]
    attn = dot(o_ref[...], w_ref[...], 0, 0) + b_ref[...]
    attn_ref[...] = attn
    x1 = x_ref[...].reshape(BLK, feat).astype(F32) + mod_ref[0, 2:3, :] * attn
    x1_ref[...] = x1
    normed, _ = norm_parts(x1)
    a2 = (normed * (1.0 + mod_ref[0, 4:5, :]) + mod_ref[0, 3:4, :]).astype(BF16)
    a_ref[...] = a2
    at_ref[...] = a2.T


def proj_forward(o_t, w_proj, b_proj, x_view, mod_blocks):
    feat = x_view.shape[-1]
    blocks = x_view.shape[1]
    rows = blocks * BLK
    by_row = pl.BlockSpec((BLK, feat), lambda k: (k, 0))
    by_column = pl.BlockSpec((feat, BLK), lambda k: (0, k))
    return pl.pallas_call(
        proj_kernel,
        grid=(blocks,),
        in_specs=[
            by_column,
            whole(feat, feat),
            whole(1, feat),
            row_spec(x_view.shape),
            pl.BlockSpec((1, 6, feat), lambda k: (k, 0, 0)),
        ],
        out_specs=[by_row, by_row, by_row, by_column],
        out_shape=[
            jax.ShapeDtypeStruct((rows, feat), F32),
            jax.ShapeDtypeStruct((rows, feat), F32),
            jax.ShapeDtypeStruct((rows, feat), BF16),
            jax.ShapeDtypeStruct((feat, rows), BF16),
        ],
        compiler_params=params(),
        cost_estimate=BRIEF,
    )(o_t, w_proj, b_proj, x_view, mod_blocks)


def gelu_both(u):
    c = math.sqrt(2.0 / math.pi)
    square = u * u
    half = 0.5 + 0.5 * jnp.tanh(u * (c + (c * 0.044715) * square))
    g = u * half
    return g, half + (g - g * half) * (2.0 * c + (6.0 * c * 0.044715) * square)


def mlp_kernel(
    half_ref, a_ref, at_ref, df_ref, dg_ref, w1_ref, w2_ref, b1_ref, *refs, first, second
):
    f_ref, da_ref, db_ref = refs[:3]
    g_ref, du_ref = refs[-2:]
    outs = refs[3:-2]
    outs_one, outs_two = outs[: len(outs) // 2], outs[len(outs) // 2 :]
    step = pl.program_id(0)
    rows = a_ref.shape[0]

    @pl.when(step == 0)
    def _():
        f_ref[...] = jnp.zeros_like(f_ref)
        da_ref[...] = jnp.zeros_like(da_ref)

    w1, w2 = w1_ref[...], w2_ref[...]
    bias = jnp.zeros((1, w1.shape[1]), F32)
    cuts = [slice(r, r + BLK) for r in range(0, rows, BLK)]
    u = dot(a_ref[cuts[0], :], w1, 1, 0)
    for r, rs in enumerate(cuts):
        later = dot(a_ref[cuts[r + 1], :], w1, 1, 0) if r + 1 < len(cuts) else None
        g, slope = gelu_both(u + b1_ref[...])
        du = dg_ref[rs, :] * slope
        bias = bias + jnp.sum(du, axis=0, keepdims=True)
        g_ref[rs, :] = g.astype(BF16)
        du_ref[rs, :] = du.astype(BF16)
        u = later
        for past in cuts[r - 1 : r] if r + 1 < len(cuts) else cuts[max(r - 1, 0) :]:
            f_ref[past, :] += dot(g_ref[past, :], w2, 1, 0)
            da_ref[past, :] += dot(du_ref[past, :], w1, 1, 1)
    db_ref[...] = bias
    first.store(half_ref[0], dot(at_ref[...], du_ref[...], 1, 0), outs_one)
    second.store(half_ref[0], dot(g_ref[...], df_ref[...], 0, 0), outs_two)


def mlp(half, a2, a2_t, df, dg, w1, w2, b1, halves, width=512):
    rows, feat = a2.shape
    hidden = w1.shape[1]
    per = feat // width
    wide = halves.wide
    part = hidden // (2 * wide)
    first = halves
    second = Halves(wide, part)
    second.split = halves.split
    one = pl.Buffered(1)

    def fixed(*shape):
        return pl.BlockSpec(shape, lambda j: (0,) * len(shape), pipeline_mode=one)

    if halves.split:
        two_specs = [pl.BlockSpec((width // (2 * part), part, feat), lambda j: (j, 0, 0))] * 2
        two_shapes = [jax.ShapeDtypeStruct((wide, part, feat), BF16)] * 2
    else:
        two_specs = [pl.BlockSpec((width, feat), lambda j: (j, 0))]
        two_shapes = [jax.ShapeDtypeStruct((hidden, feat), BF16)]
    out = pl.pallas_call(
        functools.partial(mlp_kernel, first=first, second=second),
        grid=(hidden // width,),
        in_specs=[
            pl.BlockSpec(memory_space=pltpu.SMEM),
            fixed(rows, feat),
            fixed(feat, rows),
            fixed(rows, feat),
            pl.BlockSpec((rows, width), lambda j: (0, j)),
            pl.BlockSpec((feat, width), lambda j: (0, j)),
            pl.BlockSpec((width, feat), lambda j: (j, 0)),
            pl.BlockSpec((1, width), lambda j: (0, j)),
        ],
        out_specs=[whole(rows, feat), whole(rows, feat), pl.BlockSpec((1, width), lambda j: (0, j))]
        + halves.specs(1, width, lambda j: (j // per, j % per))
        + two_specs,
        out_shape=[
            jax.ShapeDtypeStruct((rows, feat), F32),
            jax.ShapeDtypeStruct((rows, feat), F32),
            jax.ShapeDtypeStruct((1, hidden), F32),
        ]
        + halves.shapes((hidden // feat,), feat)
        + two_shapes,
        scratch_shapes=[pltpu.VMEM((rows, width), BF16), pltpu.VMEM((rows, width), BF16)],
        compiler_params=params(),
        cost_estimate=BRIEF,
    )(half, a2, a2_t, df, dg, w1, w2, b1)
    f, da2, bias = out[:3]
    rest = out[3:]
    count = len(rest) // 2
    return f, da2, bias, first.finish(rest[:count]), second.finish(rest[count:])


def to_slot(ref, slot, slots, terms):
    @pl.when(slot >= 0)
    def _():
        for i, term in enumerate(terms):
            ref[pl.ds(2 * slots * i + slot, 1), :] += jnp.sum(term, axis=0, keepdims=True)


def middle_kernel(
    half_ref, seg_ref, f_ref, b2_ref, x1_ref, attn_ref, dy_ref, da_ref, mod_ref, o_ref, w_ref, act_ref,
    y_ref, dx_ref, do_ref, db_ref, sums_ref, *rest, halves,
):
    k = pl.program_id(0)
    outs, acc_ref, slot_ref = rest[:-2], rest[-2], rest[-1]
    slots = act_ref.shape[0]

    @pl.when(k == 0)
    def _():
        acc_ref[...] = jnp.zeros_like(acc_ref)
        db_ref[...] = jnp.zeros_like(db_ref)
        slot_ref[...] = jnp.zeros_like(slot_ref)
        slot_ref[slots : 2 * slots, :] = act_ref[...].astype(F32)

    f = f_ref[...] + b2_ref[...]
    x1 = x1_ref[...]
    dy = dy_ref[...].astype(F32)
    y_ref[...] = (x1 + mod_ref[0, 5:6, :] * f).astype(BF16)
    normed, inverse = norm_parts(x1)
    da = da_ref[...]
    dx1 = dy + norm_back(da * (1.0 + mod_ref[0, 4:5, :]), normed, inverse)
    dx_ref[...] = dx1
    dattn = (mod_ref[0, 2:3, :] * dx1).astype(BF16)
    db_ref[...] += jnp.sum(dattn.astype(F32), axis=0, keepdims=True)
    to_slot(slot_ref, seg_ref[k], slots, [dx1 * attn_ref[...], da, da * normed, dy * f])
    do_ref[...] = dot(w_ref[...], dattn, 1, 1).astype(BF16)
    acc_ref[...] += dot(o_ref[...], dattn, 1, 0)

    @pl.when(k == pl.num_programs(0) - 1)
    def _():
        halves.store(half_ref[0], acc_ref[...], outs)
        sums_ref[0] = slot_ref[...].astype(BF16)


def middle(half, seg, act, f, b2, x1, attn, dy, da2, mod_blocks, o_t, w_proj, halves):
    rows, feat = x1.shape
    by_row = pl.BlockSpec((BLK, feat), lambda k: (k, 0))
    by_column = pl.BlockSpec((feat, BLK), lambda k: (0, k))
    blocks = rows // BLK
    slots = act.shape[0]
    out = pl.pallas_call(
        functools.partial(middle_kernel, halves=halves),
        grid=(blocks,),
        in_specs=[
            pl.BlockSpec(memory_space=pltpu.SMEM),
            pl.BlockSpec(memory_space=pltpu.SMEM),
            by_row, whole(1, feat), by_row, by_row, by_row, by_row,
            pl.BlockSpec((1, 6, feat), lambda k: (k, 0, 0)),
            by_column, whole(feat, feat), whole(slots, feat),
        ],
        out_specs=[
            by_row, by_row, by_column, whole(1, feat),
            whole(1, 8 * slots, feat),
        ] + halves.specs(0, feat, lambda k: (0,)),
        out_shape=[
            jax.ShapeDtypeStruct((rows, feat), BF16),
            jax.ShapeDtypeStruct((rows, feat), F32),
            jax.ShapeDtypeStruct((feat, rows), BF16),
            jax.ShapeDtypeStruct((1, feat), F32),
            jax.ShapeDtypeStruct((1, 8 * slots, feat), BF16),
        ]
        + halves.shapes((), feat),
        scratch_shapes=[pltpu.VMEM((feat, feat), F32), pltpu.VMEM((8 * slots, feat), F32)],
        compiler_params=params(),
        cost_estimate=BRIEF,
    )(half, seg, f, b2, x1, attn, dy, da2, mod_blocks, o_t, w_proj, act)
    return tuple(out[:5]) + (halves.finish(out[5:]),)


def rows_back_kernel(seg_ref, w_ref, x_ref, dx_ref, mod_ref, bias_ref, *refs):
    out_ref, sums_ref, slot_ref = refs[-3:]
    slots = bias_ref.shape[0] // 2

    @pl.when(pl.program_id(0) == 0)
    def _():
        slot_ref[...] = jnp.zeros_like(slot_ref)
        slot_ref[slots : 2 * slots, :] = bias_ref[:slots, :]
        slot_ref[3 * slots :, :] = bias_ref[slots:, :]

    feat = x_ref.shape[-1]
    da = None
    for i in range(3):
        at = i * feat
        for ref in refs[:-3]:
            more = dot(ref[i], w_ref[at : at + ref.shape[1], :], 0, 0)
            da = more if da is None else da + more
            at += ref.shape[1]
    normed, inverse = norm_parts(x_ref[...].reshape(BLK, feat).astype(F32))
    out = dx_ref[...] + norm_back(da * (1.0 + mod_ref[0, 1:2, :]), normed, inverse)
    out_ref[...] = out.astype(BF16).reshape(out_ref.shape)
    to_slot(slot_ref, seg_ref[pl.program_id(0)], slots, [da, da * normed])
    sums_ref[0] = slot_ref[...].astype(BF16)


def rows_back(seg, dqkv, w_t, x_view, dx1, mod_blocks, biases):
    rows, feat = dx1.shape
    blocks = rows // BLK
    return pl.pallas_call(
        rows_back_kernel,
        grid=(blocks,),
        in_specs=[
            pl.BlockSpec(memory_space=pltpu.SMEM),
            whole(3 * feat, feat),
            row_spec(x_view.shape),
            pl.BlockSpec((BLK, feat), lambda k: (k, 0)),
            pl.BlockSpec((1, 6, feat), lambda k: (k, 0, 0)),
            whole(*biases.shape),
        ]
        + [pl.BlockSpec((3, d.shape[1], BLK), lambda k: (0, 0, k)) for d in dqkv],
        out_specs=[row_spec(x_view.shape), whole(1, 2 * biases.shape[0], feat)],
        out_shape=[
            jax.ShapeDtypeStruct(x_view.shape, BF16),
            jax.ShapeDtypeStruct((1, 2 * biases.shape[0], feat), BF16),
        ],
        scratch_shapes=[pltpu.VMEM((2 * biases.shape[0], feat), F32)],
        compiler_params=params(),
        cost_estimate=BRIEF,
    )(seg, w_t, x_view, dx1, mod_blocks, biases, *dqkv)


def mod_grad_kernel(
    ids_ref, dev_ref, spot_ref, one_ref, two_ref, w_ref, cond_ref,
    gw_ref, gb_ref, dcond_ref, bias_ref, act_ref, moved_ref, dact_ref, picked_ref, *, part, slots,
):
    @pl.loop(0, one_ref.shape[0])
    def _(p):
        moved_ref[p] = one_ref[dev_ref[p]]

    feat = one_ref.shape[-1]

    def columns(ref):
        wide = ref[...].astype(F32)
        wide = wide.reshape(wide.shape[0], -1, 2 * slots, feat)
        return [wide[:, i].reshape(-1, feat) for i in range(wide.shape[1])]

    one, two = columns(moved_ref), columns(two_ref)
    rows = one[0].shape[0]
    first = lax.broadcasted_iota(jnp.int32, (rows, 1), 0) % (2 * slots) < slots
    act_ref[...] = jnp.where(first, pltpu.roll(two[0], rows - slots, 0), 0.0).T
    act = act_ref[pl.ds(pl.multiple_of(ids_ref[1] * part, 8), part), :].astype(BF16)
    dact = None
    for i, values in enumerate(one + two):
        at = slice(i * feat, (i + 1) * feat)
        low = values.astype(BF16)
        gw_ref[:, at] = dot(act, low, 1, 0)
        gb_ref[:, at] = jnp.sum(jnp.where(first, values, 0.0), axis=0, keepdims=True)
        more = dot(low, w_ref[:, at], 1, 1)
        dact = more if dact is None else dact + more
    dact_ref[...] = dact

    @pl.loop(0, spot_ref.shape[0])
    def _(j):
        at = spot_ref[j]
        row = dact_ref[pl.ds(jnp.maximum(at, 0), 1), :]
        picked_ref[pl.ds(j, 1), :] = jnp.where(at >= 0, row, 0.0)

    cond = cond_ref[...].astype(F32)
    gate = 1.0 / (1.0 + jnp.exp(-cond))
    dcond_ref[...] = (picked_ref[...] * (gate * (1.0 + cond * (1.0 - gate)))).astype(BF16)
    for i, values in enumerate(one):
        sums = jnp.sum(values.reshape(-1, 2 * slots, feat), axis=0)
        bias_ref[i * slots : (i + 1) * slots, :] = sums[slots:, :]


def mod_grad(group, me, device_of, spot, one, two, w_mod, cond, part, slots):
    feat, columns = w_mod.shape
    places, share = cond.shape
    count = 2 * slots * one.shape[0]

    def fixed(*shape):
        return pl.BlockSpec(shape, lambda i, *scalars: (0,) * len(shape))

    return pl.pallas_call(
        functools.partial(mod_grad_kernel, part=part, slots=slots),
        grid_spec=pltpu.PrefetchScalarGridSpec(
            num_scalar_prefetch=3,
            grid=(1,),
            in_specs=[
                fixed(*one.shape),
                fixed(*two.shape),
                pl.BlockSpec((share, columns), lambda i, ids, *scalars: (ids[0], 0)),
                fixed(places, share),
            ],
            out_specs=[
                fixed(part, columns),
                fixed(1, columns),
                fixed(places, share),
                fixed(2 * slots, feat),
            ],
            scratch_shapes=[pltpu.VMEM((feat, count), F32), pltpu.VMEM(one.shape, BF16), pltpu.VMEM((count, share), F32), pltpu.VMEM((places, share), F32)],
        ),
        out_shape=[
            jax.ShapeDtypeStruct((part, columns), F32),
            jax.ShapeDtypeStruct((1, columns), F32),
            jax.ShapeDtypeStruct((places, share), BF16),
            jax.ShapeDtypeStruct((2 * slots, feat), F32),
        ],
        compiler_params=params(),
        cost_estimate=BRIEF,
    )(jnp.stack([group, me]), device_of, spot, one, two, w_mod, cond)


def swap(values, axis, bit):
    count = lax.axis_size(axis)
    return lax.ppermute(values, axis, [(i, i ^ bit) for i in range(count)])


def bits_of(wide):
    return [1 << i for i in range(wide.bit_length() - 1)]


def chain_orders(wide):
    bits = bits_of(wide)
    x, y, z = bits[:3]
    far, rest = bits[3:4], bits[4:]
    return [[x, y, *far, z, *rest], [y, z, x, *far, *rest], [z, x, y, *far, *rest]]


class Part:
    def __init__(self, keep, got, start, rows, order):
        self.keep, self.got, self.at = keep, got, start
        self.rows = rows
        self.fresh = True
        self.dims = list(reversed(bits_of(keep.shape[0])))
        self.order = list(order)


class Rider:
    def __init__(self, values, order):
        self.keep, self.got, self.at = values, None, 0
        self.rows = values.shape[1]
        self.fresh = True
        self.order, self.done = list(order), []

    def differences(self):
        return [sum(b for i, b in enumerate(self.done) if p >> i & 1) for p in range(1 << len(self.done))]

    def place(self, difference):
        at = jnp.zeros_like(difference)
        for i, bit in enumerate(self.done):
            at = at + ((difference // bit) % 2) * (1 << i)
        return at


def masks_of(bits):
    top = len(bits) - 1
    return [sum(b for i, b in enumerate(bits) if m >> (top - i) & 1) for m in range(1 << len(bits))]


def relay_kernel(me_ref, *refs, plan, inputs, outputs):
    ins, outs, scratch = refs[:inputs], refs[inputs : inputs + outputs], list(refs[inputs + outputs :])
    arriving = {}
    if scratch:
        sems = scratch.pop()
        for i, (kind, keep, got, at, rows, *_) in enumerate(plan):
            if kind == "fresh":
                for source in (keep, got):
                    k = len(arriving)
                    copy = pltpu.make_async_copy(
                        ins[source].at[:, pl.ds(at, rows), :], scratch[k], sems.at[k]
                    )
                    copy.start()
                    arriving[i, source == got] = (copy, scratch[k])
    for i, (kind, keep, got, at, rows, bit, inner, count, targets) in enumerate(plan):
        if kind == "ride":
            pieces = [ins[keep][0]]
            if got is not None:
                pieces.append(ins[got][at : at + rows, :])
            for out, base in targets:
                for k, piece in enumerate(pieces):
                    to = slice(base + k * rows, base + (k + 1) * rows)
                    if len(outs[out].shape) == 3:
                        outs[out][0, to, :] = piece
                    else:
                        outs[out][to, :] = piece
            continue
        if kind == "fresh":
            for copy, _ in (arriving[i, False], arriving[i, True]):
                copy.wait()
            k_ref, g_ref = arriving[i, False][1], arriving[i, True][1]
        else:
            k_ref, g_ref = ins[keep], None if bit is None else ins[got]
        if bit is None:
            total = k_ref[0].astype(F32)
            for source, first in zip(got, at, strict=True):
                total = total + ins[source][first : first + rows, :].astype(F32)
            outs[targets[0][0]][...] = total
            continue
        if isinstance(bit, tuple):
            top = len(bit) - 1
            own = sum(((me_ref[0] // b) % 2) << (top - k) for k, b in enumerate(bit))
            for m, (out, base) in enumerate(targets):
                right = g_ref[pl.ds(pl.multiple_of(at + (own ^ m) * rows, TILE), rows), :]
                if base is None:
                    outs[out][0] = k_ref[own ^ m] + right
                else:
                    outs[out][base : base + rows, :] = k_ref[own ^ m] + right
            continue
        own = (me_ref[0] // bit) % 2

        @pl.loop(0, count // 2)
        def _(e, kind=kind, at=at, own=own, rows=rows, inner=inner, k_ref=k_ref, g_ref=g_ref, targets=targets):
            outer = (e // inner) * 2 * inner + e % inner
            for which, (out, base) in zip((1 - own, own), targets, strict=True):
                entry = outer + which * inner
                if kind == "fresh":
                    right = g_ref[entry]
                else:
                    right = g_ref[pl.ds(pl.multiple_of(at + entry * rows, TILE), rows), :]
                total = k_ref[entry] + right
                if base is None:
                    outs[out][e] = total
                else:
                    outs[out][pl.ds(pl.multiple_of(base + e * rows, TILE), rows), :] = total


def relay(me, moving):
    arrays, places, plan, shapes, sends = [], [], [], [], {}
    columns = moving[0].keep.shape[2]
    vmem, hbm = pl.BlockSpec(memory_space=pltpu.VMEM), pl.BlockSpec(memory_space=pl.ANY)

    def index(array, place):
        if array is None:
            return None
        for i, known in enumerate(arrays):
            if known is array:
                return i
        arrays.append(array)
        places.append(place)
        return len(arrays) - 1

    bits = set()
    for m in moving:
        if m.order:
            bits.update(masks_of(m.order[0])[1:] if isinstance(m.order[0], tuple) else m.order[:1])
    bits = sorted(bits)
    sizes = dict.fromkeys(bits, 0)
    scratch, keeps = [], []
    for m in moving:
        bit = m.order[0] if m.order else None
        ride = isinstance(m, Rider)
        kind = "ride" if ride else "fresh" if m.fresh else "add"
        place = hbm if kind == "fresh" else vmem
        keep, at = index(m.keep, place), m.at
        several = isinstance(m.got, list)
        got = [index(g, place) for g in m.got] if several else index(m.got, place)
        rows, inner, count = m.rows, 1, 1
        fan = isinstance(bit, tuple)
        to = (bits.index(bit), sizes[bit]) if bit is not None and not fan else None
        kept = len(bits) + len(shapes)
        keeps.append(kept)
        if ride:
            m.rows *= 1 if got is None else 2
            shapes.append(jax.ShapeDtypeStruct((1, m.rows, columns), BF16))
            targets = [(kept, 0)] + ([] if to is None else [to])
            size = m.rows
        elif bit is None:
            shapes.append(jax.ShapeDtypeStruct((rows, columns), F32))
            targets, size = [(kept, 0)], 0
            got, at = (got, at) if several else ([got], [at])
        elif fan:
            shapes.append(jax.ShapeDtypeStruct((1, rows, columns), BF16))
            masks_here = masks_of(bit)[1:]
            m.at = [sizes[mask] for mask in masks_here]
            targets = [(kept, None)] + [(bits.index(mask), sizes[mask]) for mask in masks_here]
            for mask in masks_here:
                sizes[mask] += rows
            m.dims = []
        else:
            dim = m.dims.index(bit)
            count, inner = 1 << len(m.dims), 1 << (len(m.dims) - 1 - dim)
            m.dims.pop(dim)
            size = count // 2 * rows
            shapes.append(jax.ShapeDtypeStruct((count // 2, rows, columns), BF16))
            targets = [to, (kept, None)]
            if kind == "fresh":
                scratch += [pltpu.VMEM((count, rows, columns), BF16)] * 2
        plan.append((kind, keep, got, at, rows, bit, inner, count, targets))
        if bit is not None and not fan:
            m.at = sizes[bit]
            sizes[bit] += size
        m.fresh = False
    if scratch:
        scratch.append(pltpu.SemaphoreType.DMA((len(scratch),)))
    shapes = [jax.ShapeDtypeStruct((sizes[b], columns), BF16) for b in bits] + shapes
    out = pl.pallas_call(
        functools.partial(relay_kernel, plan=plan, inputs=len(arrays), outputs=len(shapes)),
        in_specs=[pl.BlockSpec(memory_space=pltpu.SMEM)] + places,
        out_specs=[vmem] * len(shapes),
        out_shape=shapes,
        scratch_shapes=scratch,
        compiler_params=params(),
        cost_estimate=BRIEF,
    )(me, *arrays)
    for m, kept in zip(moving, keeps, strict=True):
        m.keep = out[kept]
    return dict(zip(bits, out))


class Sums:
    def __init__(self, me):
        self.me, self.moving, self.going = me, [], {}

    def step(self, *joining, after=()):
        came = {bit: swap(send, "wide", bit) for bit, send in self.going.items()}
        if after:
            kept, _ = lax.optimization_barrier((tuple(m.keep for m in self.moving), tuple(after)))
            for m, array in zip(self.moving, kept, strict=True):
                m.keep = array
        going = [m for m in self.moving if m.order]
        for m in going:
            bit = m.order.pop(0)
            m.got = [came[mask] for mask in masks_of(bit)[1:]] if isinstance(bit, tuple) else came[bit]
            if isinstance(m, Rider):
                m.done.append(bit)
        self.moving += joining
        self.going = relay(self.me, going + list(joining))

    def arrays(self):
        return tuple(self.going.values()) + tuple(m.keep for m in self.moving)

    def put(self, arrays):
        count = len(self.going)
        self.going = dict(zip(self.going, arrays[:count], strict=True))
        for m, kept in zip(self.moving, arrays[count:], strict=True):
            m.keep = kept


def tie(values, moving):
    out = lax.optimization_barrier((tuple(values), tuple(m.arrays() for m in moving)))
    for one, kept in zip(moving, out[1], strict=True):
        one.put(kept)
    return out[0]


def local(
    x_src,
    cond,
    lengths,
    bucket,
    w_mod,
    b_mod,
    w_qkv,
    b_qv,
    w_proj,
    b_proj,
    w_fc1,
    b_fc1,
    w_fc2,
    b_fc2,
    grad_out,
):
    wide = lax.axis_size("wide")
    halves = lax.axis_size("narrow")
    devices = wide * halves
    group = lax.axis_index("wide")
    half = lax.axis_index("narrow")
    rows, feat = x_src.shape
    hidden = w_fc1.shape[1]
    places = lengths.shape[0] // halves
    slots = places // wide
    blocks = rows // BLK
    per_block = BLK // wide
    tiled = per_block % TILE == 0

    split = regroup if tiled else regroup_any
    send, scond, seg, src, cidx = split(x_src, cond, lengths, bucket, jnp.stack([group, half]), wide)
    exchange = functools.partial(
        lax.all_to_all, axis_name="wide", split_axis=0, concat_axis=0, tiled=True
    )
    came = exchange(send)
    came_cond = exchange(scond.reshape(wide, slots, feat // wide))
    cond_in = came_cond.transpose(1, 0, 2).reshape(slots, feat)
    x_view = came.reshape(wide, blocks, per_block, feat)
    if not tiled:
        x_view = x_view.transpose(1, 0, 2, 3).reshape(1, blocks, BLK, feat)

    act_low = jax.nn.silu(cond_in.astype(F32)).astype(BF16)
    modulate = jnp.dot(act_low, w_mod, preferred_element_type=F32) + b_mod.astype(F32)
    slot_ids = jnp.arange(slots, dtype=jnp.int32)
    in_slot = seg[:, None] == slot_ids[None, :]
    mod_blocks = jnp.sum(
        jnp.where(in_slot[:, :, None], modulate[None], 0.0), axis=1
    ).reshape(blocks, 6, feat)

    dy = (
        grad_out.reshape(blocks, per_block, wide, feat)
        .transpose(0, 2, 1, 3)
        .reshape(rows, feat)
    )
    gate_two = mod_blocks[:, 5:6, :]
    df = (
        (gate_two * dy.reshape(blocks, BLK, feat).astype(F32)).astype(BF16).reshape(rows, feat)
    )
    grad_b_fc2 = jnp.sum(df.astype(F32), axis=0)
    dg = dot(df, w_fc2, 1, 1)
    w_qkv_t = w_qkv.T
    bias_qkv = jnp.concatenate(
        [b_qv[:feat].astype(F32), jnp.zeros((feat,), F32), b_qv[feat:].astype(F32)]
    ).reshape(3 * feat, 1)

    qkv_t, a1_t = qkv_forward(x_view, mod_blocks, w_qkv_t, bias_qkv)
    o_t, lse = attend(seg, qkv_t)
    attn, x1, a2, a2_t = proj_forward(
        o_t, w_proj, b_proj.astype(F32).reshape(1, feat), x_view, mod_blocks
    )
    own, place = half.reshape(1), group.reshape(1)
    part = feat // devices
    halved = Halves(wide, part)
    both = ("wide", "narrow")
    orders = chain_orders(wide)
    near, far = bits_of(wide)[:3], bits_of(wide)[3:]
    sums = Sums(place)

    def shares(grad, got, cuts, ways):
        return [
            Part(grad[1], got, a, b - a, way)
            for a, b, way in zip(cuts[:-1], cuts[1:], ways, strict=True)
        ]

    def thirds(rows_of):
        third = -(-rows_of // 3 // TILE) * TILE
        return [0, third, min(2 * third, rows_of - TILE), rows_of]

    f, da2, grad_b_fc1, d_fc1, d_fc2 = mlp(
        own, a2, a2_t, df, dg, w_fc1, w_fc2, b_fc1.astype(F32).reshape(1, hidden), halved
    )

    if halved.split:
        fc2_got, fc1_got = swap(d_fc2[0], "narrow", 1), swap(d_fc1[0], "narrow", 1)
    y, dx1, do_t, grad_b_proj, two, d_proj = middle(
        own, seg, act_low, f, b_fc2.astype(F32).reshape(1, feat), x1, attn, dy, da2, mod_blocks, o_t,
        w_proj, halved,
    )
    y_dest = (
        y.reshape(blocks, wide, per_block, feat).transpose(0, 2, 1, 3).reshape(rows, feat)
    )
    pieces, row_sums, head = [], [], 0

    def attention(counts):
        nonlocal head
        for count in counts:
            piece, piece_sums = attend_back(
                seg, qkv_t, o_t, do_t, lse, first=head, count=count
            )
            pieces.append(piece)
            row_sums.append(piece_sums[:, 0])
            head += count

    def bias_rows():
        of_qv = jnp.concatenate(row_sums, axis=1)
        rows_of = [grad_b_fc1[0], grad_b_fc2, grad_b_proj[0], of_qv[0], of_qv[1]]
        return jnp.concatenate(rows_of).reshape(2 * slots, feat)

    ride_order = far + near[2:] + near[:2]
    if halved.split:
        proj_got = swap(d_proj[0], "narrow", 1)
        third = (d_fc2[1].shape[1] + d_fc1[1].shape[1] + part) // 3 // TILE * TILE
        fc2_parts = shares(d_fc2, fc2_got, [0, third, d_fc2[1].shape[1]], [orders[0], orders[2]])
        fc1_parts = shares(d_fc1, fc1_got, [0, third, d_fc1[1].shape[1]], [orders[1], orders[2]])
        proj_parts = shares(d_proj, proj_got, [0, part], orders[2:])
        two = Rider(two, ride_order)
        sums.step(*fc2_parts, *fc1_parts, *proj_parts, two)
        for counts in ((12,), (4,)):
            (do_t, *pieces) = tie((do_t, *pieces), [sums])
            attention(counts)
            sums.step()
        (a1_t, *pieces) = tie((a1_t, *pieces), [sums])
    else:
        attention((4, 4, 4, 4))
    d_qkv = qkv_grad(own, a1_t, pieces, halved)
    if halved.split:
        sums.step(after=d_qkv)
        qkv_got = swap(d_qkv[0], "narrow", 1)
        (dx1, *pieces) = tie((dx1, *pieces), [sums])
    drows, one = rows_back(seg, pieces, w_qkv_t, x_view, dx1, mod_blocks, bias_rows())
    if halved.split:
        sums.step()
        (drows,) = tie((drows,), [sums])
    back = drows
    if not tiled:
        back = back.reshape(blocks, wide, per_block, feat).transpose(1, 0, 2, 3)
    back = exchange(back.reshape(wide, rows // wide, feat))
    me = group * halves + half

    def modulation_grads(device_of, one_all, two_all):
        bucket_of, slot_of = jnp.maximum(cidx, 0) // slots, jnp.maximum(cidx, 0) % slots
        if halved.split:
            spot = two.place(bucket_of ^ group) * 2 * slots + slot_of
        else:
            spot = (bucket_of * halves + half) * 2 * slots + slot_of
        spot = jnp.where(cidx >= 0, spot, -1)
        return mod_grad(group, me, device_of, spot, one_all, two_all, w_mod, cond, part, slots)

    one_all = lax.all_gather(one, both, axis=0, tiled=True)
    if halved.split:
        last = tuple(reversed(near[2:] + far))
        flat, turned = [*near[:2], last], [*near[:2][::-1], last]
        qkv_parts = shares(
            d_qkv, qkv_got, [0, part, 2 * part, 2 * part + part // 2, 3 * part], [flat, turned, flat, turned]
        )
        sums = Sums(place)
        sums.step(*qkv_parts)
        tie((), [sums])
        sums.step()
        tie((), [sums])
        sums.step()
        (back,) = tie((back,), [sums])
        two_all = two.keep.reshape(wide, -1, feat)
        two_all = jnp.concatenate([two_all, swap(two_all, "narrow", 1)], axis=0)
        differs = jnp.asarray(two.differences(), jnp.int32)
        device_of = jnp.concatenate(
            [(differs ^ group) * halves + half, (differs ^ group) * halves + 1 - half]
        )
        sums.step()
        while sums.going:
            sums.step()
        (one_all,) = tie((one_all,), [sums])
        modulation = modulation_grads(device_of, one_all, two_all)
        grad_w_fc2 = jnp.concatenate([p.keep for p in fc2_parts], axis=0)
        grad_w_fc1 = jnp.concatenate([p.keep for p in fc1_parts], axis=0)
        grad_w_fc1 = (
            grad_w_fc1.reshape(hidden // feat, part, feat).transpose(1, 0, 2).reshape(part, hidden)
        )
        (grad_w_proj,) = (p.keep for p in proj_parts)

        kept = [p.keep for p in qkv_parts]
        grad_w_qkv = jnp.concatenate(kept[:2] + [jnp.concatenate(kept[2:], axis=0)], axis=1)
    else:
        two_all = lax.all_gather(two, both, axis=0, tiled=True)
        modulation = modulation_grads(jnp.arange(devices, dtype=jnp.int32), one_all, two_all)

        def scattered(full):
            return lax.psum_scatter(full, both, scatter_dimension=0, tiled=True).astype(F32)

        grad_w_fc2 = scattered(d_fc2[0])
        grad_w_fc1 = scattered(d_fc1[0].transpose(1, 0, 2).reshape(feat, hidden))
        grad_w_proj = scattered(d_proj[0])
        grad_w_qkv = scattered(d_qkv[0].transpose(1, 0, 2).reshape(feat, 3 * feat))
    merge = restore if tiled else restore_any
    dx_src = merge(src, back.reshape(rows, feat))

    grad_w_mod, grad_b_mod, dcond, biases = modulation
    grad_b_mod = lax.dynamic_slice_in_dim(grad_b_mod[0], me * 6 * part, 6 * part)

    def own_part(first, count):
        rows_of = biases[first : first + count].reshape(-1)
        share = rows_of.shape[0] // devices
        return lax.dynamic_slice_in_dim(rows_of, me * share, share)

    fc1_lines = hidden // feat
    s_fc1, s_fc2, s_proj = own_part(0, fc1_lines), own_part(fc1_lines, 1), own_part(fc1_lines + 1, 1)
    s_qv = own_part(fc1_lines + 2, 2)
    return (
        y_dest,
        dx_src,
        dcond,
        grad_w_mod,
        grad_b_mod,
        grad_w_qkv,
        s_qv,
        grad_w_proj,
        s_proj,
        grad_w_fc1,
        s_fc1,
        grad_w_fc2,
        s_fc2,
    )


def solution(mesh):
    both = ("wide", "narrow")
    placed = (P("narrow", "wide"), P("narrow", "wide")) + (P(),) * 12 + (P(both, None),)
    matrix, vector = P(both, None), P(both)
    return jax.shard_map(
        local,
        mesh=mesh,
        in_specs=placed,
        out_specs=(
            matrix,
            P("narrow", "wide"),
            P("narrow", "wide"),
            matrix,
            vector,
            matrix,
            vector,
            matrix,
            vector,
            matrix,
            vector,
            matrix,
            vector,
        ),
        check_vma=False,
    )
```

```python
import functools
import math

import jax
import jax.numpy as jnp
from jax import lax
from jax.experimental import pallas as pl
from jax.experimental.pallas import tpu as pltpu
from jax.sharding import PartitionSpec as P

HEADS = 16
HEAD_DIM = 64
EPS = 1e-06
MASKED = -1000000000.0
LOG2E = 1.4426950408889634
BLK = 256
TILE = 16
VMEM_LIMIT = 58 * 2**20
BRIEF = pl.CostEstimate(flops=1, bytes_accessed=1, transcendentals=0)
BF16 = jnp.bfloat16
F32 = jnp.float32


def params(**more):
    return pltpu.CompilerParams(vmem_limit_bytes=VMEM_LIMIT, **more)


def dot(left, right, left_dim, right_dim):
    return lax.dot_general(
        left, right, (((left_dim,), (right_dim,)), ((), ())), preferred_element_type=F32
    )


def norm_parts(values):
    centre = values - jnp.mean(values, axis=1, keepdims=True)
    spread = jnp.mean(centre * centre, axis=1, keepdims=True)
    inverse = lax.rsqrt(spread + EPS)
    return centre * inverse, inverse


def norm_back(grad, normed, inverse):
    return (
        grad
        - jnp.mean(grad, axis=1, keepdims=True)
        - normed * jnp.mean(grad * normed, axis=1, keepdims=True)
    ) * inverse


def each_place(len_ref, buck_ref, base, count, off_ref, slot_ref, wide, visit):
    for i in range(wide):
        off_ref[i] = 0
        slot_ref[i] = 0

    def place(j, offset):
        units = len_ref[base + j] // wide
        b = buck_ref[base + j]

        @pl.when(units > 0)
        def _():
            start = off_ref[b]
            slot = slot_ref[b]
            off_ref[b] = start + units
            slot_ref[b] = slot + 1
            visit(j, b, units, offset, start, slot)

        return offset + units

    lax.fori_loop(0, count, place, 0)


def regroup_rows_kernel(
    len_ref, buck_ref, me_ref, x_ref, send_ref, src_ref, off_ref, slot_ref, *, wide, places
):
    cells = send_ref.shape[1]
    send_ref[...] = jnp.zeros_like(send_ref)

    @pl.loop(0, src_ref.shape[0])
    def _(i):
        src_ref[i] = -1

    def visit(j, b, units, offset, start, slot):
        @pl.loop(0, units // TILE)
        def _(t):
            a = pl.multiple_of(offset + t * TILE, TILE)
            c = pl.multiple_of(start + t * TILE, TILE)
            send_ref[b, pl.ds(c, TILE), :] = x_ref[pl.ds(a, TILE), :]
            src_ref[a // TILE] = (b * cells + c) // TILE

    each_place(len_ref, buck_ref, me_ref[1] * places, places, off_ref, slot_ref, wide, visit)


def regroup_cond_kernel(
    len_ref, buck_ref, me_ref, cond_ref, scond_ref, seg_ref, cidx_ref,
    off_ref, slot_ref, cond_in, cond_out, *, wide, slots,
):
    cond_out[...] = jnp.zeros_like(cond_out)
    cond_in[...] = cond_ref[...].astype(F32)
    for i in range(seg_ref.shape[0]):
        seg_ref[i] = -1

    @pl.loop(0, cidx_ref.shape[0])
    def _(j):
        cidx_ref[j] = -1

    def visit(j, b, units, offset, start, slot):
        cidx_ref[j] = b * slots + slot
        cond_out[pl.ds(b * slots + slot, 1), :] = cond_in[pl.ds(j, 1), :]

        @pl.when(b == me_ref[0])
        def _():
            @pl.loop(0, units * wide // BLK)
            def _(t):
                seg_ref[start * wide // BLK + t] = slot

    places = cidx_ref.shape[0]
    each_place(len_ref, buck_ref, me_ref[1] * places, places, off_ref, slot_ref, wide, visit)
    scond_ref[...] = cond_out[...].astype(BF16)


def regroup(x_src, cond, lens, buck, me, wide):
    rows, feat = x_src.shape
    places, part = cond.shape
    slots = places // wide
    smem = pl.BlockSpec(memory_space=pltpu.SMEM)
    vmem = pl.BlockSpec(memory_space=pltpu.VMEM)
    counters = [pltpu.SMEM((wide,), jnp.int32), pltpu.SMEM((wide,), jnp.int32)]
    scond, seg, cidx = pl.pallas_call(
        functools.partial(regroup_cond_kernel, wide=wide, slots=slots),
        in_specs=[smem, smem, smem, vmem],
        out_specs=[vmem, smem, smem],
        out_shape=[
            jax.ShapeDtypeStruct((places, part), BF16),
            jax.ShapeDtypeStruct((rows // BLK,), jnp.int32),
            jax.ShapeDtypeStruct((places,), jnp.int32),
        ],
        scratch_shapes=counters + [pltpu.VMEM((places, part), F32), pltpu.VMEM((places, part), F32)],
        compiler_params=params(),
        cost_estimate=BRIEF,
    )(lens, buck, me, cond)
    send, src = pl.pallas_call(
        functools.partial(regroup_rows_kernel, wide=wide, places=places),
        in_specs=[smem, smem, smem, vmem],
        out_specs=[vmem, smem],
        out_shape=[
            jax.ShapeDtypeStruct((wide, rows // wide, feat), BF16),
            jax.ShapeDtypeStruct((rows // TILE,), jnp.int32),
        ],
        scratch_shapes=counters,
        compiler_params=params(),
        cost_estimate=BRIEF,
    )(lens, buck, me, x_src)
    return send, scond, seg, src, cidx


def restore_kernel(src_ref, back_ref, dx_ref):
    @pl.loop(0, src_ref.shape[0])
    def _(i):
        at = src_ref[i]
        rows = back_ref[pl.ds(pl.multiple_of(jnp.maximum(at, 0) * TILE, TILE), TILE), :]
        dx_ref[pl.ds(pl.multiple_of(i * TILE, TILE), TILE), :] = jnp.where(
            at >= 0, rows, jnp.zeros_like(rows)
        )


def restore(src, back):
    vmem = pl.BlockSpec(memory_space=pltpu.VMEM)
    return pl.pallas_call(
        restore_kernel,
        in_specs=[pl.BlockSpec(memory_space=pltpu.SMEM), vmem],
        out_specs=vmem,
        out_shape=jax.ShapeDtypeStruct(back.shape, BF16),
        compiler_params=params(),
        cost_estimate=BRIEF,
    )(src, back)


def regroup_any(x_src, cond, lens, buck, me, wide):
    rows, feat = x_src.shape
    places = cond.shape[0]
    lens = lax.dynamic_slice_in_dim(lens, me[1] * places, places)
    buck = lax.dynamic_slice_in_dim(buck, me[1] * places, places)
    slots, cells = places // wide, rows // wide
    units = lens // wide
    order = jnp.arange(places, dtype=jnp.int32)
    earlier = (order[:, None] < order[None, :]) & (buck[:, None] == buck[None, :])
    live = (lens > 0).astype(jnp.int32)
    offset = jnp.cumsum(units) - units
    start = jnp.sum(jnp.where(earlier, units[:, None], 0), axis=0)
    slot = jnp.sum(jnp.where(earlier, live[:, None], 0), axis=0)
    cell = jnp.arange(cells, dtype=jnp.int32)[None, :, None]
    to_target = (buck[None, :] == jnp.arange(wide, dtype=jnp.int32)[:, None]) & (live[None, :] > 0)
    hit = (
        to_target[:, None, :]
        & (cell >= start[None, None, :])
        & (cell < (start + units)[None, None, :])
    ).astype(jnp.int32)
    valid = jnp.sum(hit, axis=2)
    source = jnp.sum(hit * (offset - start)[None, None, :], axis=2) + cell[:, :, 0]
    source = jnp.where(valid > 0, source, 0)
    picked = jnp.take(x_src, source.reshape(-1), axis=0).reshape(wide, cells, feat)
    send = jnp.where(valid[:, :, None] > 0, picked, jnp.zeros((), BF16))
    cond_hit = to_target[:, None, :] & (
        slot[None, None, :] == jnp.arange(slots, dtype=jnp.int32)[None, :, None]
    )
    scond = jnp.einsum("wqs,sf->wqf", cond_hit.astype(BF16), cond, preferred_element_type=F32)
    scond = scond.astype(BF16).reshape(cond.shape)
    first = jnp.arange(rows // BLK, dtype=jnp.int32)[:, None] * BLK
    mine = (
        ((buck == me[0]) & (live > 0))[None, :]
        & (first >= (start * wide)[None, :])
        & (first < ((start + units) * wide)[None, :])
    )
    seg = jnp.sum(jnp.where(mine, slot[None, :] + 1, 0), axis=1) - 1
    spot = jnp.arange(rows, dtype=jnp.int32)[:, None]
    inside = (live[None, :] > 0) & (spot >= offset[None, :]) & (spot < (offset + units)[None, :])
    src = jnp.sum(jnp.where(inside, (buck * cells + start - offset)[None, :] + spot + 1, 0), axis=1)
    cidx = jnp.where(live > 0, buck * slots + slot, -1)
    return send, scond, seg.astype(jnp.int32), src - 1, cidx


def restore_any(src, back):
    dx = jnp.take(back, jnp.maximum(src, 0), axis=0)
    return jnp.where(src[:, None] >= 0, dx, jnp.zeros((), BF16))


def qkv_kernel(x_ref, mod_ref, w_ref, b_ref, q_ref, a_ref):
    feat = x_ref.shape[-1]
    x = x_ref[...].reshape(BLK, feat).astype(F32)
    normed, _ = norm_parts(x)
    a1 = (normed * (1.0 + mod_ref[0, 1:2, :]) + mod_ref[0, 0:1, :]).astype(BF16)
    a1_t = a1.T
    a_ref[...] = a1_t
    for i in range(3):
        part = slice(i * feat, (i + 1) * feat)
        q_ref[part, :] = (dot(w_ref[part, :], a1_t, 1, 0) + b_ref[part, :]).astype(BF16)


def row_spec(view):
    return pl.BlockSpec((view[0], 1, view[2], view[3]), lambda k: (0, k, 0, 0))


def whole(*shape):
    return pl.BlockSpec(shape, lambda k: (0,) * len(shape))


def qkv_forward(x_view, mod_blocks, w_t, bias):
    feat = x_view.shape[-1]
    blocks = x_view.shape[1]
    return pl.pallas_call(
        qkv_kernel,
        grid=(blocks,),
        in_specs=[
            row_spec(x_view.shape),
            pl.BlockSpec((1, 6, feat), lambda k: (k, 0, 0)),
            whole(3 * feat, feat),
            whole(3 * feat, 1),
        ],
        out_specs=[
            pl.BlockSpec((3 * feat, BLK), lambda k: (0, k)),
            pl.BlockSpec((feat, BLK), lambda k: (0, k)),
        ],
        out_shape=[
            jax.ShapeDtypeStruct((3 * feat, blocks * BLK), BF16),
            jax.ShapeDtypeStruct((feat, blocks * BLK), BF16),
        ],
        compiler_params=params(),
        cost_estimate=BRIEF,
    )(x_view, mod_blocks, w_t, bias)


def masks(seg_ref, query_block, blocks):
    base = LOG2E / math.sqrt(HEAD_DIM)
    same = [seg_ref[query_block] == seg_ref[kb] for kb in range(blocks)]
    scales = [jnp.where(s, base, 0.0) for s in same]
    shifts = [jnp.where(s, 0.0, MASKED * LOG2E) for s in same]
    return scales, shifts


def attend_kernel(seg_ref, q_ref, k_ref, v_ref, o_ref, lse_ref, *, blocks, heads):
    units = [(h, qb) for h in range(heads) for qb in range(blocks)]
    keys = [k_ref[h * HEAD_DIM : (h + 1) * HEAD_DIM, :].T for h in range(heads)]

    def spans(h, qb):
        return slice(h * HEAD_DIM, (h + 1) * HEAD_DIM), slice(qb * BLK, (qb + 1) * BLK)

    def scores_of(h, qb):
        q_t = q_ref[spans(h, qb)]
        return [dot(keys[h][kb * BLK : (kb + 1) * BLK], q_t, 1, 0) for kb in range(blocks)]

    def finish(h, qb, probs, total, top):
        hs, qs = spans(h, qb)
        out = dot(v_ref[hs, :], probs, 1, 0)
        o_ref[hs, qs] = (out / total).astype(BF16)
        lse_ref[h, :, qs] = top + jnp.log2(total)

    ahead, behind = scores_of(*units[0]), None
    for i, (h, qb) in enumerate(units):
        scores, ahead = ahead, scores_of(*units[i + 1]) if i + 1 < len(units) else None
        scales, shifts = masks(seg_ref, qb, blocks)
        top = None
        for kb in range(blocks):
            peak = jnp.max(scores[kb], axis=0, keepdims=True) * scales[kb] + shifts[kb]
            top = peak if top is None else jnp.maximum(top, peak)
        if behind is not None:
            finish(*behind)
        total = jnp.zeros((1, BLK), F32)
        parts = []
        for kb in range(blocks):
            expo = jnp.exp2(scores[kb] * scales[kb] - (top - shifts[kb]))
            total = total + jnp.sum(expo, axis=0, keepdims=True)
            parts.append(expo.astype(BF16))
        behind = (h, qb, jnp.concatenate(parts, axis=0), total, top)
    finish(*behind)


def attend(seg, qkv_t, heads=4):
    feat3, rows = qkv_t.shape
    feat = feat3 // 3
    span = heads * HEAD_DIM
    groups = feat // span
    return pl.pallas_call(
        functools.partial(attend_kernel, blocks=rows // BLK, heads=heads),
        grid_spec=pltpu.PrefetchScalarGridSpec(
            num_scalar_prefetch=1,
            grid=(groups,),
            in_specs=[
                pl.BlockSpec((span, rows), lambda g, s: (g, 0)),
                pl.BlockSpec((span, rows), lambda g, s: (groups + g, 0)),
                pl.BlockSpec((span, rows), lambda g, s: (2 * groups + g, 0)),
            ],
            out_specs=[
                pl.BlockSpec((span, rows), lambda g, s: (g, 0)),
                pl.BlockSpec((heads, 1, rows), lambda g, s: (g, 0, 0)),
            ],
        ),
        out_shape=[
            jax.ShapeDtypeStruct((feat, rows), BF16),
            jax.ShapeDtypeStruct((feat // HEAD_DIM, 1, rows), F32),
        ],
        compiler_params=params(),
        cost_estimate=BRIEF,
    )(seg, qkv_t, qkv_t, qkv_t)


def attend_back_kernel(
    seg_ref, q_ref, k_ref, v_ref, o_ref, do_ref, lse_ref, out_ref, sums_ref, *, blocks, heads
):
    scale = 1.0 / math.sqrt(HEAD_DIM)
    units = [(h, qb) for h in range(heads) for qb in range(blocks)]
    keys = [k_ref[h * HEAD_DIM : (h + 1) * HEAD_DIM, :].T for h in range(heads)]
    values = [v_ref[h * HEAD_DIM : (h + 1) * HEAD_DIM, :].T for h in range(heads)]

    def spans(h, qb):
        return slice(h * HEAD_DIM, (h + 1) * HEAD_DIM), slice(qb * BLK, (qb + 1) * BLK)

    def products(h, qb):
        q_t, do_t = q_ref[spans(h, qb)], do_ref[spans(h, qb)]
        cuts = [slice(kb * BLK, (kb + 1) * BLK) for kb in range(blocks)]
        return [(dot(keys[h][c], q_t, 1, 0), dot(values[h][c], do_t, 1, 0)) for c in cuts]

    ahead = products(*units[0])
    grad_k = grad_v = inner = None
    for i, (h, qb) in enumerate(units):
        present, ahead = ahead, products(*units[i + 1]) if i + 1 < len(units) else None
        hs, qs = spans(h, qb)
        if qb == 0:
            inner = jnp.sum(
                o_ref[hs, :].astype(F32) * do_ref[hs, :].astype(F32), axis=0, keepdims=True
            )
        scales, shifts = masks(seg_ref, qb, blocks)
        probs, grads = [], []
        for kb, (score, grad_p) in enumerate(present):
            prob = jnp.exp2(score * scales[kb] - (lse_ref[h, :, qs] - shifts[kb]))
            probs.append(prob.astype(BF16))
            grads.append((prob * (grad_p - inner[:, qs])).astype(BF16))
        probs = jnp.concatenate(probs, axis=0)
        grads = jnp.concatenate(grads, axis=0)
        out_ref[0, hs, qs] = (dot(k_ref[hs, :], grads, 1, 0) * scale).astype(BF16)
        more_k, more_v = dot(q_ref[hs, qs], grads, 1, 1), dot(do_ref[hs, qs], probs, 1, 1)
        grad_k = more_k if qb == 0 else grad_k + more_k
        grad_v = more_v if qb == 0 else grad_v + more_v
        if qb == blocks - 1:
            out_ref[1, hs, :] = (grad_k * scale).astype(BF16)
            out_ref[2, hs, :] = grad_v.astype(BF16)
    ones = jnp.ones((8, out_ref.shape[2]), BF16)
    sums_ref[0] = dot(ones, out_ref[0], 1, 1)
    sums_ref[1] = dot(ones, out_ref[2], 1, 1)


def attend_back(seg, qkv_t, o_t, do_t, lse, first, count, heads=2):
    feat3, rows = qkv_t.shape
    feat = feat3 // 3
    span = heads * HEAD_DIM
    groups = feat // span
    at = first // heads
    return pl.pallas_call(
        functools.partial(attend_back_kernel, blocks=rows // BLK, heads=heads),
        grid_spec=pltpu.PrefetchScalarGridSpec(
            num_scalar_prefetch=1,
            grid=(count // heads,),
            in_specs=[
                pl.BlockSpec((span, rows), lambda g, s: (at + g, 0)),
                pl.BlockSpec((span, rows), lambda g, s: (groups + at + g, 0)),
                pl.BlockSpec((span, rows), lambda g, s: (2 * groups + at + g, 0)),
                pl.BlockSpec((span, rows), lambda g, s: (at + g, 0)),
                pl.BlockSpec((span, rows), lambda g, s: (at + g, 0)),
                pl.BlockSpec((heads, 1, rows), lambda g, s: (at + g, 0, 0)),
            ],
            out_specs=[
                pl.BlockSpec((3, span, rows), lambda g, s: (0, g, 0)),
                pl.BlockSpec((2, 8, span), lambda g, s: (0, 0, g)),
            ],
        ),
        out_shape=[
            jax.ShapeDtypeStruct((3, count * HEAD_DIM, rows), BF16),
            jax.ShapeDtypeStruct((2, 8, count * HEAD_DIM), F32),
        ],
        compiler_params=params(),
        cost_estimate=BRIEF,
    )(seg, qkv_t, qkv_t, qkv_t, o_t, do_t, lse)


class Halves:
    def __init__(self, wide, part, split=None):
        self.wide, self.part = wide, part
        self.split = part % TILE == 0 if split is None else split

    def shapes(self, between, columns):
        if self.split:
            shape = (self.wide,) + between + (self.part, columns)
            return [jax.ShapeDtypeStruct(shape, BF16)] * 2
        return [jax.ShapeDtypeStruct(between + (2 * self.wide * self.part, columns), BF16)]

    def specs(self, between, columns, index):
        ones = (1,) * between
        if self.split:
            return [
                pl.BlockSpec(
                    (self.wide,) + ones + (self.part, columns),
                    lambda *g: (0,) + index(*g)[:-1] + (0, index(*g)[-1]),
                )
            ] * 2
        return [
            pl.BlockSpec(
                ones + (2 * self.wide * self.part, columns),
                lambda *g: index(*g)[:-1] + (0, index(*g)[-1]),
            )
        ]

    def store(self, half, value, refs):
        if not self.split:
            refs[0][...] = value.astype(BF16).reshape(refs[0].shape)
            return
        value = value.reshape(value.shape[0] // (2 * self.part), 2, self.part, value.shape[1])
        even, odd = value[:, 0], value[:, 1]
        folds = refs[0].shape[-1] // value.shape[-1]
        if folds > 1:
            even, odd = (
                jnp.concatenate(jnp.split(half_value, folds, axis=1), axis=2) for half_value in (even, odd)
            )
        refs[0][...] = jnp.where(half == 0, odd, even).astype(BF16).reshape(refs[0].shape)
        refs[1][...] = jnp.where(half == 0, even, odd).astype(BF16).reshape(refs[1].shape)

    def finish(self, arrays):
        if self.split:
            return [a.reshape(self.wide, -1, a.shape[-1]) for a in arrays]
        return arrays


def qkv_grad_kernel(half_ref, a_ref, *refs, pieces, halves):
    ins, outs = refs[:pieces], refs[pieces:]
    value = jnp.concatenate([dot(a_ref[...], r[0], 1, 1) for r in ins], axis=1)
    halves.store(half_ref[0], value, outs)


def qkv_grad(half, a1_t, dqkv, halves):
    feat, rows = a1_t.shape
    columns = sum(d.shape[1] for d in dqkv)
    folds = feat // columns if halves.split else 1
    packed = Halves(halves.wide, halves.part // folds, halves.split)
    packed_columns = folds * columns
    out = pl.pallas_call(
        functools.partial(qkv_grad_kernel, pieces=len(dqkv), halves=halves),
        grid=(3,),
        in_specs=[pl.BlockSpec(memory_space=pltpu.SMEM), whole(feat, rows)]
        + [pl.BlockSpec((1, d.shape[1], rows), lambda i: (i, 0, 0)) for d in dqkv],
        out_specs=packed.specs(1, packed_columns, lambda i: (i, 0)),
        out_shape=packed.shapes((3,), packed_columns),
        compiler_params=params(),
        cost_estimate=BRIEF,
    )(half, a1_t, *dqkv)
    return halves.finish(out)


def proj_kernel(o_ref, w_ref, b_ref, x_ref, mod_ref, attn_ref, x1_ref, a_ref, at_ref):
    feat = x_ref.shape[-1]
    attn = dot(o_ref[...], w_ref[...], 0, 0) + b_ref[...]
    attn_ref[...] = attn
    x1 = x_ref[...].reshape(BLK, feat).astype(F32) + mod_ref[0, 2:3, :] * attn
    x1_ref[...] = x1
    normed, _ = norm_parts(x1)
    a2 = (normed * (1.0 + mod_ref[0, 4:5, :]) + mod_ref[0, 3:4, :]).astype(BF16)
    a_ref[...] = a2
    at_ref[...] = a2.T


def proj_forward(o_t, w_proj, b_proj, x_view, mod_blocks):
    feat = x_view.shape[-1]
    blocks = x_view.shape[1]
    rows = blocks * BLK
    by_row = pl.BlockSpec((BLK, feat), lambda k: (k, 0))
    by_column = pl.BlockSpec((feat, BLK), lambda k: (0, k))
    return pl.pallas_call(
        proj_kernel,
        grid=(blocks,),
        in_specs=[
            by_column,
            whole(feat, feat),
            whole(1, feat),
            row_spec(x_view.shape),
            pl.BlockSpec((1, 6, feat), lambda k: (k, 0, 0)),
        ],
        out_specs=[by_row, by_row, by_row, by_column],
        out_shape=[
            jax.ShapeDtypeStruct((rows, feat), F32),
            jax.ShapeDtypeStruct((rows, feat), F32),
            jax.ShapeDtypeStruct((rows, feat), BF16),
            jax.ShapeDtypeStruct((feat, rows), BF16),
        ],
        compiler_params=params(),
        cost_estimate=BRIEF,
    )(o_t, w_proj, b_proj, x_view, mod_blocks)


def gelu_both(u):
    c = math.sqrt(2.0 / math.pi)
    square = u * u
    half = 0.5 + 0.5 * jnp.tanh(u * (c + (c * 0.044715) * square))
    g = u * half
    return g, half + (g - g * half) * (2.0 * c + (6.0 * c * 0.044715) * square)


def mlp_kernel(
    half_ref, a_ref, at_ref, df_ref, dg_ref, w1_ref, w2_ref, b1_ref, *refs, first, second
):
    f_ref, da_ref, db_ref = refs[:3]
    g_ref, du_ref = refs[-2:]
    outs = refs[3:-2]
    outs_one, outs_two = outs[: len(outs) // 2], outs[len(outs) // 2 :]
    step = pl.program_id(0)
    rows = a_ref.shape[0]

    @pl.when(step == 0)
    def _():
        f_ref[...] = jnp.zeros_like(f_ref)
        da_ref[...] = jnp.zeros_like(da_ref)

    w1, w2 = w1_ref[...], w2_ref[...]
    bias = jnp.zeros((1, w1.shape[1]), F32)
    cuts = [slice(r, r + BLK) for r in range(0, rows, BLK)]
    u = dot(a_ref[cuts[0], :], w1, 1, 0)
    for r, rs in enumerate(cuts):
        later = dot(a_ref[cuts[r + 1], :], w1, 1, 0) if r + 1 < len(cuts) else None
        g, slope = gelu_both(u + b1_ref[...])
        du = dg_ref[rs, :] * slope
        bias = bias + jnp.sum(du, axis=0, keepdims=True)
        g_ref[rs, :] = g.astype(BF16)
        du_ref[rs, :] = du.astype(BF16)
        u = later
        for past in cuts[r - 1 : r] if r + 1 < len(cuts) else cuts[max(r - 1, 0) :]:
            f_ref[past, :] += dot(g_ref[past, :], w2, 1, 0)
            da_ref[past, :] += dot(du_ref[past, :], w1, 1, 1)
    db_ref[...] = bias
    first.store(half_ref[0], dot(at_ref[...], du_ref[...], 1, 0), outs_one)
    second.store(half_ref[0], dot(g_ref[...], df_ref[...], 0, 0), outs_two)


def mlp(half, a2, a2_t, df, dg, w1, w2, b1, halves, width=512):
    rows, feat = a2.shape
    hidden = w1.shape[1]
    per = feat // width
    wide = halves.wide
    part = hidden // (2 * wide)
    first = halves
    second = Halves(wide, part)
    second.split = halves.split
    one = pl.Buffered(1)

    def fixed(*shape):
        return pl.BlockSpec(shape, lambda j: (0,) * len(shape), pipeline_mode=one)

    if halves.split:
        two_specs = [pl.BlockSpec((width // (2 * part), part, feat), lambda j: (j, 0, 0))] * 2
        two_shapes = [jax.ShapeDtypeStruct((wide, part, feat), BF16)] * 2
    else:
        two_specs = [pl.BlockSpec((width, feat), lambda j: (j, 0))]
        two_shapes = [jax.ShapeDtypeStruct((hidden, feat), BF16)]
    out = pl.pallas_call(
        functools.partial(mlp_kernel, first=first, second=second),
        grid=(hidden // width,),
        in_specs=[
            pl.BlockSpec(memory_space=pltpu.SMEM),
            fixed(rows, feat),
            fixed(feat, rows),
            fixed(rows, feat),
            pl.BlockSpec((rows, width), lambda j: (0, j)),
            pl.BlockSpec((feat, width), lambda j: (0, j)),
            pl.BlockSpec((width, feat), lambda j: (j, 0)),
            pl.BlockSpec((1, width), lambda j: (0, j)),
        ],
        out_specs=[whole(rows, feat), whole(rows, feat), pl.BlockSpec((1, width), lambda j: (0, j))]
        + halves.specs(1, width, lambda j: (j // per, j % per))
        + two_specs,
        out_shape=[
            jax.ShapeDtypeStruct((rows, feat), F32),
            jax.ShapeDtypeStruct((rows, feat), F32),
            jax.ShapeDtypeStruct((1, hidden), F32),
        ]
        + halves.shapes((hidden // feat,), feat)
        + two_shapes,
        scratch_shapes=[pltpu.VMEM((rows, width), BF16), pltpu.VMEM((rows, width), BF16)],
        compiler_params=params(),
        cost_estimate=BRIEF,
    )(half, a2, a2_t, df, dg, w1, w2, b1)
    f, da2, bias = out[:3]
    rest = out[3:]
    count = len(rest) // 2
    return f, da2, bias, first.finish(rest[:count]), second.finish(rest[count:])


def to_slot(ref, slot, slots, terms):
    @pl.when(slot >= 0)
    def _():
        for i, term in enumerate(terms):
            ref[pl.ds(2 * slots * i + slot, 1), :] += jnp.sum(term, axis=0, keepdims=True)


def middle_kernel(
    half_ref, seg_ref, f_ref, b2_ref, x1_ref, attn_ref, dy_ref, da_ref, mod_ref, o_ref, w_ref, act_ref,
    y_ref, dx_ref, do_ref, db_ref, sums_ref, *rest, halves,
):
    k = pl.program_id(0)
    outs, acc_ref, slot_ref = rest[:-2], rest[-2], rest[-1]
    slots = act_ref.shape[0]

    @pl.when(k == 0)
    def _():
        acc_ref[...] = jnp.zeros_like(acc_ref)
        db_ref[...] = jnp.zeros_like(db_ref)
        slot_ref[...] = jnp.zeros_like(slot_ref)
        slot_ref[slots : 2 * slots, :] = act_ref[...].astype(F32)

    f = f_ref[...] + b2_ref[...]
    x1 = x1_ref[...]
    dy = dy_ref[...].astype(F32)
    y_ref[...] = (x1 + mod_ref[0, 5:6, :] * f).astype(BF16)
    normed, inverse = norm_parts(x1)
    da = da_ref[...]
    dx1 = dy + norm_back(da * (1.0 + mod_ref[0, 4:5, :]), normed, inverse)
    dx_ref[...] = dx1
    dattn = (mod_ref[0, 2:3, :] * dx1).astype(BF16)
    db_ref[...] += jnp.sum(dattn.astype(F32), axis=0, keepdims=True)
    to_slot(slot_ref, seg_ref[k], slots, [dx1 * attn_ref[...], da, da * normed, dy * f])
    do_ref[...] = dot(w_ref[...], dattn, 1, 1).astype(BF16)
    acc_ref[...] += dot(o_ref[...], dattn, 1, 0)

    @pl.when(k == pl.num_programs(0) - 1)
    def _():
        halves.store(half_ref[0], acc_ref[...], outs)
        sums_ref[0] = slot_ref[...].astype(BF16)


def middle(half, seg, act, f, b2, x1, attn, dy, da2, mod_blocks, o_t, w_proj, halves):
    rows, feat = x1.shape
    by_row = pl.BlockSpec((BLK, feat), lambda k: (k, 0))
    by_column = pl.BlockSpec((feat, BLK), lambda k: (0, k))
    blocks = rows // BLK
    slots = act.shape[0]
    out = pl.pallas_call(
        functools.partial(middle_kernel, halves=halves),
        grid=(blocks,),
        in_specs=[
            pl.BlockSpec(memory_space=pltpu.SMEM),
            pl.BlockSpec(memory_space=pltpu.SMEM),
            by_row, whole(1, feat), by_row, by_row, by_row, by_row,
            pl.BlockSpec((1, 6, feat), lambda k: (k, 0, 0)),
            by_column, whole(feat, feat), whole(slots, feat),
        ],
        out_specs=[
            by_row, by_row, by_column, whole(1, feat),
            whole(1, 8 * slots, feat),
        ] + halves.specs(0, feat, lambda k: (0,)),
        out_shape=[
            jax.ShapeDtypeStruct((rows, feat), BF16),
            jax.ShapeDtypeStruct((rows, feat), F32),
            jax.ShapeDtypeStruct((feat, rows), BF16),
            jax.ShapeDtypeStruct((1, feat), F32),
            jax.ShapeDtypeStruct((1, 8 * slots, feat), BF16),
        ]
        + halves.shapes((), feat),
        scratch_shapes=[pltpu.VMEM((feat, feat), F32), pltpu.VMEM((8 * slots, feat), F32)],
        compiler_params=params(),
        cost_estimate=BRIEF,
    )(half, seg, f, b2, x1, attn, dy, da2, mod_blocks, o_t, w_proj, act)
    return tuple(out[:5]) + (halves.finish(out[5:]),)


def rows_back_kernel(seg_ref, w_ref, x_ref, dx_ref, mod_ref, bias_ref, *refs):
    out_ref, sums_ref, slot_ref = refs[-3:]
    slots = bias_ref.shape[0] // 2

    @pl.when(pl.program_id(0) == 0)
    def _():
        slot_ref[...] = jnp.zeros_like(slot_ref)
        slot_ref[slots : 2 * slots, :] = bias_ref[:slots, :]
        slot_ref[3 * slots :, :] = bias_ref[slots:, :]

    feat = x_ref.shape[-1]
    da = None
    for i in range(3):
        at = i * feat
        for ref in refs[:-3]:
            more = dot(ref[i], w_ref[at : at + ref.shape[1], :], 0, 0)
            da = more if da is None else da + more
            at += ref.shape[1]
    normed, inverse = norm_parts(x_ref[...].reshape(BLK, feat).astype(F32))
    out = dx_ref[...] + norm_back(da * (1.0 + mod_ref[0, 1:2, :]), normed, inverse)
    out_ref[...] = out.astype(BF16).reshape(out_ref.shape)
    to_slot(slot_ref, seg_ref[pl.program_id(0)], slots, [da, da * normed])
    sums_ref[0] = slot_ref[...].astype(BF16)


def rows_back(seg, dqkv, w_t, x_view, dx1, mod_blocks, biases):
    rows, feat = dx1.shape
    blocks = rows // BLK
    return pl.pallas_call(
        rows_back_kernel,
        grid=(blocks,),
        in_specs=[
            pl.BlockSpec(memory_space=pltpu.SMEM),
            whole(3 * feat, feat),
            row_spec(x_view.shape),
            pl.BlockSpec((BLK, feat), lambda k: (k, 0)),
            pl.BlockSpec((1, 6, feat), lambda k: (k, 0, 0)),
            whole(*biases.shape),
        ]
        + [pl.BlockSpec((3, d.shape[1], BLK), lambda k: (0, 0, k)) for d in dqkv],
        out_specs=[row_spec(x_view.shape), whole(1, 2 * biases.shape[0], feat)],
        out_shape=[
            jax.ShapeDtypeStruct(x_view.shape, BF16),
            jax.ShapeDtypeStruct((1, 2 * biases.shape[0], feat), BF16),
        ],
        scratch_shapes=[pltpu.VMEM((2 * biases.shape[0], feat), F32)],
        compiler_params=params(),
        cost_estimate=BRIEF,
    )(seg, w_t, x_view, dx1, mod_blocks, biases, *dqkv)


def mod_grad_kernel(
    ids_ref, dev_ref, spot_ref, one_ref, two_ref, w_ref, cond_ref,
    gw_ref, gb_ref, dcond_ref, bias_ref, act_ref, moved_ref, dact_ref, picked_ref, *, part, slots,
):
    @pl.loop(0, one_ref.shape[0])
    def _(p):
        moved_ref[p] = one_ref[dev_ref[p]]

    feat = one_ref.shape[-1]

    def columns(ref):
        wide = ref[...].astype(F32)
        wide = wide.reshape(wide.shape[0], -1, 2 * slots, feat)
        return [wide[:, i].reshape(-1, feat) for i in range(wide.shape[1])]

    one, two = columns(moved_ref), columns(two_ref)
    rows = one[0].shape[0]
    first = lax.broadcasted_iota(jnp.int32, (rows, 1), 0) % (2 * slots) < slots
    act_ref[...] = jnp.where(first, pltpu.roll(two[0], rows - slots, 0), 0.0).T
    act = act_ref[pl.ds(pl.multiple_of(ids_ref[1] * part, 8), part), :].astype(BF16)
    dact = None
    for i, values in enumerate(one + two):
        at = slice(i * feat, (i + 1) * feat)
        low = values.astype(BF16)
        gw_ref[:, at] = dot(act, low, 1, 0)
        gb_ref[:, at] = jnp.sum(jnp.where(first, values, 0.0), axis=0, keepdims=True)
        more = dot(low, w_ref[:, at], 1, 1)
        dact = more if dact is None else dact + more
    dact_ref[...] = dact

    @pl.loop(0, spot_ref.shape[0])
    def _(j):
        at = spot_ref[j]
        row = dact_ref[pl.ds(jnp.maximum(at, 0), 1), :]
        picked_ref[pl.ds(j, 1), :] = jnp.where(at >= 0, row, 0.0)

    cond = cond_ref[...].astype(F32)
    gate = 1.0 / (1.0 + jnp.exp(-cond))
    dcond_ref[...] = (picked_ref[...] * (gate * (1.0 + cond * (1.0 - gate)))).astype(BF16)
    for i, values in enumerate(one):
        sums = jnp.sum(values.reshape(-1, 2 * slots, feat), axis=0)
        bias_ref[i * slots : (i + 1) * slots, :] = sums[slots:, :]


def mod_grad(group, me, device_of, spot, one, two, w_mod, cond, part, slots):
    feat, columns = w_mod.shape
    places, share = cond.shape
    count = 2 * slots * one.shape[0]

    def fixed(*shape):
        return pl.BlockSpec(shape, lambda i, *scalars: (0,) * len(shape))

    return pl.pallas_call(
        functools.partial(mod_grad_kernel, part=part, slots=slots),
        grid_spec=pltpu.PrefetchScalarGridSpec(
            num_scalar_prefetch=3,
            grid=(1,),
            in_specs=[
                fixed(*one.shape),
                fixed(*two.shape),
                pl.BlockSpec((share, columns), lambda i, ids, *scalars: (ids[0], 0)),
                fixed(places, share),
            ],
            out_specs=[
                fixed(part, columns),
                fixed(1, columns),
                fixed(places, share),
                fixed(2 * slots, feat),
            ],
            scratch_shapes=[pltpu.VMEM((feat, count), F32), pltpu.VMEM(one.shape, BF16), pltpu.VMEM((count, share), F32), pltpu.VMEM((places, share), F32)],
        ),
        out_shape=[
            jax.ShapeDtypeStruct((part, columns), F32),
            jax.ShapeDtypeStruct((1, columns), F32),
            jax.ShapeDtypeStruct((places, share), BF16),
            jax.ShapeDtypeStruct((2 * slots, feat), F32),
        ],
        compiler_params=params(),
        cost_estimate=BRIEF,
    )(jnp.stack([group, me]), device_of, spot, one, two, w_mod, cond)


def swap(values, axis, bit):
    count = lax.axis_size(axis)
    return lax.ppermute(values, axis, [(i, i ^ bit) for i in range(count)])


def bits_of(wide):
    return [1 << i for i in range(wide.bit_length() - 1)]


def chain_orders(wide):
    bits = bits_of(wide)
    x, y, z = bits[:3]
    far, rest = bits[3:4], bits[4:]
    return [[x, y, *far, z, *rest], [y, z, x, *far, *rest], [z, x, y, *far, *rest]]


class Part:
    def __init__(self, keep, got, start, rows, order):
        self.keep, self.got, self.at = keep, got, start
        self.rows = rows
        self.fresh = True
        self.dims = list(reversed(bits_of(keep.shape[0])))
        self.order = list(order)


class Rider:
    def __init__(self, values, order):
        self.keep, self.got, self.at = values, None, 0
        self.rows = values.shape[1]
        self.fresh = True
        self.order, self.done = list(order), []

    def differences(self):
        return [sum(b for i, b in enumerate(self.done) if p >> i & 1) for p in range(1 << len(self.done))]

    def place(self, difference):
        at = jnp.zeros_like(difference)
        for i, bit in enumerate(self.done):
            at = at + ((difference // bit) % 2) * (1 << i)
        return at


def masks_of(bits):
    top = len(bits) - 1
    return [sum(b for i, b in enumerate(bits) if m >> (top - i) & 1) for m in range(1 << len(bits))]


def relay_kernel(me_ref, *refs, plan, inputs, outputs):
    ins, outs, scratch = refs[:inputs], refs[inputs : inputs + outputs], list(refs[inputs + outputs :])
    arriving = {}
    if scratch:
        sems = scratch.pop()
        for i, (kind, keep, got, at, rows, *_) in enumerate(plan):
            if kind == "fresh":
                for source in (keep, got):
                    k = len(arriving)
                    copy = pltpu.make_async_copy(
                        ins[source].at[:, pl.ds(at, rows), :], scratch[k], sems.at[k]
                    )
                    copy.start()
                    arriving[i, source == got] = (copy, scratch[k])
    for i, (kind, keep, got, at, rows, bit, inner, count, targets) in enumerate(plan):
        if kind == "ride":
            pieces = [ins[keep][0]]
            if got is not None:
                pieces.append(ins[got][at : at + rows, :])
            for out, base in targets:
                for k, piece in enumerate(pieces):
                    to = slice(base + k * rows, base + (k + 1) * rows)
                    if len(outs[out].shape) == 3:
                        outs[out][0, to, :] = piece
                    else:
                        outs[out][to, :] = piece
            continue
        if kind == "fresh":
            for copy, _ in (arriving[i, False], arriving[i, True]):
                copy.wait()
            k_ref, g_ref = arriving[i, False][1], arriving[i, True][1]
        else:
            k_ref, g_ref = ins[keep], None if bit is None else ins[got]
        if bit is None:
            total = k_ref[0].astype(F32)
            for source, first in zip(got, at, strict=True):
                total = total + ins[source][first : first + rows, :].astype(F32)
            outs[targets[0][0]][...] = total
            continue
        if isinstance(bit, tuple):
            top = len(bit) - 1
            own = sum(((me_ref[0] // b) % 2) << (top - k) for k, b in enumerate(bit))
            for m, (out, base) in enumerate(targets):
                right = g_ref[pl.ds(pl.multiple_of(at + (own ^ m) * rows, TILE), rows), :]
                if base is None:
                    outs[out][0] = k_ref[own ^ m] + right
                else:
                    outs[out][base : base + rows, :] = k_ref[own ^ m] + right
            continue
        own = (me_ref[0] // bit) % 2

        @pl.loop(0, count // 2)
        def _(e, kind=kind, at=at, own=own, rows=rows, inner=inner, k_ref=k_ref, g_ref=g_ref, targets=targets):
            outer = (e // inner) * 2 * inner + e % inner
            for which, (out, base) in zip((1 - own, own), targets, strict=True):
                entry = outer + which * inner
                if kind == "fresh":
                    right = g_ref[entry]
                else:
                    right = g_ref[pl.ds(pl.multiple_of(at + entry * rows, TILE), rows), :]
                total = k_ref[entry] + right
                if base is None:
                    outs[out][e] = total
                else:
                    outs[out][pl.ds(pl.multiple_of(base + e * rows, TILE), rows), :] = total


def relay(me, moving):
    arrays, places, plan, shapes, sends = [], [], [], [], {}
    columns = moving[0].keep.shape[2]
    vmem, hbm = pl.BlockSpec(memory_space=pltpu.VMEM), pl.BlockSpec(memory_space=pl.ANY)

    def index(array, place):
        if array is None:
            return None
        for i, known in enumerate(arrays):
            if known is array:
                return i
        arrays.append(array)
        places.append(place)
        return len(arrays) - 1

    bits = set()
    for m in moving:
        if m.order:
            bits.update(masks_of(m.order[0])[1:] if isinstance(m.order[0], tuple) else m.order[:1])
    bits = sorted(bits)
    sizes = dict.fromkeys(bits, 0)
    scratch, keeps = [], []
    for m in moving:
        bit = m.order[0] if m.order else None
        ride = isinstance(m, Rider)
        kind = "ride" if ride else "fresh" if m.fresh else "add"
        place = hbm if kind == "fresh" else vmem
        keep, at = index(m.keep, place), m.at
        several = isinstance(m.got, list)
        got = [index(g, place) for g in m.got] if several else index(m.got, place)
        rows, inner, count = m.rows, 1, 1
        fan = isinstance(bit, tuple)
        to = (bits.index(bit), sizes[bit]) if bit is not None and not fan else None
        kept = len(bits) + len(shapes)
        keeps.append(kept)
        if ride:
            m.rows *= 1 if got is None else 2
            shapes.append(jax.ShapeDtypeStruct((1, m.rows, columns), BF16))
            targets = [(kept, 0)] + ([] if to is None else [to])
            size = m.rows
        elif bit is None:
            shapes.append(jax.ShapeDtypeStruct((rows, columns), F32))
            targets, size = [(kept, 0)], 0
            got, at = (got, at) if several else ([got], [at])
        elif fan:
            shapes.append(jax.ShapeDtypeStruct((1, rows, columns), BF16))
            masks_here = masks_of(bit)[1:]
            m.at = [sizes[mask] for mask in masks_here]
            targets = [(kept, None)] + [(bits.index(mask), sizes[mask]) for mask in masks_here]
            for mask in masks_here:
                sizes[mask] += rows
            m.dims = []
        else:
            dim = m.dims.index(bit)
            count, inner = 1 << len(m.dims), 1 << (len(m.dims) - 1 - dim)
            m.dims.pop(dim)
            size = count // 2 * rows
            shapes.append(jax.ShapeDtypeStruct((count // 2, rows, columns), BF16))
            targets = [to, (kept, None)]
            if kind == "fresh":
                scratch += [pltpu.VMEM((count, rows, columns), BF16)] * 2
        plan.append((kind, keep, got, at, rows, bit, inner, count, targets))
        if bit is not None and not fan:
            m.at = sizes[bit]
            sizes[bit] += size
        m.fresh = False
    if scratch:
        scratch.append(pltpu.SemaphoreType.DMA((len(scratch),)))
    shapes = [jax.ShapeDtypeStruct((sizes[b], columns), BF16) for b in bits] + shapes
    out = pl.pallas_call(
        functools.partial(relay_kernel, plan=plan, inputs=len(arrays), outputs=len(shapes)),
        in_specs=[pl.BlockSpec(memory_space=pltpu.SMEM)] + places,
        out_specs=[vmem] * len(shapes),
        out_shape=shapes,
        scratch_shapes=scratch,
        compiler_params=params(),
        cost_estimate=BRIEF,
    )(me, *arrays)
    for m, kept in zip(moving, keeps, strict=True):
        m.keep = out[kept]
    return dict(zip(bits, out))


class Sums:
    def __init__(self, me):
        self.me, self.moving, self.going = me, [], {}

    def step(self, *joining, after=()):
        came = {bit: swap(send, "wide", bit) for bit, send in self.going.items()}
        if callable(after):
            after = after(came)
        if after:
            kept, _ = lax.optimization_barrier((tuple(m.keep for m in self.moving), tuple(after)))
            for m, array in zip(self.moving, kept, strict=True):
                m.keep = array
        going = [m for m in self.moving if m.order]
        for m in going:
            bit = m.order.pop(0)
            m.got = [came[mask] for mask in masks_of(bit)[1:]] if isinstance(bit, tuple) else came[bit]
            if isinstance(m, Rider):
                m.done.append(bit)
        self.moving += joining
        self.going = relay(self.me, going + list(joining))

    def arrays(self):
        return tuple(self.going.values()) + tuple(m.keep for m in self.moving)

    def put(self, arrays):
        count = len(self.going)
        self.going = dict(zip(self.going, arrays[:count], strict=True))
        for m, kept in zip(self.moving, arrays[count:], strict=True):
            m.keep = kept


def tie(values, moving):
    out = lax.optimization_barrier((tuple(values), tuple(m.arrays() for m in moving)))
    for one, kept in zip(moving, out[1], strict=True):
        one.put(kept)
    return out[0]


def local(
    x_src,
    cond,
    lengths,
    bucket,
    w_mod,
    b_mod,
    w_qkv,
    b_qv,
    w_proj,
    b_proj,
    w_fc1,
    b_fc1,
    w_fc2,
    b_fc2,
    grad_out,
):
    wide = lax.axis_size("wide")
    halves = lax.axis_size("narrow")
    devices = wide * halves
    group = lax.axis_index("wide")
    half = lax.axis_index("narrow")
    rows, feat = x_src.shape
    hidden = w_fc1.shape[1]
    places = lengths.shape[0] // halves
    slots = places // wide
    blocks = rows // BLK
    per_block = BLK // wide
    tiled = per_block % TILE == 0

    split = regroup if tiled else regroup_any
    send, scond, seg, src, cidx = split(x_src, cond, lengths, bucket, jnp.stack([group, half]), wide)
    exchange = functools.partial(
        lax.all_to_all, axis_name="wide", split_axis=0, concat_axis=0, tiled=True
    )
    came = exchange(send)
    came_cond = exchange(scond.reshape(wide, slots, feat // wide))
    cond_in = came_cond.transpose(1, 0, 2).reshape(slots, feat)
    x_view = came.reshape(wide, blocks, per_block, feat)
    if not tiled:
        x_view = x_view.transpose(1, 0, 2, 3).reshape(1, blocks, BLK, feat)

    act_low = jax.nn.silu(cond_in.astype(F32)).astype(BF16)
    modulate = jnp.dot(act_low, w_mod, preferred_element_type=F32) + b_mod.astype(F32)
    slot_ids = jnp.arange(slots, dtype=jnp.int32)
    in_slot = seg[:, None] == slot_ids[None, :]
    mod_blocks = jnp.sum(
        jnp.where(in_slot[:, :, None], modulate[None], 0.0), axis=1
    ).reshape(blocks, 6, feat)

    dy = (
        grad_out.reshape(blocks, per_block, wide, feat)
        .transpose(0, 2, 1, 3)
        .reshape(rows, feat)
    )
    gate_two = mod_blocks[:, 5:6, :]
    df = (
        (gate_two * dy.reshape(blocks, BLK, feat).astype(F32)).astype(BF16).reshape(rows, feat)
    )
    grad_b_fc2 = jnp.sum(df.astype(F32), axis=0)
    dg = dot(df, w_fc2, 1, 1)
    w_qkv_t = w_qkv.T
    bias_qkv = jnp.concatenate(
        [b_qv[:feat].astype(F32), jnp.zeros((feat,), F32), b_qv[feat:].astype(F32)]
    ).reshape(3 * feat, 1)

    qkv_t, a1_t = qkv_forward(x_view, mod_blocks, w_qkv_t, bias_qkv)
    o_t, lse = attend(seg, qkv_t)
    attn, x1, a2, a2_t = proj_forward(
        o_t, w_proj, b_proj.astype(F32).reshape(1, feat), x_view, mod_blocks
    )
    own, place = half.reshape(1), group.reshape(1)
    part = feat // devices
    halved = Halves(wide, part)
    both = ("wide", "narrow")
    orders = chain_orders(wide)
    near, far = bits_of(wide)[:3], bits_of(wide)[3:]
    sums = Sums(place)

    def shares(grad, got, cuts, ways):
        return [
            Part(grad[1], got, a, b - a, way)
            for a, b, way in zip(cuts[:-1], cuts[1:], ways, strict=True)
        ]

    def thirds(rows_of):
        third = -(-rows_of // 3 // TILE) * TILE
        return [0, third, min(2 * third, rows_of - TILE), rows_of]

    f, da2, grad_b_fc1, d_fc1, d_fc2 = mlp(
        own, a2, a2_t, df, dg, w_fc1, w_fc2, b_fc1.astype(F32).reshape(1, hidden), halved
    )

    if halved.split:
        fc2_got, fc1_got = swap(d_fc2[0], "narrow", 1), swap(d_fc1[0], "narrow", 1)
    y, dx1, do_t, grad_b_proj, two, d_proj = middle(
        own, seg, act_low, f, b_fc2.astype(F32).reshape(1, feat), x1, attn, dy, da2, mod_blocks, o_t,
        w_proj, halved,
    )
    y_dest = (
        y.reshape(blocks, wide, per_block, feat).transpose(0, 2, 1, 3).reshape(rows, feat)
    )
    pieces, row_sums, head = [], [], 0

    def attention(counts):
        nonlocal head
        for count in counts:
            piece, piece_sums = attend_back(
                seg, qkv_t, o_t, do_t, lse, first=head, count=count
            )
            pieces.append(piece)
            row_sums.append(piece_sums[:, 0])
            head += count

    def bias_rows():
        of_qv = jnp.concatenate(row_sums, axis=1)
        rows_of = [grad_b_fc1[0], grad_b_fc2, grad_b_proj[0], of_qv[0], of_qv[1]]
        return jnp.concatenate(rows_of).reshape(2 * slots, feat)

    ride_order = far + near[2:] + near[:2]
    if halved.split:
        proj_got = swap(d_proj[0], "narrow", 1)
        third = (d_fc2[1].shape[1] + d_fc1[1].shape[1] + part) // 3 // TILE * TILE
        fc2_parts = shares(d_fc2, fc2_got, [0, third, d_fc2[1].shape[1]], [orders[0], orders[2]])
        fc1_parts = shares(d_fc1, fc1_got, [0, third, d_fc1[1].shape[1]], [orders[1], orders[2]])
        proj_parts = shares(d_proj, proj_got, [0, part], orders[2:])
        two = Rider(two, ride_order)
        sums.step(*fc2_parts, *fc1_parts, *proj_parts, two)
        for counts in ((12,), (4,)):
            (do_t, *pieces) = tie((do_t, *pieces), [sums])
            attention(counts)
            sums.step()
        (a1_t, *pieces) = tie((a1_t, *pieces), [sums])
    else:
        attention((4, 4, 4, 4))
    d_qkv = qkv_grad(own, a1_t, pieces, halved)
    if halved.split:
        sums.step(after=d_qkv)
        qkv_got = swap(d_qkv[0], "narrow", 1)
        (dx1, *pieces) = tie((dx1, *pieces), [sums])
    drows, one = rows_back(seg, pieces, w_qkv_t, x_view, dx1, mod_blocks, bias_rows())
    if halved.split:
        sums.step()
        (drows,) = tie((drows,), [sums])
    back = drows
    if not tiled:
        back = back.reshape(blocks, wide, per_block, feat).transpose(1, 0, 2, 3)
    back = exchange(back.reshape(wide, rows // wide, feat))
    me = group * halves + half

    def modulation_grads(device_of, one_all, two_all):
        bucket_of, slot_of = jnp.maximum(cidx, 0) // slots, jnp.maximum(cidx, 0) % slots
        if halved.split:
            spot = two.place(bucket_of ^ group) * 2 * slots + slot_of
        else:
            spot = (bucket_of * halves + half) * 2 * slots + slot_of
        spot = jnp.where(cidx >= 0, spot, -1)
        return mod_grad(group, me, device_of, spot, one_all, two_all, w_mod, cond, part, slots)

    one_all = lax.all_gather(one, both, axis=0, tiled=True)
    if halved.split:
        last = tuple(reversed(near[2:] + far))
        flat, turned = [*near[:2], last], [*near[:2][::-1], last]
        qkv_parts = shares(
            d_qkv, qkv_got, [0, part, 2 * part, 2 * part + part // 2, 3 * part], [flat, turned, flat, turned]
        )
        sums = Sums(place)
        sums.step(*qkv_parts)
        tie((), [sums])
        sums.step()
        tie((), [sums])
        sums.step()
        (back,) = tie((back,), [sums])
        two_all = two.keep.reshape(wide, -1, feat)
        two_all = jnp.concatenate([two_all, swap(two_all, "narrow", 1)], axis=0)
        differs = jnp.asarray(two.differences(), jnp.int32)
        device_of = jnp.concatenate(
            [(differs ^ group) * halves + half, (differs ^ group) * halves + 1 - half]
        )
        held = {}

        def between(came):
            held["all"], came[near[2]] = lax.optimization_barrier((one_all, came[near[2]]))
            held["grads"] = modulation_grads(device_of, held["all"], two_all)
            return held["grads"][:1]

        sums.step(after=between)
        while sums.going:
            sums.step()
        modulation = held["grads"]
        grad_w_fc2 = jnp.concatenate([p.keep for p in fc2_parts], axis=0)
        grad_w_fc1 = jnp.concatenate([p.keep for p in fc1_parts], axis=0)
        grad_w_fc1 = (
            grad_w_fc1.reshape(hidden // feat, part, feat).transpose(1, 0, 2).reshape(part, hidden)
        )
        (grad_w_proj,) = (p.keep for p in proj_parts)

        kept = [p.keep for p in qkv_parts]
        grad_w_qkv = jnp.concatenate(kept[:2] + [jnp.concatenate(kept[2:], axis=0)], axis=1)
    else:
        two_all = lax.all_gather(two, both, axis=0, tiled=True)
        modulation = modulation_grads(jnp.arange(devices, dtype=jnp.int32), one_all, two_all)

        def scattered(full):
            return lax.psum_scatter(full, both, scatter_dimension=0, tiled=True).astype(F32)

        grad_w_fc2 = scattered(d_fc2[0])
        grad_w_fc1 = scattered(d_fc1[0].transpose(1, 0, 2).reshape(feat, hidden))
        grad_w_proj = scattered(d_proj[0])
        grad_w_qkv = scattered(d_qkv[0].transpose(1, 0, 2).reshape(feat, 3 * feat))
    merge = restore if tiled else restore_any
    dx_src = merge(src, back.reshape(rows, feat))

    grad_w_mod, grad_b_mod, dcond, biases = modulation
    grad_b_mod = lax.dynamic_slice_in_dim(grad_b_mod[0], me * 6 * part, 6 * part)

    def own_part(first, count):
        rows_of = biases[first : first + count].reshape(-1)
        share = rows_of.shape[0] // devices
        return lax.dynamic_slice_in_dim(rows_of, me * share, share)

    fc1_lines = hidden // feat
    s_fc1, s_fc2, s_proj = own_part(0, fc1_lines), own_part(fc1_lines, 1), own_part(fc1_lines + 1, 1)
    s_qv = own_part(fc1_lines + 2, 2)
    return (
        y_dest,
        dx_src,
        dcond,
        grad_w_mod,
        grad_b_mod,
        grad_w_qkv,
        s_qv,
        grad_w_proj,
        s_proj,
        grad_w_fc1,
        s_fc1,
        grad_w_fc2,
        s_fc2,
    )


def solution(mesh):
    both = ("wide", "narrow")
    placed = (P("narrow", "wide"), P("narrow", "wide")) + (P(),) * 12 + (P(both, None),)
    matrix, vector = P(both, None), P(both)
    return jax.shard_map(
        local,
        mesh=mesh,
        in_specs=placed,
        out_specs=(
            matrix,
            P("narrow", "wide"),
            P("narrow", "wide"),
            matrix,
            vector,
            matrix,
            vector,
            matrix,
            vector,
            matrix,
            vector,
            matrix,
            vector,
        ),
        check_vma=False,
    )
```

```python
import functools
import math

import jax
import jax.numpy as jnp
from jax import lax
from jax.experimental import pallas as pl
from jax.experimental.pallas import tpu as pltpu
from jax.sharding import PartitionSpec as P

HEADS = 16
HEAD_DIM = 64
EPS = 1e-06
MASKED = -1000000000.0
LOG2E = 1.4426950408889634
BLK = 256
TILE = 16
VMEM_LIMIT = 58 * 2**20
BRIEF = pl.CostEstimate(flops=1, bytes_accessed=1, transcendentals=0)
BF16 = jnp.bfloat16
F32 = jnp.float32


def params(**more):
    return pltpu.CompilerParams(vmem_limit_bytes=VMEM_LIMIT, **more)


def dot(left, right, left_dim, right_dim):
    return lax.dot_general(
        left, right, (((left_dim,), (right_dim,)), ((), ())), preferred_element_type=F32
    )


def norm_parts(values):
    centre = values - jnp.mean(values, axis=1, keepdims=True)
    spread = jnp.mean(centre * centre, axis=1, keepdims=True)
    inverse = lax.rsqrt(spread + EPS)
    return centre * inverse, inverse


def norm_back(grad, normed, inverse):
    return (
        grad
        - jnp.mean(grad, axis=1, keepdims=True)
        - normed * jnp.mean(grad * normed, axis=1, keepdims=True)
    ) * inverse


def each_place(len_ref, buck_ref, base, count, off_ref, slot_ref, wide, visit):
    for i in range(wide):
        off_ref[i] = 0
        slot_ref[i] = 0

    def place(j, offset):
        units = len_ref[base + j] // wide
        b = buck_ref[base + j]

        @pl.when(units > 0)
        def _():
            start = off_ref[b]
            slot = slot_ref[b]
            off_ref[b] = start + units
            slot_ref[b] = slot + 1
            visit(j, b, units, offset, start, slot)

        return offset + units

    lax.fori_loop(0, count, place, 0)


def regroup_rows_kernel(
    len_ref, buck_ref, me_ref, x_ref, send_ref, src_ref, off_ref, slot_ref, *, wide, places
):
    cells = send_ref.shape[1]
    send_ref[...] = jnp.zeros_like(send_ref)

    @pl.loop(0, src_ref.shape[0])
    def _(i):
        src_ref[i] = -1

    def visit(j, b, units, offset, start, slot):
        @pl.loop(0, units // TILE)
        def _(t):
            a = pl.multiple_of(offset + t * TILE, TILE)
            c = pl.multiple_of(start + t * TILE, TILE)
            send_ref[b, pl.ds(c, TILE), :] = x_ref[pl.ds(a, TILE), :]
            src_ref[a // TILE] = (b * cells + c) // TILE

    each_place(len_ref, buck_ref, me_ref[1] * places, places, off_ref, slot_ref, wide, visit)


def regroup_cond_kernel(
    len_ref, buck_ref, me_ref, cond_ref, scond_ref, seg_ref, cidx_ref,
    off_ref, slot_ref, cond_in, cond_out, *, wide, slots,
):
    cond_out[...] = jnp.zeros_like(cond_out)
    cond_in[...] = cond_ref[...].astype(F32)
    for i in range(seg_ref.shape[0]):
        seg_ref[i] = -1

    @pl.loop(0, cidx_ref.shape[0])
    def _(j):
        cidx_ref[j] = -1

    def visit(j, b, units, offset, start, slot):
        cidx_ref[j] = b * slots + slot
        cond_out[pl.ds(b * slots + slot, 1), :] = cond_in[pl.ds(j, 1), :]

        @pl.when(b == me_ref[0])
        def _():
            @pl.loop(0, units * wide // BLK)
            def _(t):
                seg_ref[start * wide // BLK + t] = slot

    places = cidx_ref.shape[0]
    each_place(len_ref, buck_ref, me_ref[1] * places, places, off_ref, slot_ref, wide, visit)
    scond_ref[...] = cond_out[...].astype(BF16)


def regroup(x_src, cond, lens, buck, me, wide):
    rows, feat = x_src.shape
    places, part = cond.shape
    slots = places // wide
    smem = pl.BlockSpec(memory_space=pltpu.SMEM)
    vmem = pl.BlockSpec(memory_space=pltpu.VMEM)
    counters = [pltpu.SMEM((wide,), jnp.int32), pltpu.SMEM((wide,), jnp.int32)]
    scond, seg, cidx = pl.pallas_call(
        functools.partial(regroup_cond_kernel, wide=wide, slots=slots),
        in_specs=[smem, smem, smem, vmem],
        out_specs=[vmem, smem, smem],
        out_shape=[
            jax.ShapeDtypeStruct((places, part), BF16),
            jax.ShapeDtypeStruct((rows // BLK,), jnp.int32),
            jax.ShapeDtypeStruct((places,), jnp.int32),
        ],
        scratch_shapes=counters + [pltpu.VMEM((places, part), F32), pltpu.VMEM((places, part), F32)],
        compiler_params=params(),
        cost_estimate=BRIEF,
    )(lens, buck, me, cond)
    send, src = pl.pallas_call(
        functools.partial(regroup_rows_kernel, wide=wide, places=places),
        in_specs=[smem, smem, smem, vmem],
        out_specs=[vmem, smem],
        out_shape=[
            jax.ShapeDtypeStruct((wide, rows // wide, feat), BF16),
            jax.ShapeDtypeStruct((rows // TILE,), jnp.int32),
        ],
        scratch_shapes=counters,
        compiler_params=params(),
        cost_estimate=BRIEF,
    )(lens, buck, me, x_src)
    return send, scond, seg, src, cidx


def restore_kernel(src_ref, back_ref, dx_ref):
    @pl.loop(0, src_ref.shape[0])
    def _(i):
        at = src_ref[i]
        rows = back_ref[pl.ds(pl.multiple_of(jnp.maximum(at, 0) * TILE, TILE), TILE), :]
        dx_ref[pl.ds(pl.multiple_of(i * TILE, TILE), TILE), :] = jnp.where(
            at >= 0, rows, jnp.zeros_like(rows)
        )


def restore(src, back):
    vmem = pl.BlockSpec(memory_space=pltpu.VMEM)
    return pl.pallas_call(
        restore_kernel,
        in_specs=[pl.BlockSpec(memory_space=pltpu.SMEM), vmem],
        out_specs=vmem,
        out_shape=jax.ShapeDtypeStruct(back.shape, BF16),
        compiler_params=params(),
        cost_estimate=BRIEF,
    )(src, back)


def regroup_any(x_src, cond, lens, buck, me, wide):
    rows, feat = x_src.shape
    places = cond.shape[0]
    lens = lax.dynamic_slice_in_dim(lens, me[1] * places, places)
    buck = lax.dynamic_slice_in_dim(buck, me[1] * places, places)
    slots, cells = places // wide, rows // wide
    units = lens // wide
    order = jnp.arange(places, dtype=jnp.int32)
    earlier = (order[:, None] < order[None, :]) & (buck[:, None] == buck[None, :])
    live = (lens > 0).astype(jnp.int32)
    offset = jnp.cumsum(units) - units
    start = jnp.sum(jnp.where(earlier, units[:, None], 0), axis=0)
    slot = jnp.sum(jnp.where(earlier, live[:, None], 0), axis=0)
    cell = jnp.arange(cells, dtype=jnp.int32)[None, :, None]
    to_target = (buck[None, :] == jnp.arange(wide, dtype=jnp.int32)[:, None]) & (live[None, :] > 0)
    hit = (
        to_target[:, None, :]
        & (cell >= start[None, None, :])
        & (cell < (start + units)[None, None, :])
    ).astype(jnp.int32)
    valid = jnp.sum(hit, axis=2)
    source = jnp.sum(hit * (offset - start)[None, None, :], axis=2) + cell[:, :, 0]
    source = jnp.where(valid > 0, source, 0)
    picked = jnp.take(x_src, source.reshape(-1), axis=0).reshape(wide, cells, feat)
    send = jnp.where(valid[:, :, None] > 0, picked, jnp.zeros((), BF16))
    cond_hit = to_target[:, None, :] & (
        slot[None, None, :] == jnp.arange(slots, dtype=jnp.int32)[None, :, None]
    )
    scond = jnp.einsum("wqs,sf->wqf", cond_hit.astype(BF16), cond, preferred_element_type=F32)
    scond = scond.astype(BF16).reshape(cond.shape)
    first = jnp.arange(rows // BLK, dtype=jnp.int32)[:, None] * BLK
    mine = (
        ((buck == me[0]) & (live > 0))[None, :]
        & (first >= (start * wide)[None, :])
        & (first < ((start + units) * wide)[None, :])
    )
    seg = jnp.sum(jnp.where(mine, slot[None, :] + 1, 0), axis=1) - 1
    spot = jnp.arange(rows, dtype=jnp.int32)[:, None]
    inside = (live[None, :] > 0) & (spot >= offset[None, :]) & (spot < (offset + units)[None, :])
    src = jnp.sum(jnp.where(inside, (buck * cells + start - offset)[None, :] + spot + 1, 0), axis=1)
    cidx = jnp.where(live > 0, buck * slots + slot, -1)
    return send, scond, seg.astype(jnp.int32), src - 1, cidx


def restore_any(src, back):
    dx = jnp.take(back, jnp.maximum(src, 0), axis=0)
    return jnp.where(src[:, None] >= 0, dx, jnp.zeros((), BF16))


def qkv_kernel(x_ref, mod_ref, w_ref, b_ref, q_ref, a_ref):
    feat = x_ref.shape[-1]
    x = x_ref[...].reshape(BLK, feat).astype(F32)
    normed, _ = norm_parts(x)
    a1 = (normed * (1.0 + mod_ref[0, 1:2, :]) + mod_ref[0, 0:1, :]).astype(BF16)
    a_ref[...] = a1.T
    for i in range(3):
        part = slice(i * feat, (i + 1) * feat)
        q_ref[part, :] = (dot(a1, w_ref[:, part], 1, 0) + b_ref[:, part]).astype(BF16).T


def row_spec(view):
    return pl.BlockSpec((view[0], 1, view[2], view[3]), lambda k: (0, k, 0, 0))


def whole(*shape):
    return pl.BlockSpec(shape, lambda k: (0,) * len(shape))


def qkv_forward(x_view, mod_blocks, w_t, bias):
    feat = x_view.shape[-1]
    blocks = x_view.shape[1]
    return pl.pallas_call(
        qkv_kernel,
        grid=(blocks,),
        in_specs=[
            row_spec(x_view.shape),
            pl.BlockSpec((1, 6, feat), lambda k: (k, 0, 0)),
            whole(feat, 3 * feat),
            whole(1, 3 * feat),
        ],
        out_specs=[
            pl.BlockSpec((3 * feat, BLK), lambda k: (0, k)),
            pl.BlockSpec((feat, BLK), lambda k: (0, k)),
        ],
        out_shape=[
            jax.ShapeDtypeStruct((3 * feat, blocks * BLK), BF16),
            jax.ShapeDtypeStruct((feat, blocks * BLK), BF16),
        ],
        compiler_params=params(),
        cost_estimate=BRIEF,
    )(x_view, mod_blocks, w_t, bias)


def masks(seg_ref, query_block, blocks):
    base = LOG2E / math.sqrt(HEAD_DIM)
    same = [seg_ref[query_block] == seg_ref[kb] for kb in range(blocks)]
    scales = [jnp.where(s, base, 0.0) for s in same]
    shifts = [jnp.where(s, 0.0, MASKED * LOG2E) for s in same]
    return scales, shifts


def attend_kernel(seg_ref, q_ref, k_ref, v_ref, o_ref, lse_ref, *, blocks, heads):
    units = [(h, qb) for h in range(heads) for qb in range(blocks)]
    keys = [k_ref[h * HEAD_DIM : (h + 1) * HEAD_DIM, :].T for h in range(heads)]

    def spans(h, qb):
        return slice(h * HEAD_DIM, (h + 1) * HEAD_DIM), slice(qb * BLK, (qb + 1) * BLK)

    def scores_of(h, qb):
        q_t = q_ref[spans(h, qb)]
        return [dot(keys[h][kb * BLK : (kb + 1) * BLK], q_t, 1, 0) for kb in range(blocks)]

    def finish(h, qb, probs, total, top):
        hs, qs = spans(h, qb)
        out = dot(v_ref[hs, :], probs, 1, 0)
        o_ref[hs, qs] = (out / total).astype(BF16)
        lse_ref[h, :, qs] = top + jnp.log2(total)

    ahead, behind = scores_of(*units[0]), None
    for i, (h, qb) in enumerate(units):
        scores, ahead = ahead, scores_of(*units[i + 1]) if i + 1 < len(units) else None
        scales, shifts = masks(seg_ref, qb, blocks)
        top = None
        for kb in range(blocks):
            peak = jnp.max(scores[kb], axis=0, keepdims=True) * scales[kb] + shifts[kb]
            top = peak if top is None else jnp.maximum(top, peak)
        if behind is not None:
            finish(*behind)
        total = jnp.zeros((1, BLK), F32)
        parts = []
        for kb in range(blocks):
            expo = jnp.exp2(scores[kb] * scales[kb] - (top - shifts[kb]))
            total = total + jnp.sum(expo, axis=0, keepdims=True)
            parts.append(expo.astype(BF16))
        behind = (h, qb, jnp.concatenate(parts, axis=0), total, top)
    finish(*behind)


def attend(seg, qkv_t, heads=4):
    feat3, rows = qkv_t.shape
    feat = feat3 // 3
    span = heads * HEAD_DIM
    groups = feat // span
    return pl.pallas_call(
        functools.partial(attend_kernel, blocks=rows // BLK, heads=heads),
        grid_spec=pltpu.PrefetchScalarGridSpec(
            num_scalar_prefetch=1,
            grid=(groups,),
            in_specs=[
                pl.BlockSpec((span, rows), lambda g, s: (g, 0)),
                pl.BlockSpec((span, rows), lambda g, s: (groups + g, 0)),
                pl.BlockSpec((span, rows), lambda g, s: (2 * groups + g, 0)),
            ],
            out_specs=[
                pl.BlockSpec((span, rows), lambda g, s: (g, 0)),
                pl.BlockSpec((heads, 1, rows), lambda g, s: (g, 0, 0)),
            ],
        ),
        out_shape=[
            jax.ShapeDtypeStruct((feat, rows), BF16),
            jax.ShapeDtypeStruct((feat // HEAD_DIM, 1, rows), F32),
        ],
        compiler_params=params(),
        cost_estimate=BRIEF,
    )(seg, qkv_t, qkv_t, qkv_t)


def attend_back_kernel(
    seg_ref, q_ref, k_ref, v_ref, o_ref, do_ref, lse_ref, out_ref, sums_ref, *, blocks, heads
):
    scale = 1.0 / math.sqrt(HEAD_DIM)
    units = [(h, qb) for h in range(heads) for qb in range(blocks)]
    keys = [k_ref[h * HEAD_DIM : (h + 1) * HEAD_DIM, :].T for h in range(heads)]
    values = [v_ref[h * HEAD_DIM : (h + 1) * HEAD_DIM, :].T for h in range(heads)]

    def spans(h, qb):
        return slice(h * HEAD_DIM, (h + 1) * HEAD_DIM), slice(qb * BLK, (qb + 1) * BLK)

    def products(h, qb):
        q_t, do_t = q_ref[spans(h, qb)], do_ref[spans(h, qb)]
        cuts = [slice(kb * BLK, (kb + 1) * BLK) for kb in range(blocks)]
        return [(dot(keys[h][c], q_t, 1, 0), dot(values[h][c], do_t, 1, 0)) for c in cuts]

    ahead = products(*units[0])
    grad_k = grad_v = inner = None
    for i, (h, qb) in enumerate(units):
        present, ahead = ahead, products(*units[i + 1]) if i + 1 < len(units) else None
        hs, qs = spans(h, qb)
        if qb == 0:
            inner = jnp.sum(
                o_ref[hs, :].astype(F32) * do_ref[hs, :].astype(F32), axis=0, keepdims=True
            )
        scales, shifts = masks(seg_ref, qb, blocks)
        probs, grads = [], []
        for kb, (score, grad_p) in enumerate(present):
            prob = jnp.exp2(score * scales[kb] - (lse_ref[h, :, qs] - shifts[kb]))
            probs.append(prob.astype(BF16))
            grads.append((prob * (grad_p - inner[:, qs])).astype(BF16))
        probs = jnp.concatenate(probs, axis=0)
        grads = jnp.concatenate(grads, axis=0)
        out_ref[0, hs, qs] = (dot(k_ref[hs, :], grads, 1, 0) * scale).astype(BF16)
        more_k, more_v = dot(q_ref[hs, qs], grads, 1, 1), dot(do_ref[hs, qs], probs, 1, 1)
        grad_k = more_k if qb == 0 else grad_k + more_k
        grad_v = more_v if qb == 0 else grad_v + more_v
        if qb == blocks - 1:
            out_ref[1, hs, :] = (grad_k * scale).astype(BF16)
            out_ref[2, hs, :] = grad_v.astype(BF16)
    ones = jnp.ones((8, out_ref.shape[2]), BF16)
    sums_ref[0] = dot(ones, out_ref[0], 1, 1)
    sums_ref[1] = dot(ones, out_ref[2], 1, 1)


def attend_back(seg, qkv_t, o_t, do_t, lse, first, count, heads=2):
    feat3, rows = qkv_t.shape
    feat = feat3 // 3
    span = heads * HEAD_DIM
    groups = feat // span
    at = first // heads
    return pl.pallas_call(
        functools.partial(attend_back_kernel, blocks=rows // BLK, heads=heads),
        grid_spec=pltpu.PrefetchScalarGridSpec(
            num_scalar_prefetch=1,
            grid=(count // heads,),
            in_specs=[
                pl.BlockSpec((span, rows), lambda g, s: (at + g, 0)),
                pl.BlockSpec((span, rows), lambda g, s: (groups + at + g, 0)),
                pl.BlockSpec((span, rows), lambda g, s: (2 * groups + at + g, 0)),
                pl.BlockSpec((span, rows), lambda g, s: (at + g, 0)),
                pl.BlockSpec((span, rows), lambda g, s: (at + g, 0)),
                pl.BlockSpec((heads, 1, rows), lambda g, s: (at + g, 0, 0)),
            ],
            out_specs=[
                pl.BlockSpec((3, span, rows), lambda g, s: (0, g, 0)),
                pl.BlockSpec((2, 8, span), lambda g, s: (0, 0, g)),
            ],
        ),
        out_shape=[
            jax.ShapeDtypeStruct((3, count * HEAD_DIM, rows), BF16),
            jax.ShapeDtypeStruct((2, 8, count * HEAD_DIM), F32),
        ],
        compiler_params=params(),
        cost_estimate=BRIEF,
    )(seg, qkv_t, qkv_t, qkv_t, o_t, do_t, lse)


class Halves:
    def __init__(self, wide, part, split=None):
        self.wide, self.part = wide, part
        self.split = part % TILE == 0 if split is None else split

    def shapes(self, between, columns):
        if self.split:
            shape = (self.wide,) + between + (self.part, columns)
            return [jax.ShapeDtypeStruct(shape, BF16)] * 2
        return [jax.ShapeDtypeStruct(between + (2 * self.wide * self.part, columns), BF16)]

    def specs(self, between, columns, index):
        ones = (1,) * between
        if self.split:
            return [
                pl.BlockSpec(
                    (self.wide,) + ones + (self.part, columns),
                    lambda *g: (0,) + index(*g)[:-1] + (0, index(*g)[-1]),
                )
            ] * 2
        return [
            pl.BlockSpec(
                ones + (2 * self.wide * self.part, columns),
                lambda *g: index(*g)[:-1] + (0, index(*g)[-1]),
            )
        ]

    def store(self, half, value, refs):
        if not self.split:
            refs[0][...] = value.astype(BF16).reshape(refs[0].shape)
            return
        value = value.reshape(value.shape[0] // (2 * self.part), 2, self.part, value.shape[1])
        even, odd = value[:, 0], value[:, 1]
        folds = refs[0].shape[-1] // value.shape[-1]
        if folds > 1:
            even, odd = (
                jnp.concatenate(jnp.split(half_value, folds, axis=1), axis=2) for half_value in (even, odd)
            )
        refs[0][...] = jnp.where(half == 0, odd, even).astype(BF16).reshape(refs[0].shape)
        refs[1][...] = jnp.where(half == 0, even, odd).astype(BF16).reshape(refs[1].shape)

    def finish(self, arrays):
        if self.split:
            return [a.reshape(self.wide, -1, a.shape[-1]) for a in arrays]
        return arrays


def qkv_grad_kernel(half_ref, a_ref, *refs, pieces, halves):
    ins, outs = refs[:pieces], refs[pieces:]
    value = jnp.concatenate([dot(a_ref[...], r[0], 1, 1) for r in ins], axis=1)
    halves.store(half_ref[0], value, outs)


def qkv_grad(half, a1_t, dqkv, halves):
    feat, rows = a1_t.shape
    columns = sum(d.shape[1] for d in dqkv)
    folds = feat // columns if halves.split else 1
    packed = Halves(halves.wide, halves.part // folds, halves.split)
    packed_columns = folds * columns
    out = pl.pallas_call(
        functools.partial(qkv_grad_kernel, pieces=len(dqkv), halves=halves),
        grid=(3,),
        in_specs=[pl.BlockSpec(memory_space=pltpu.SMEM), whole(feat, rows)]
        + [pl.BlockSpec((1, d.shape[1], rows), lambda i: (i, 0, 0)) for d in dqkv],
        out_specs=packed.specs(1, packed_columns, lambda i: (i, 0)),
        out_shape=packed.shapes((3,), packed_columns),
        compiler_params=params(),
        cost_estimate=BRIEF,
    )(half, a1_t, *dqkv)
    return halves.finish(out)


def proj_kernel(o_ref, w_ref, b_ref, x_ref, mod_ref, attn_ref, x1_ref, a_ref, at_ref):
    feat = x_ref.shape[-1]
    attn = dot(o_ref[...], w_ref[...], 0, 0) + b_ref[...]
    attn_ref[...] = attn
    x1 = x_ref[...].reshape(BLK, feat).astype(F32) + mod_ref[0, 2:3, :] * attn
    x1_ref[...] = x1
    normed, _ = norm_parts(x1)
    a2 = (normed * (1.0 + mod_ref[0, 4:5, :]) + mod_ref[0, 3:4, :]).astype(BF16)
    a_ref[...] = a2
    at_ref[...] = a2.T


def proj_forward(o_t, w_proj, b_proj, x_view, mod_blocks):
    feat = x_view.shape[-1]
    blocks = x_view.shape[1]
    rows = blocks * BLK
    by_row = pl.BlockSpec((BLK, feat), lambda k: (k, 0))
    by_column = pl.BlockSpec((feat, BLK), lambda k: (0, k))
    return pl.pallas_call(
        proj_kernel,
        grid=(blocks,),
        in_specs=[
            by_column,
            whole(feat, feat),
            whole(1, feat),
            row_spec(x_view.shape),
            pl.BlockSpec((1, 6, feat), lambda k: (k, 0, 0)),
        ],
        out_specs=[by_row, by_row, by_row, by_column],
        out_shape=[
            jax.ShapeDtypeStruct((rows, feat), F32),
            jax.ShapeDtypeStruct((rows, feat), F32),
            jax.ShapeDtypeStruct((rows, feat), BF16),
            jax.ShapeDtypeStruct((feat, rows), BF16),
        ],
        compiler_params=params(),
        cost_estimate=BRIEF,
    )(o_t, w_proj, b_proj, x_view, mod_blocks)


def gelu_both(u):
    c = math.sqrt(2.0 / math.pi)
    square = u * u
    half = 0.5 + 0.5 * jnp.tanh(u * (c + (c * 0.044715) * square))
    g = u * half
    return g, half + (g - g * half) * (2.0 * c + (6.0 * c * 0.044715) * square)


def mlp_kernel(
    half_ref, a_ref, at_ref, df_ref, dg_ref, w1_ref, w2_ref, b1_ref, *refs, first, second
):
    f_ref, da_ref, db_ref = refs[:3]
    g_ref, du_ref = refs[-2:]
    outs = refs[3:-2]
    outs_one, outs_two = outs[: len(outs) // 2], outs[len(outs) // 2 :]
    step = pl.program_id(0)
    rows = a_ref.shape[0]

    @pl.when(step == 0)
    def _():
        f_ref[...] = jnp.zeros_like(f_ref)
        da_ref[...] = jnp.zeros_like(da_ref)

    w1, w2 = w1_ref[...], w2_ref[...]
    bias = jnp.zeros((1, w1.shape[1]), F32)
    cuts = [slice(r, r + BLK) for r in range(0, rows, BLK)]
    u = dot(a_ref[cuts[0], :], w1, 1, 0)
    for r, rs in enumerate(cuts):
        later = dot(a_ref[cuts[r + 1], :], w1, 1, 0) if r + 1 < len(cuts) else None
        g, slope = gelu_both(u + b1_ref[...])
        du = dg_ref[rs, :] * slope
        bias = bias + jnp.sum(du, axis=0, keepdims=True)
        g_ref[rs, :] = g.astype(BF16)
        du_ref[rs, :] = du.astype(BF16)
        u = later
        for past in cuts[r - 1 : r] if r + 1 < len(cuts) else cuts[max(r - 1, 0) :]:
            f_ref[past, :] += dot(g_ref[past, :], w2, 1, 0)
            da_ref[past, :] += dot(du_ref[past, :], w1, 1, 1)
    db_ref[...] = bias
    first.store(half_ref[0], dot(at_ref[...], du_ref[...], 1, 0), outs_one)
    second.store(half_ref[0], dot(g_ref[...], df_ref[...], 0, 0), outs_two)


def mlp(half, a2, a2_t, df, dg, w1, w2, b1, halves, width=512):
    rows, feat = a2.shape
    hidden = w1.shape[1]
    per = feat // width
    wide = halves.wide
    part = hidden // (2 * wide)
    first = halves
    second = Halves(wide, part)
    second.split = halves.split
    one = pl.Buffered(1)

    def fixed(*shape):
        return pl.BlockSpec(shape, lambda j: (0,) * len(shape), pipeline_mode=one)

    if halves.split:
        two_specs = [pl.BlockSpec((width // (2 * part), part, feat), lambda j: (j, 0, 0))] * 2
        two_shapes = [jax.ShapeDtypeStruct((wide, part, feat), BF16)] * 2
    else:
        two_specs = [pl.BlockSpec((width, feat), lambda j: (j, 0))]
        two_shapes = [jax.ShapeDtypeStruct((hidden, feat), BF16)]
    out = pl.pallas_call(
        functools.partial(mlp_kernel, first=first, second=second),
        grid=(hidden // width,),
        in_specs=[
            pl.BlockSpec(memory_space=pltpu.SMEM),
            fixed(rows, feat),
            fixed(feat, rows),
            fixed(rows, feat),
            pl.BlockSpec((rows, width), lambda j: (0, j)),
            pl.BlockSpec((feat, width), lambda j: (0, j)),
            pl.BlockSpec((width, feat), lambda j: (j, 0)),
            pl.BlockSpec((1, width), lambda j: (0, j)),
        ],
        out_specs=[whole(rows, feat), whole(rows, feat), pl.BlockSpec((1, width), lambda j: (0, j))]
        + halves.specs(1, width, lambda j: (j // per, j % per))
        + two_specs,
        out_shape=[
            jax.ShapeDtypeStruct((rows, feat), F32),
            jax.ShapeDtypeStruct((rows, feat), F32),
            jax.ShapeDtypeStruct((1, hidden), F32),
        ]
        + halves.shapes((hidden // feat,), feat)
        + two_shapes,
        scratch_shapes=[pltpu.VMEM((rows, width), BF16), pltpu.VMEM((rows, width), BF16)],
        compiler_params=params(),
        cost_estimate=BRIEF,
    )(half, a2, a2_t, df, dg, w1, w2, b1)
    f, da2, bias = out[:3]
    rest = out[3:]
    count = len(rest) // 2
    return f, da2, bias, first.finish(rest[:count]), second.finish(rest[count:])


def to_slot(ref, slot, slots, terms):
    @pl.when(slot >= 0)
    def _():
        for i, term in enumerate(terms):
            ref[pl.ds(2 * slots * i + slot, 1), :] += jnp.sum(term, axis=0, keepdims=True)


def middle_kernel(
    half_ref, seg_ref, f_ref, b2_ref, x1_ref, attn_ref, dy_ref, da_ref, mod_ref, o_ref, w_ref, act_ref,
    y_ref, dx_ref, do_ref, db_ref, sums_ref, *rest, halves,
):
    k = pl.program_id(0)
    outs, acc_ref, slot_ref = rest[:-2], rest[-2], rest[-1]
    slots = act_ref.shape[0]

    @pl.when(k == 0)
    def _():
        acc_ref[...] = jnp.zeros_like(acc_ref)
        db_ref[...] = jnp.zeros_like(db_ref)
        slot_ref[...] = jnp.zeros_like(slot_ref)
        slot_ref[slots : 2 * slots, :] = act_ref[...].astype(F32)

    f = f_ref[...] + b2_ref[...]
    x1 = x1_ref[...]
    dy = dy_ref[...].astype(F32)
    y_ref[...] = (x1 + mod_ref[0, 5:6, :] * f).astype(BF16)
    normed, inverse = norm_parts(x1)
    da = da_ref[...]
    dx1 = dy + norm_back(da * (1.0 + mod_ref[0, 4:5, :]), normed, inverse)
    dx_ref[...] = dx1
    dattn = (mod_ref[0, 2:3, :] * dx1).astype(BF16)
    db_ref[...] += jnp.sum(dattn.astype(F32), axis=0, keepdims=True)
    to_slot(slot_ref, seg_ref[k], slots, [dx1 * attn_ref[...], da, da * normed, dy * f])
    do_ref[...] = dot(w_ref[...], dattn, 1, 1).astype(BF16)
    acc_ref[...] += dot(o_ref[...], dattn, 1, 0)

    @pl.when(k == pl.num_programs(0) - 1)
    def _():
        halves.store(half_ref[0], acc_ref[...], outs)
        sums_ref[0] = slot_ref[...].astype(BF16)


def middle(half, seg, act, f, b2, x1, attn, dy, da2, mod_blocks, o_t, w_proj, halves):
    rows, feat = x1.shape
    by_row = pl.BlockSpec((BLK, feat), lambda k: (k, 0))
    by_column = pl.BlockSpec((feat, BLK), lambda k: (0, k))
    blocks = rows // BLK
    slots = act.shape[0]
    out = pl.pallas_call(
        functools.partial(middle_kernel, halves=halves),
        grid=(blocks,),
        in_specs=[
            pl.BlockSpec(memory_space=pltpu.SMEM),
            pl.BlockSpec(memory_space=pltpu.SMEM),
            by_row, whole(1, feat), by_row, by_row, by_row, by_row,
            pl.BlockSpec((1, 6, feat), lambda k: (k, 0, 0)),
            by_column, whole(feat, feat), whole(slots, feat),
        ],
        out_specs=[
            by_row, by_row, by_column, whole(1, feat),
            whole(1, 8 * slots, feat),
        ] + halves.specs(0, feat, lambda k: (0,)),
        out_shape=[
            jax.ShapeDtypeStruct((rows, feat), BF16),
            jax.ShapeDtypeStruct((rows, feat), F32),
            jax.ShapeDtypeStruct((feat, rows), BF16),
            jax.ShapeDtypeStruct((1, feat), F32),
            jax.ShapeDtypeStruct((1, 8 * slots, feat), BF16),
        ]
        + halves.shapes((), feat),
        scratch_shapes=[pltpu.VMEM((feat, feat), F32), pltpu.VMEM((8 * slots, feat), F32)],
        compiler_params=params(),
        cost_estimate=BRIEF,
    )(half, seg, f, b2, x1, attn, dy, da2, mod_blocks, o_t, w_proj, act)
    return tuple(out[:5]) + (halves.finish(out[5:]),)


def rows_back_kernel(seg_ref, w_ref, x_ref, dx_ref, mod_ref, bias_ref, *refs):
    out_ref, sums_ref, slot_ref = refs[-3:]
    slots = bias_ref.shape[0] // 2

    @pl.when(pl.program_id(0) == 0)
    def _():
        slot_ref[...] = jnp.zeros_like(slot_ref)
        slot_ref[slots : 2 * slots, :] = bias_ref[:slots, :]
        slot_ref[3 * slots :, :] = bias_ref[slots:, :]

    feat = x_ref.shape[-1]
    da = None
    for i in range(3):
        at = i * feat
        for ref in refs[:-3]:
            more = dot(ref[i], w_ref[:, at : at + ref.shape[1]], 0, 1)
            da = more if da is None else da + more
            at += ref.shape[1]
    normed, inverse = norm_parts(x_ref[...].reshape(BLK, feat).astype(F32))
    out = dx_ref[...] + norm_back(da * (1.0 + mod_ref[0, 1:2, :]), normed, inverse)
    out_ref[...] = out.astype(BF16).reshape(out_ref.shape)
    to_slot(slot_ref, seg_ref[pl.program_id(0)], slots, [da, da * normed])
    sums_ref[0] = slot_ref[...].astype(BF16)


def rows_back(seg, dqkv, w_t, x_view, dx1, mod_blocks, biases):
    rows, feat = dx1.shape
    blocks = rows // BLK
    return pl.pallas_call(
        rows_back_kernel,
        grid=(blocks,),
        in_specs=[
            pl.BlockSpec(memory_space=pltpu.SMEM),
            whole(feat, 3 * feat),
            row_spec(x_view.shape),
            pl.BlockSpec((BLK, feat), lambda k: (k, 0)),
            pl.BlockSpec((1, 6, feat), lambda k: (k, 0, 0)),
            whole(*biases.shape),
        ]
        + [pl.BlockSpec((3, d.shape[1], BLK), lambda k: (0, 0, k)) for d in dqkv],
        out_specs=[row_spec(x_view.shape), whole(1, 2 * biases.shape[0], feat)],
        out_shape=[
            jax.ShapeDtypeStruct(x_view.shape, BF16),
            jax.ShapeDtypeStruct((1, 2 * biases.shape[0], feat), BF16),
        ],
        scratch_shapes=[pltpu.VMEM((2 * biases.shape[0], feat), F32)],
        compiler_params=params(),
        cost_estimate=BRIEF,
    )(seg, w_t, x_view, dx1, mod_blocks, biases, *dqkv)


def mod_grad_kernel(
    ids_ref, dev_ref, spot_ref, one_ref, two_ref, w_ref, cond_ref,
    gw_ref, gb_ref, dcond_ref, bias_ref, act_ref, moved_ref, dact_ref, picked_ref, *, part, slots,
):
    @pl.loop(0, one_ref.shape[0])
    def _(p):
        moved_ref[p] = one_ref[dev_ref[p]]

    feat = one_ref.shape[-1]

    def columns(ref):
        wide = ref[...].astype(F32)
        wide = wide.reshape(wide.shape[0], -1, 2 * slots, feat)
        return [wide[:, i].reshape(-1, feat) for i in range(wide.shape[1])]

    one, two = columns(moved_ref), columns(two_ref)
    rows = one[0].shape[0]
    first = lax.broadcasted_iota(jnp.int32, (rows, 1), 0) % (2 * slots) < slots
    act_ref[...] = jnp.where(first, pltpu.roll(two[0], rows - slots, 0), 0.0).T
    act = act_ref[pl.ds(pl.multiple_of(ids_ref[1] * part, 8), part), :].astype(BF16)
    dact = None
    for i, values in enumerate(one + two):
        at = slice(i * feat, (i + 1) * feat)
        low = values.astype(BF16)
        gw_ref[:, at] = dot(act, low, 1, 0)
        gb_ref[:, at] = jnp.sum(jnp.where(first, values, 0.0), axis=0, keepdims=True)
        more = dot(low, w_ref[:, at], 1, 1)
        dact = more if dact is None else dact + more
    dact_ref[...] = dact

    @pl.loop(0, spot_ref.shape[0])
    def _(j):
        at = spot_ref[j]
        row = dact_ref[pl.ds(jnp.maximum(at, 0), 1), :]
        picked_ref[pl.ds(j, 1), :] = jnp.where(at >= 0, row, 0.0)

    cond = cond_ref[...].astype(F32)
    gate = 1.0 / (1.0 + jnp.exp(-cond))
    dcond_ref[...] = (picked_ref[...] * (gate * (1.0 + cond * (1.0 - gate)))).astype(BF16)
    for i, values in enumerate(one):
        sums = jnp.sum(values.reshape(-1, 2 * slots, feat), axis=0)
        bias_ref[i * slots : (i + 1) * slots, :] = sums[slots:, :]


def mod_grad(group, me, device_of, spot, one, two, w_mod, cond, part, slots):
    feat, columns = w_mod.shape
    places, share = cond.shape
    count = 2 * slots * one.shape[0]

    def fixed(*shape):
        return pl.BlockSpec(shape, lambda i, *scalars: (0,) * len(shape))

    return pl.pallas_call(
        functools.partial(mod_grad_kernel, part=part, slots=slots),
        grid_spec=pltpu.PrefetchScalarGridSpec(
            num_scalar_prefetch=3,
            grid=(1,),
            in_specs=[
                fixed(*one.shape),
                fixed(*two.shape),
                pl.BlockSpec((share, columns), lambda i, ids, *scalars: (ids[0], 0)),
                fixed(places, share),
            ],
            out_specs=[
                fixed(part, columns),
                fixed(1, columns),
                fixed(places, share),
                fixed(2 * slots, feat),
            ],
            scratch_shapes=[pltpu.VMEM((feat, count), F32), pltpu.VMEM(one.shape, BF16), pltpu.VMEM((count, share), F32), pltpu.VMEM((places, share), F32)],
        ),
        out_shape=[
            jax.ShapeDtypeStruct((part, columns), F32),
            jax.ShapeDtypeStruct((1, columns), F32),
            jax.ShapeDtypeStruct((places, share), BF16),
            jax.ShapeDtypeStruct((2 * slots, feat), F32),
        ],
        compiler_params=params(),
        cost_estimate=BRIEF,
    )(jnp.stack([group, me]), device_of, spot, one, two, w_mod, cond)


def swap(values, axis, bit):
    count = lax.axis_size(axis)
    return lax.ppermute(values, axis, [(i, i ^ bit) for i in range(count)])


def bits_of(wide):
    return [1 << i for i in range(wide.bit_length() - 1)]


def chain_orders(wide):
    bits = bits_of(wide)
    x, y, z = bits[:3]
    far, rest = bits[3:4], bits[4:]
    return [[x, y, *far, z, *rest], [y, z, x, *far, *rest], [z, x, y, *far, *rest]]


class Part:
    def __init__(self, keep, got, start, rows, order):
        self.keep, self.got, self.at = keep, got, start
        self.rows = rows
        self.fresh = True
        self.dims = list(reversed(bits_of(keep.shape[0])))
        self.order = list(order)


class Rider:
    def __init__(self, values, order):
        self.keep, self.got, self.at = values, None, 0
        self.rows = values.shape[1]
        self.fresh = True
        self.order, self.done = list(order), []

    def differences(self):
        return [sum(b for i, b in enumerate(self.done) if p >> i & 1) for p in range(1 << len(self.done))]

    def place(self, difference):
        at = jnp.zeros_like(difference)
        for i, bit in enumerate(self.done):
            at = at + ((difference // bit) % 2) * (1 << i)
        return at


def masks_of(bits):
    top = len(bits) - 1
    return [sum(b for i, b in enumerate(bits) if m >> (top - i) & 1) for m in range(1 << len(bits))]


def relay_kernel(me_ref, *refs, plan, inputs, outputs):
    ins, outs, scratch = refs[:inputs], refs[inputs : inputs + outputs], list(refs[inputs + outputs :])
    arriving = {}
    if scratch:
        sems = scratch.pop()
        for i, (kind, keep, got, at, rows, *_) in enumerate(plan):
            if kind == "fresh":
                for source in (keep, got):
                    k = len(arriving)
                    copy = pltpu.make_async_copy(
                        ins[source].at[:, pl.ds(at, rows), :], scratch[k], sems.at[k]
                    )
                    copy.start()
                    arriving[i, source == got] = (copy, scratch[k])
    for i, (kind, keep, got, at, rows, bit, inner, count, targets) in enumerate(plan):
        if kind == "ride":
            pieces = [ins[keep][0]]
            if got is not None:
                pieces.append(ins[got][at : at + rows, :])
            for out, base in targets:
                for k, piece in enumerate(pieces):
                    to = slice(base + k * rows, base + (k + 1) * rows)
                    if len(outs[out].shape) == 3:
                        outs[out][0, to, :] = piece
                    else:
                        outs[out][to, :] = piece
            continue
        if kind == "fresh":
            for copy, _ in (arriving[i, False], arriving[i, True]):
                copy.wait()
            k_ref, g_ref = arriving[i, False][1], arriving[i, True][1]
        else:
            k_ref, g_ref = ins[keep], None if bit is None else ins[got]
        if bit is None:
            total = k_ref[0].astype(F32)
            for source, first in zip(got, at, strict=True):
                total = total + ins[source][first : first + rows, :].astype(F32)
            outs[targets[0][0]][...] = total
            continue
        if isinstance(bit, tuple):
            top = len(bit) - 1
            own = sum(((me_ref[0] // b) % 2) << (top - k) for k, b in enumerate(bit))
            for m, (out, base) in enumerate(targets):
                right = g_ref[pl.ds(pl.multiple_of(at + (own ^ m) * rows, TILE), rows), :]
                if base is None:
                    outs[out][0] = k_ref[own ^ m] + right
                else:
                    outs[out][base : base + rows, :] = k_ref[own ^ m] + right
            continue
        own = (me_ref[0] // bit) % 2

        @pl.loop(0, count // 2)
        def _(e, kind=kind, at=at, own=own, rows=rows, inner=inner, k_ref=k_ref, g_ref=g_ref, targets=targets):
            outer = (e // inner) * 2 * inner + e % inner
            for which, (out, base) in zip((1 - own, own), targets, strict=True):
                entry = outer + which * inner
                if kind == "fresh":
                    right = g_ref[entry]
                else:
                    right = g_ref[pl.ds(pl.multiple_of(at + entry * rows, TILE), rows), :]
                total = k_ref[entry] + right
                if base is None:
                    outs[out][e] = total
                else:
                    outs[out][pl.ds(pl.multiple_of(base + e * rows, TILE), rows), :] = total


def relay(me, moving):
    arrays, places, plan, shapes, sends = [], [], [], [], {}
    columns = moving[0].keep.shape[2]
    vmem, hbm = pl.BlockSpec(memory_space=pltpu.VMEM), pl.BlockSpec(memory_space=pl.ANY)

    def index(array, place):
        if array is None:
            return None
        for i, known in enumerate(arrays):
            if known is array:
                return i
        arrays.append(array)
        places.append(place)
        return len(arrays) - 1

    bits = set()
    for m in moving:
        if m.order:
            bits.update(masks_of(m.order[0])[1:] if isinstance(m.order[0], tuple) else m.order[:1])
    bits = sorted(bits)
    sizes = dict.fromkeys(bits, 0)
    scratch, keeps = [], []
    for m in moving:
        bit = m.order[0] if m.order else None
        ride = isinstance(m, Rider)
        kind = "ride" if ride else "fresh" if m.fresh else "add"
        place = hbm if kind == "fresh" else vmem
        keep, at = index(m.keep, place), m.at
        several = isinstance(m.got, list)
        got = [index(g, place) for g in m.got] if several else index(m.got, place)
        rows, inner, count = m.rows, 1, 1
        fan = isinstance(bit, tuple)
        to = (bits.index(bit), sizes[bit]) if bit is not None and not fan else None
        kept = len(bits) + len(shapes)
        keeps.append(kept)
        if ride:
            m.rows *= 1 if got is None else 2
            shapes.append(jax.ShapeDtypeStruct((1, m.rows, columns), BF16))
            targets = [(kept, 0)] + ([] if to is None else [to])
            size = m.rows
        elif bit is None:
            shapes.append(jax.ShapeDtypeStruct((rows, columns), F32))
            targets, size = [(kept, 0)], 0
            got, at = (got, at) if several else ([got], [at])
        elif fan:
            shapes.append(jax.ShapeDtypeStruct((1, rows, columns), BF16))
            masks_here = masks_of(bit)[1:]
            m.at = [sizes[mask] for mask in masks_here]
            targets = [(kept, None)] + [(bits.index(mask), sizes[mask]) for mask in masks_here]
            for mask in masks_here:
                sizes[mask] += rows
            m.dims = []
        else:
            dim = m.dims.index(bit)
            count, inner = 1 << len(m.dims), 1 << (len(m.dims) - 1 - dim)
            m.dims.pop(dim)
            size = count // 2 * rows
            shapes.append(jax.ShapeDtypeStruct((count // 2, rows, columns), BF16))
            targets = [to, (kept, None)]
            if kind == "fresh":
                scratch += [pltpu.VMEM((count, rows, columns), BF16)] * 2
        plan.append((kind, keep, got, at, rows, bit, inner, count, targets))
        if bit is not None and not fan:
            m.at = sizes[bit]
            sizes[bit] += size
        m.fresh = False
    if scratch:
        scratch.append(pltpu.SemaphoreType.DMA((len(scratch),)))
    shapes = [jax.ShapeDtypeStruct((sizes[b], columns), BF16) for b in bits] + shapes
    out = pl.pallas_call(
        functools.partial(relay_kernel, plan=plan, inputs=len(arrays), outputs=len(shapes)),
        in_specs=[pl.BlockSpec(memory_space=pltpu.SMEM)] + places,
        out_specs=[vmem] * len(shapes),
        out_shape=shapes,
        scratch_shapes=scratch,
        compiler_params=params(),
        cost_estimate=BRIEF,
    )(me, *arrays)
    for m, kept in zip(moving, keeps, strict=True):
        m.keep = out[kept]
    return dict(zip(bits, out))


class Sums:
    def __init__(self, me):
        self.me, self.moving, self.going = me, [], {}

    def step(self, *joining, after=()):
        came = {bit: swap(send, "wide", bit) for bit, send in self.going.items()}
        if callable(after):
            after = after(came)
        if after:
            kept, _ = lax.optimization_barrier((tuple(m.keep for m in self.moving), tuple(after)))
            for m, array in zip(self.moving, kept, strict=True):
                m.keep = array
        going = [m for m in self.moving if m.order]
        for m in going:
            bit = m.order.pop(0)
            m.got = [came[mask] for mask in masks_of(bit)[1:]] if isinstance(bit, tuple) else came[bit]
            if isinstance(m, Rider):
                m.done.append(bit)
        self.moving += joining
        self.going = relay(self.me, going + list(joining))

    def arrays(self):
        return tuple(self.going.values()) + tuple(m.keep for m in self.moving)

    def put(self, arrays):
        count = len(self.going)
        self.going = dict(zip(self.going, arrays[:count], strict=True))
        for m, kept in zip(self.moving, arrays[count:], strict=True):
            m.keep = kept


def tie(values, moving):
    out = lax.optimization_barrier((tuple(values), tuple(m.arrays() for m in moving)))
    for one, kept in zip(moving, out[1], strict=True):
        one.put(kept)
    return out[0]


def local(
    x_src,
    cond,
    lengths,
    bucket,
    w_mod,
    b_mod,
    w_qkv,
    b_qv,
    w_proj,
    b_proj,
    w_fc1,
    b_fc1,
    w_fc2,
    b_fc2,
    grad_out,
):
    wide = lax.axis_size("wide")
    halves = lax.axis_size("narrow")
    devices = wide * halves
    group = lax.axis_index("wide")
    half = lax.axis_index("narrow")
    rows, feat = x_src.shape
    hidden = w_fc1.shape[1]
    places = lengths.shape[0] // halves
    slots = places // wide
    blocks = rows // BLK
    per_block = BLK // wide
    tiled = per_block % TILE == 0

    split = regroup if tiled else regroup_any
    send, scond, seg, src, cidx = split(x_src, cond, lengths, bucket, jnp.stack([group, half]), wide)
    exchange = functools.partial(
        lax.all_to_all, axis_name="wide", split_axis=0, concat_axis=0, tiled=True
    )
    came = exchange(send)
    came_cond = exchange(scond.reshape(wide, slots, feat // wide))
    cond_in = came_cond.transpose(1, 0, 2).reshape(slots, feat)
    x_view = came.reshape(wide, blocks, per_block, feat)
    if not tiled:
        x_view = x_view.transpose(1, 0, 2, 3).reshape(1, blocks, BLK, feat)

    act_low = jax.nn.silu(cond_in.astype(F32)).astype(BF16)
    modulate = jnp.dot(act_low, w_mod, preferred_element_type=F32) + b_mod.astype(F32)
    slot_ids = jnp.arange(slots, dtype=jnp.int32)
    in_slot = seg[:, None] == slot_ids[None, :]
    mod_blocks = jnp.sum(
        jnp.where(in_slot[:, :, None], modulate[None], 0.0), axis=1
    ).reshape(blocks, 6, feat)

    dy = (
        grad_out.reshape(blocks, per_block, wide, feat)
        .transpose(0, 2, 1, 3)
        .reshape(rows, feat)
    )
    gate_two = mod_blocks[:, 5:6, :]
    df = (
        (gate_two * dy.reshape(blocks, BLK, feat).astype(F32)).astype(BF16).reshape(rows, feat)
    )
    grad_b_fc2 = jnp.sum(df.astype(F32), axis=0)
    dg = dot(df, w_fc2, 1, 1)
    bias_qkv = jnp.concatenate(
        [b_qv[:feat].astype(F32), jnp.zeros((feat,), F32), b_qv[feat:].astype(F32)]
    ).reshape(1, 3 * feat)

    qkv_t, a1_t = qkv_forward(x_view, mod_blocks, w_qkv, bias_qkv)
    o_t, lse = attend(seg, qkv_t)
    attn, x1, a2, a2_t = proj_forward(
        o_t, w_proj, b_proj.astype(F32).reshape(1, feat), x_view, mod_blocks
    )
    own, place = half.reshape(1), group.reshape(1)
    part = feat // devices
    halved = Halves(wide, part)
    both = ("wide", "narrow")
    orders = chain_orders(wide)
    near, far = bits_of(wide)[:3], bits_of(wide)[3:]
    sums = Sums(place)

    def shares(grad, got, cuts, ways):
        return [
            Part(grad[1], got, a, b - a, way)
            for a, b, way in zip(cuts[:-1], cuts[1:], ways, strict=True)
        ]

    def thirds(rows_of):
        third = -(-rows_of // 3 // TILE) * TILE
        return [0, third, min(2 * third, rows_of - TILE), rows_of]

    f, da2, grad_b_fc1, d_fc1, d_fc2 = mlp(
        own, a2, a2_t, df, dg, w_fc1, w_fc2, b_fc1.astype(F32).reshape(1, hidden), halved
    )

    if halved.split:
        fc2_got, fc1_got = swap(d_fc2[0], "narrow", 1), swap(d_fc1[0], "narrow", 1)
    y, dx1, do_t, grad_b_proj, two, d_proj = middle(
        own, seg, act_low, f, b_fc2.astype(F32).reshape(1, feat), x1, attn, dy, da2, mod_blocks, o_t,
        w_proj, halved,
    )
    y_dest = (
        y.reshape(blocks, wide, per_block, feat).transpose(0, 2, 1, 3).reshape(rows, feat)
    )
    pieces, row_sums, head = [], [], 0

    def attention(counts):
        nonlocal head
        for count in counts:
            piece, piece_sums = attend_back(
                seg, qkv_t, o_t, do_t, lse, first=head, count=count
            )
            pieces.append(piece)
            row_sums.append(piece_sums[:, 0])
            head += count

    def bias_rows():
        of_qv = jnp.concatenate(row_sums, axis=1)
        rows_of = [grad_b_fc1[0], grad_b_fc2, grad_b_proj[0], of_qv[0], of_qv[1]]
        return jnp.concatenate(rows_of).reshape(2 * slots, feat)

    ride_order = far + near[2:] + near[:2]
    if halved.split:
        proj_got = swap(d_proj[0], "narrow", 1)
        third = (d_fc2[1].shape[1] + d_fc1[1].shape[1] + part) // 3 // TILE * TILE
        fc2_parts = shares(d_fc2, fc2_got, [0, third, d_fc2[1].shape[1]], [orders[0], orders[2]])
        fc1_parts = shares(d_fc1, fc1_got, [0, third, d_fc1[1].shape[1]], [orders[1], orders[2]])
        proj_parts = shares(d_proj, proj_got, [0, part], orders[2:])
        two = Rider(two, ride_order)
        sums.step(*fc2_parts, *fc1_parts, *proj_parts, two)
        for counts in ((12,), (4,)):
            (do_t, *pieces) = tie((do_t, *pieces), [sums])
            attention(counts)
            sums.step()
        (a1_t, *pieces) = tie((a1_t, *pieces), [sums])
    else:
        attention((4, 4, 4, 4))
    d_qkv = qkv_grad(own, a1_t, pieces, halved)
    if halved.split:
        sums.step(after=d_qkv)
        qkv_got = swap(d_qkv[0], "narrow", 1)
        (dx1, *pieces) = tie((dx1, *pieces), [sums])
    drows, one = rows_back(seg, pieces, w_qkv, x_view, dx1, mod_blocks, bias_rows())
    if halved.split:
        sums.step()
        (drows,) = tie((drows,), [sums])
    back = drows
    if not tiled:
        back = back.reshape(blocks, wide, per_block, feat).transpose(1, 0, 2, 3)
    back = exchange(back.reshape(wide, rows // wide, feat))
    me = group * halves + half

    def modulation_grads(device_of, one_all, two_all):
        bucket_of, slot_of = jnp.maximum(cidx, 0) // slots, jnp.maximum(cidx, 0) % slots
        if halved.split:
            spot = two.place(bucket_of ^ group) * 2 * slots + slot_of
        else:
            spot = (bucket_of * halves + half) * 2 * slots + slot_of
        spot = jnp.where(cidx >= 0, spot, -1)
        return mod_grad(group, me, device_of, spot, one_all, two_all, w_mod, cond, part, slots)

    one_all = lax.all_gather(one, both, axis=0, tiled=True)
    if halved.split:
        last = tuple(reversed(near[2:] + far))
        flat, turned = [*near[:2], last], [*near[:2][::-1], last]
        qkv_parts = shares(
            d_qkv, qkv_got, [0, part, 2 * part, 2 * part + part // 2, 3 * part], [flat, turned, flat, turned]
        )
        sums = Sums(place)
        sums.step(*qkv_parts)
        tie((), [sums])
        sums.step()
        tie((), [sums])
        sums.step()
        (back,) = tie((back,), [sums])
        two_all = two.keep.reshape(wide, -1, feat)
        two_all = jnp.concatenate([two_all, swap(two_all, "narrow", 1)], axis=0)
        differs = jnp.asarray(two.differences(), jnp.int32)
        device_of = jnp.concatenate(
            [(differs ^ group) * halves + half, (differs ^ group) * halves + 1 - half]
        )
        held = {}

        def between(came):
            held["all"], came[near[2]] = lax.optimization_barrier((one_all, came[near[2]]))
            held["grads"] = modulation_grads(device_of, held["all"], two_all)
            return held["grads"][:1]

        sums.step(after=between)
        while sums.going:
            sums.step()
        modulation = held["grads"]
        grad_w_fc2 = jnp.concatenate([p.keep for p in fc2_parts], axis=0)
        grad_w_fc1 = jnp.concatenate([p.keep for p in fc1_parts], axis=0)
        grad_w_fc1 = (
            grad_w_fc1.reshape(hidden // feat, part, feat).transpose(1, 0, 2).reshape(part, hidden)
        )
        (grad_w_proj,) = (p.keep for p in proj_parts)

        kept = [p.keep for p in qkv_parts]
        grad_w_qkv = jnp.concatenate(kept[:2] + [jnp.concatenate(kept[2:], axis=0)], axis=1)
    else:
        two_all = lax.all_gather(two, both, axis=0, tiled=True)
        modulation = modulation_grads(jnp.arange(devices, dtype=jnp.int32), one_all, two_all)

        def scattered(full):
            return lax.psum_scatter(full, both, scatter_dimension=0, tiled=True).astype(F32)

        grad_w_fc2 = scattered(d_fc2[0])
        grad_w_fc1 = scattered(d_fc1[0].transpose(1, 0, 2).reshape(feat, hidden))
        grad_w_proj = scattered(d_proj[0])
        grad_w_qkv = scattered(d_qkv[0].transpose(1, 0, 2).reshape(feat, 3 * feat))
    merge = restore if tiled else restore_any
    dx_src = merge(src, back.reshape(rows, feat))

    grad_w_mod, grad_b_mod, dcond, biases = modulation
    grad_b_mod = lax.dynamic_slice_in_dim(grad_b_mod[0], me * 6 * part, 6 * part)

    def own_part(first, count):
        rows_of = biases[first : first + count].reshape(-1)
        share = rows_of.shape[0] // devices
        return lax.dynamic_slice_in_dim(rows_of, me * share, share)

    fc1_lines = hidden // feat
    s_fc1, s_fc2, s_proj = own_part(0, fc1_lines), own_part(fc1_lines, 1), own_part(fc1_lines + 1, 1)
    s_qv = own_part(fc1_lines + 2, 2)
    return (
        y_dest,
        dx_src,
        dcond,
        grad_w_mod,
        grad_b_mod,
        grad_w_qkv,
        s_qv,
        grad_w_proj,
        s_proj,
        grad_w_fc1,
        s_fc1,
        grad_w_fc2,
        s_fc2,
    )


def solution(mesh):
    both = ("wide", "narrow")
    placed = (P("narrow", "wide"), P("narrow", "wide")) + (P(),) * 12 + (P(both, None),)
    matrix, vector = P(both, None), P(both)
    return jax.shard_map(
        local,
        mesh=mesh,
        in_specs=placed,
        out_specs=(
            matrix,
            P("narrow", "wide"),
            P("narrow", "wide"),
            matrix,
            vector,
            matrix,
            vector,
            matrix,
            vector,
            matrix,
            vector,
            matrix,
            vector,
        ),
        check_vma=False,
    )
```
